32 devices in a mesh: seq: 8 (over y, x, core), exp: 4 (over z).
Axes of the slice: x: 2, y: 2, z: 4, core: 2. Of those that a mesh axis runs over, the one named last changes fastest.
Arguments:
- tokens: bfloat16 [48, 4, 1024], P('exp'), may hold values from -48 to 48
- attn_gain: float32 [1024], replicated, may hold values from 0.1 to 1.9
- w_qkv: bfloat16 [3072, 1024], P('seq'), may hold values from -0.1875 to 0.1875
- window_cache: bfloat16 [2, 48, 4096, 1024], P(None, 'exp', 'seq'), may hold values from -180 to 180
- sink_cache: bfloat16 [2, 48, 4, 1024], P(None, 'exp'), may hold values from -6 to 6
- lengths: int32 [48], P('exp'), may hold values from 8 to 16384, as said below
- w_out: bfloat16 [1024, 1024], P('seq'), may hold values from -0.1875 to 0.1875
- moe_gain: float32 [1024], replicated, may hold values from 0.1 to 1.9
- router: bfloat16 [1024, 16], replicated, may hold values from -0.1875 to 0.1875
- expert_ids: int32 [48, 4, 2], P('exp'), may hold values from 0 to 15, all different within a row
- slot_order: int32 [4, 48], P('exp'), may hold values from 0 to 47, each once within a row
- expert_in: bfloat16 [2, 4, 11264, 1024], P(None, 'exp', 'seq'), may hold values from -0.1875 to 0.1875
- expert_down: bfloat16 [4, 11264, 1024], P('exp', 'seq'), may hold values from -0.109375 to 0.109375
Outputs:
- output: bfloat16 [48, 4, 1024], P('exp')
The draws below stay inside these ranges and needn't reach their ends.
Inputs may be any that keep to these rules, and one draw needn't show every extreme that they name: `lengths`: at least one request holds 16384 tokens. `expert_ids`: the 2 experts of a token differ, and every expert is named by some token. `slot_order`: each group's row holds every number of 0 to 47 once.
All inputs are finite; a program needn't handle non-finite values.
Results may differ from the reference program's by a relative error of at most 0.0083.
The reference program's roundings to bfloat16 on the way count: a program that leaves them out, or rounds other values in their place, can miss the bound.
Values may be sent and summed in bfloat16 or wider, within the bound.
No kernel may reach another device: no remote copies, remote signals or barrier semaphores. Data moves between devices by JAX's collectives and lax.ppermute only.
A program may use at most 128 MiB of HBM per device.

```python
import math
import jax
import jax.numpy as jnp
from jax import lax

D = 1024
FF = 2816
HEADS = 16
HD = 64
EXPERTS = 16
TOPK = 2
SINKS = 4
WIN = 4096
STEPS = 4
MAXLEN = 16384
GROUPS = 4
REQS = 48
ROWS_GRP = 48
CAP = 8
EXP_GRP = 4
N_EXP = 4


def draw_tokens(key, part):
    key_noise, key_rows, key_cols = jax.random.split(key, 3)
    row_scale = jnp.exp(jax.random.uniform(key_rows, (REQS, STEPS, 1), jnp.float32, math.log(0.5), math.log(5.0)))
    column_scale = jnp.exp(jax.random.uniform(key_cols, (D,), jnp.float32, math.log(0.3), math.log(3.0)))
    base_part = jnp.clip(jax.random.normal(key_noise, (REQS, STEPS, D), jnp.float32), -3.0, 3.0)
    return (base_part * row_scale * column_scale).astype(jnp.bfloat16)


def draw_window_cache(key, part):
    key_keys, key_values = jax.random.split(key)
    key_table = 2.0 * jnp.clip(jax.random.normal(key_keys, (REQS, WIN, D), jnp.float32), -4.0, 4.0)
    value_table = jnp.clip(jax.random.normal(key_values, (REQS, WIN, D), jnp.float32), -4.0, 4.0)
    return jnp.stack([key_table, value_table]).astype(jnp.bfloat16)


def draw_lengths(key, part):
    key_power, key_extra, key_long, key_short = jax.random.split(key, 4)
    top_power = MAXLEN.bit_length() - 1
    doubling = jax.random.randint(key_power, (REQS,), 3, top_power + 1)
    floor_len = jnp.left_shift(jnp.ones((REQS,), jnp.int32), doubling)
    added_len = jax.random.randint(key_extra, (REQS,), 0, floor_len)
    length = jnp.minimum(floor_len + added_len, MAXLEN)
    longest = jax.random.randint(key_long, (), 0, REQS)
    offset = jax.random.randint(key_short, (), 1, REQS)
    length = length.at[longest].set(MAXLEN)
    length = length.at[(longest + offset) % REQS].set(8)
    return length.astype(jnp.int32)


def block_levels(key, extent, shards, smallest, high):
    gain = 1.0
    for axis_at, parts in shards:
        draws = jax.random.uniform(jax.random.fold_in(jax.random.fold_in(key, 6), axis_at), (parts,), jnp.float32, smallest / len(shards), high / len(shards))
        gain = gain * jnp.repeat(jnp.exp(draws), extent[axis_at] // parts).reshape((-1,) + (1,) * (len(extent) - 1 - axis_at))
    return gain


def distinct(own_key, rows, amount, top, lift):
    sequence = jax.random.permutation(jax.random.fold_in(own_key, 1), amount)
    favour = sequence
    for power in range(3):
        favour = favour * favour // amount
    favour = favour * lift // amount
    tickets = jax.random.randint(jax.random.fold_in(own_key, 2), (rows, amount), 0, 4096) + favour
    fixed_rows = jax.random.permutation(jax.random.fold_in(own_key, 3), rows)[jnp.arange(amount) % rows]
    tickets = jnp.where(jnp.arange(rows)[:, None] == fixed_rows[None, :], 1 << 14, tickets)
    merit = tickets * amount + jnp.arange(amount)
    return lax.top_k(merit.astype(jnp.int32), top)[1].astype(jnp.int32)


def normal_values(rng, extent, width, limit, shards=(), held_as=jnp.bfloat16):
    gain = block_levels(rng, extent, shards, -0.22, 0.18) if shards else 1.0
    array = jax.random.normal(rng, extent, jnp.float32) * width * gain
    return jnp.minimum(jnp.maximum(array, -limit), limit).astype(held_as)


def setup_inputs(seed: int = 0) -> dict:
    key_list = jax.random.split(jax.random.key(seed), 14)
    tokens = draw_tokens(jax.random.fold_in(key_list[13], 71), 0)
    attn_gain = jnp.clip(1.0 + 0.18 * jax.random.normal(key_list[1], (D,), jnp.float32), 0.1, 1.9)
    w_qkv = normal_values(key_list[2], (3 * D, D), D ** -0.5, 0.1875, ((0, 8),))
    window_cache = draw_window_cache(jax.random.fold_in(key_list[13], 71), 0)
    sink_cache = normal_values(key_list[4], (2, REQS, SINKS, D), 1.5, 6.0, ((1, 4),))
    lengths = draw_lengths(jax.random.fold_in(key_list[13], 71), 0)
    w_out = normal_values(key_list[6], (D, D), D ** -0.5, 0.1875, ((0, 8),))
    moe_gain = jnp.clip(1.0 + 0.18 * jax.random.normal(key_list[7], (D,), jnp.float32), 0.1, 1.9)
    router = normal_values(key_list[8], (D, EXPERTS), D ** -0.5, 0.1875)
    expert_ids = distinct(key_list[9], REQS * STEPS, EXPERTS, TOPK, 2048).reshape((REQS, STEPS, TOPK))
    slot_order = jax.vmap(lambda own: jax.random.permutation(own, ROWS_GRP))(jax.random.split(key_list[10], GROUPS)).reshape((GROUPS, ROWS_GRP)).astype(jnp.int32)
    expert_in = normal_values(key_list[11], (2, N_EXP, EXP_GRP * FF, D), D ** -0.5, 0.1875, ((1, 4), (2, 8)))
    expert_down = normal_values(key_list[12], (N_EXP, EXP_GRP * FF, D), FF ** -0.5, 0.109375, ((0, 4), (1, 8)))
    return dict(tokens=tokens, attn_gain=attn_gain, w_qkv=w_qkv, window_cache=window_cache, sink_cache=sink_cache, lengths=lengths, w_out=w_out, moe_gain=moe_gain, router=router, expert_ids=expert_ids, slot_order=slot_order, expert_in=expert_in, expert_down=expert_down)


EPSILON = 1e-06
MASKED = -1e+30

def rms_scale(values, gain_row):
    widened = values.astype(jnp.float32)
    inverse = lax.rsqrt(lax.optimization_barrier(jnp.mean(widened * widened, axis=-1, keepdims=True)) + EPSILON)
    return (widened * inverse * gain_row).astype(jnp.bfloat16)

def attend_request(inputs):
    queries, new_keys, new_values, window_keys, window_values, sink_keys, sink_values, length = inputs
    step_ids = jnp.arange(STEPS, dtype=jnp.int32)
    slot_ids = jnp.arange(WIN, dtype=jnp.int32)
    written = (length + step_ids - SINKS) % WIN
    overwritten = jnp.cumsum((slot_ids[None, :] == written[:, None]).astype(jnp.int32), axis=0) > 0
    window_live = (slot_ids[None, :] < jnp.minimum(WIN, length - SINKS)) & jnp.logical_not(overwritten)
    causal = step_ids[None, :] <= step_ids[:, None]
    live_keys = jnp.concatenate([window_live, jnp.ones((STEPS, SINKS), jnp.bool_), causal], axis=1)[:, None, :]
    all_keys = jnp.concatenate([window_keys.reshape(WIN, HEADS, HD), sink_keys.reshape(SINKS, HEADS, HD), new_keys], axis=0).astype(jnp.float32)
    all_values = jnp.concatenate([window_values.reshape(WIN, HEADS, HD), sink_values.reshape(SINKS, HEADS, HD), new_values], axis=0).astype(jnp.float32)
    scores = jnp.einsum('she,khe->shk', queries.astype(jnp.float32), all_keys) * HD ** (-0.5)
    peak_score = lax.optimization_barrier(jnp.max(jnp.where(live_keys, scores, MASKED), axis=-1, keepdims=True))
    exponent = jnp.where(live_keys, jnp.exp(scores - peak_score), 0.0)
    weight_sum = lax.optimization_barrier(jnp.sum(exponent, axis=-1, keepdims=True))
    rounded = lax.optimization_barrier(exponent.astype(jnp.bfloat16)).astype(jnp.float32)
    weighted = jnp.einsum('shk,khe->she', rounded, all_values) / weight_sum
    return weighted.reshape(STEPS, D).astype(jnp.bfloat16)

def route_group(chosen, priority, features, logits):
    onehot = (chosen[:, :, None] == jnp.arange(EXPERTS, dtype=jnp.int32)).astype(jnp.float32)
    gate_values = jax.nn.sigmoid(lax.optimization_barrier(jnp.sum(onehot * logits[:, None, :], axis=-1)))
    earlier = (priority[None, :] < priority[:, None]).astype(jnp.float32)
    counts = jnp.dot(earlier, lax.optimization_barrier(jnp.sum(onehot, axis=1)), precision=lax.Precision.HIGHEST)
    position = lax.optimization_barrier(jnp.sum(onehot * counts[:, None, :], axis=-1)).astype(jnp.int32)
    column = chosen * CAP + position
    select = ((column[:, :, None] == jnp.arange(EXPERTS * CAP, dtype=jnp.int32)) & (position < CAP)[:, :, None]).astype(jnp.float32)
    dispatch = lax.optimization_barrier(jnp.sum(select, axis=1)).astype(jnp.bfloat16)
    buffer = jnp.dot(dispatch.T, features, preferred_element_type=jnp.float32).astype(jnp.bfloat16)
    return (buffer, select, gate_values)

def run_expert(inputs):
    rows_in, weights_in, weights_down = inputs
    gate_up = jnp.einsum('nd,pfd->pnf', rows_in.astype(jnp.float32), weights_in.astype(jnp.float32))
    hidden = (jax.nn.gelu(gate_up[0], approximate=True) * gate_up[1]).astype(jnp.bfloat16)
    return jnp.dot(hidden, weights_down, preferred_element_type=jnp.float32).astype(jnp.bfloat16)

def reference(tokens, attn_gain, w_qkv, window_cache, sink_cache, lengths, w_out, moe_gain, router, expert_ids, slot_order, expert_in, expert_down):
    flat_rows = tokens.reshape(REQS * STEPS, D)
    normed_attn = rms_scale(flat_rows, attn_gain)
    mixed_rows = jnp.dot(normed_attn, w_qkv.T, preferred_element_type=jnp.float32).astype(jnp.bfloat16)
    mixed_rows = lax.optimization_barrier(mixed_rows).reshape(REQS, STEPS, 3, HEADS, HD)
    attended = lax.map(attend_request, (mixed_rows[:, :, 0], mixed_rows[:, :, 1], mixed_rows[:, :, 2], window_cache[0], window_cache[1], sink_cache[0], sink_cache[1], lengths))
    projected = jnp.dot(attended.reshape(REQS * STEPS, D), w_out.T, preferred_element_type=jnp.float32).astype(jnp.bfloat16)
    residual = flat_rows.astype(jnp.float32) + lax.optimization_barrier(projected).astype(jnp.float32)
    normed_moe = rms_scale(residual, moe_gain)
    logits = jnp.dot(normed_moe, router, preferred_element_type=jnp.float32)
    buffers, selects, gate_values = jax.vmap(route_group)(expert_ids.reshape(GROUPS, ROWS_GRP, TOPK), slot_order, normed_moe.reshape(GROUPS, ROWS_GRP, D), logits.reshape(GROUPS, ROWS_GRP, EXPERTS))
    by_expert = buffers.reshape(GROUPS, EXPERTS, CAP, D).transpose(1, 0, 2, 3).reshape(EXPERTS, GROUPS * CAP, D)
    weights_in = expert_in.reshape(2, EXPERTS, FF, D).transpose(1, 0, 2, 3)
    weights_down = expert_down.reshape(EXPERTS, FF, D)
    outputs = lax.map(run_expert, (by_expert, weights_in, weights_down))
    outputs = lax.optimization_barrier(outputs)
    by_group = outputs.reshape(EXPERTS, GROUPS, CAP, D).transpose(1, 0, 2, 3).reshape(GROUPS, EXPERTS * CAP, D)
    picked = jnp.einsum('grkc,gcd->grkd', selects, by_group.astype(jnp.float32))
    moe_rows = lax.optimization_barrier(jnp.sum(gate_values[..., None] * picked, axis=2))
    final_rows = (residual.reshape(GROUPS, ROWS_GRP, D) + moe_rows).astype(jnp.bfloat16)
    return final_rows.reshape(REQS, STEPS, D)
```

```python
import functools

import jax
import jax.numpy as jnp
from jax import lax
from jax.experimental import pallas as pl
from jax.experimental.pallas import tpu as pltpu
from jax.sharding import PartitionSpec as P

HEADS = 16
HD = 64
EXPERTS = 16
TOPK = 2
SINKS = 4
WIN = 4096
CAP = 8
LANES = 128
PIECES = 3

EPSILON = 1e-06
MASKED = -1e30
MIB = 1 << 20
ROWS_BY_ROWS = (((1,), (1,)), ((), ()))
ROWS_BY_COLS = (((1,), (0,)), ((), ()))


def dot(a, b, dims=ROWS_BY_COLS):
    return lax.dot_general(a, b, dims, preferred_element_type=jnp.float32)


def params(limit_mib=32):
    return pltpu.CompilerParams(vmem_limit_bytes=limit_mib * MIB)


def split(value, count):
    parts = []
    for _ in range(count):
        part = value.astype(jnp.bfloat16)
        parts.append(part)
        value = value - part.astype(jnp.float32)
    return parts


def rms_rows(widened, gain_row):
    inverse = lax.rsqrt(jnp.mean(widened * widened, axis=-1, keepdims=True) + EPSILON)
    return (widened * inverse * gain_row).astype(jnp.bfloat16)


def qkv_kernel(tokens_ref, gain_ref, weight_ref, out_ref, rows_ref):
    requests, steps, _ = tokens_ref.shape
    for r in range(requests):
        rows_ref[r * steps : (r + 1) * steps, :] = tokens_ref[r].astype(jnp.float32)
    normed = rms_rows(rows_ref[...], gain_ref[...])
    out_ref[...] = dot(normed, weight_ref[...], ROWS_BY_ROWS).astype(jnp.bfloat16)


def attention_kernel(
    lengths_ref,
    place_ref,
    mixed_ref,
    keys_ref,
    values_ref,
    sinks_ref,
    out_ref,
    flat_ref,
    query_ref,
    extra_ref,
    part_ref,
):
    request = pl.program_id(0)
    requests = pl.num_programs(0)
    devices, rows, share = mixed_ref.shape
    steps = query_ref.shape[1]
    width = keys_ref.shape[-1]
    span = keys_ref.shape[2]
    groups = steps * HEADS

    @pl.when(request == 0)
    def _():
        for d in range(devices):
            flat_ref[:, d * share : (d + 1) * share] = mixed_ref[d].astype(jnp.float32)
        for r in range(query_ref.shape[0]):
            own = slice(r * steps, (r + 1) * steps)
            query_ref[r] = flat_ref[own, 0:width]
            for p in range(2):
                extra_ref[p, r, 0:SINKS] = sinks_ref[p, r].astype(jnp.float32)
                extra_ref[p, r, SINKS : SINKS + steps] = flat_ref[
                    own, (p + 1) * width : (p + 2) * width
                ]

    length = lengths_ref[request]
    base = place_ref[0] * span
    head_of_row = lax.broadcasted_iota(jnp.int32, (HEADS, width), 0)
    head_of_col = lax.broadcasted_iota(jnp.int32, (HEADS, width), 1) // HD
    own_head = (head_of_row == head_of_col).astype(jnp.float32)
    queries = query_ref[request]
    spread = jnp.concatenate([queries[t : t + 1] * own_head for t in range(steps)], axis=0).astype(
        jnp.bfloat16
    )
    scale = HD ** (-0.5)
    scores = dot(spread, keys_ref[0, 0], ROWS_BY_ROWS) * scale
    extra_keys = extra_ref[0, request].astype(jnp.bfloat16)
    extra_scores = dot(spread, extra_keys, ROWS_BY_ROWS) * scale

    slot = base + lax.broadcasted_iota(jnp.int32, (groups, span), 1)
    step = lax.broadcasted_iota(jnp.int32, (groups, span), 0) // HEADS
    age = jnp.bitwise_and(slot - (length - SINKS), WIN - 1)
    live = (slot < jnp.minimum(WIN, length - SINKS)) & (age > step)
    count = SINKS + steps
    extra_at = lax.broadcasted_iota(jnp.int32, (groups, count), 1)
    extra_step = lax.broadcasted_iota(jnp.int32, (groups, count), 0) // HEADS
    extra_live = (extra_at - SINKS <= extra_step) & (place_ref[0] == 0)

    scores = jnp.where(live, scores, MASKED)
    extra_scores = jnp.where(extra_live, extra_scores, MASKED)
    peak = jnp.maximum(
        jnp.max(scores, axis=-1, keepdims=True), jnp.max(extra_scores, axis=-1, keepdims=True)
    )
    weight = jnp.where(live, jnp.exp(scores - peak), 0.0)
    extra_weight = jnp.where(extra_live, jnp.exp(extra_scores - peak), 0.0)
    total = jnp.sum(weight, axis=-1, keepdims=True) + jnp.sum(extra_weight, axis=-1, keepdims=True)
    mixed = dot(weight.astype(jnp.bfloat16), values_ref[0, 0])
    mixed = mixed + dot(
        extra_weight.astype(jnp.bfloat16), extra_ref[1, request].astype(jnp.bfloat16)
    )
    lane = lax.broadcasted_iota(jnp.int32, (HEADS, LANES), 1)
    row_head = lax.broadcasted_iota(jnp.int32, (HEADS, LANES), 0)
    rows_out = []
    for t in range(steps):
        own = slice(t * HEADS, (t + 1) * HEADS)
        rows_out.append(jnp.sum(mixed[own] * own_head, axis=0, keepdims=True))
        stats = jnp.zeros((HEADS, LANES), jnp.float32)
        parts = split(peak[own], PIECES) + split(total[own], PIECES)
        for i, part in enumerate(parts):
            stats = jnp.where(lane == row_head + i * HEADS, part.astype(jnp.float32), stats)
        rows_out.append(jnp.sum(stats, axis=0, keepdims=True))
    part_ref[request] = jnp.concatenate(
        [
            jnp.concatenate(rows_out[0::2], axis=0),
            jnp.concatenate(rows_out[1::2], axis=0),
        ],
        axis=1,
    )

    @pl.when(request == requests - 1)
    def _():
        for r in range(part_ref.shape[0]):
            flat_ref[r * steps : (r + 1) * steps, 0 : width + LANES] = part_ref[r]
        out_ref[...] = flat_ref[:, 0 : width + LANES].astype(jnp.bfloat16)


def combine(parts_ref):
    devices, rows, padded = parts_ref.shape
    width = padded - LANES
    stats = [parts_ref[d][:, width:].astype(jnp.float32) for d in range(devices)]

    def joined(stat, first):
        return sum(
            stat[:, (first + i) * HEADS : (first + i + 1) * HEADS] for i in range(PIECES)
        )

    peaks = [joined(stat, 0) for stat in stats]
    totals = [joined(stat, PIECES) for stat in stats]
    overall = functools.reduce(jnp.maximum, peaks)
    factors = [jnp.exp(peak - overall) for peak in peaks]
    total = sum(f * t for f, t in zip(factors, totals))
    inverse = 1.0 / total
    head_of_row = lax.broadcasted_iota(jnp.int32, (HEADS, width), 0)
    head_of_col = lax.broadcasted_iota(jnp.int32, (HEADS, width), 1) // HD
    expand = (head_of_row == head_of_col).astype(jnp.bfloat16)
    attended = jnp.zeros((rows, width), jnp.float32)
    for d in range(devices):
        share = sum(dot(part, expand) for part in split(factors[d] * inverse, 2))
        attended = attended + share * parts_ref[d][:, :width].astype(jnp.float32)
    return attended.astype(jnp.bfloat16)


def project_kernel(parts_ref, weight_ref, out_ref):
    attended = combine(parts_ref)
    out_ref[...] = dot(attended, weight_ref[...], ROWS_BY_ROWS).astype(jnp.bfloat16)


def routing_kernel(ids_ref, order_ref, select_ref, turned_ref, chosen_ref, rows_ref):
    requests, steps, _ = ids_ref.shape
    rows = requests * steps
    for r in range(requests):
        rows_ref[r * steps : (r + 1) * steps, :] = ids_ref[r]
    lane = lax.broadcasted_iota(jnp.int32, (rows, LANES), 1)
    chosen = [rows_ref[:, c : c + 1] for c in range(TOPK)]
    onehot = [(lane == ids).astype(jnp.float32) for ids in chosen]
    across = order_ref[...]
    square_row = lax.broadcasted_iota(jnp.int32, (rows, rows), 0)
    square_col = lax.broadcasted_iota(jnp.int32, (rows, rows), 1)
    order_wide = jnp.broadcast_to(across, (rows, rows))
    down = jnp.sum(
        jnp.where(square_row == square_col, order_wide, 0).astype(jnp.float32),
        axis=1,
        keepdims=True,
    )
    earlier = (order_wide.astype(jnp.float32) < down).astype(jnp.bfloat16)
    counts = dot(earlier, sum(onehot).astype(jnp.bfloat16))
    slot = lax.broadcasted_iota(jnp.int32, (rows, EXPERTS * CAP), 1)
    both = jnp.zeros((rows, EXPERTS * CAP), jnp.float32)
    for c in range(TOPK):
        position = jnp.sum(onehot[c] * counts, axis=-1, keepdims=True).astype(jnp.int32)
        column = chosen[c] * CAP + position
        select = ((column == slot) & (position < CAP)).astype(jnp.float32)
        select_ref[c] = select
        chosen_ref[c] = onehot[c]
        both = both + select
    turned_ref[...] = jnp.transpose(both)


def residual_kernel(
    own_ref, projected_ref, tokens_ref, gain_ref, turned_ref, normed_ref, residual_ref, send_ref
):
    requests, steps, _ = tokens_ref.shape
    devices, rows, share = projected_ref.shape
    for r in range(requests):
        residual_ref[r * steps : (r + 1) * steps, :] = tokens_ref[r].astype(jnp.float32)
    for d in range(devices):
        own = slice(d * share, (d + 1) * share)
        residual_ref[:, own] = residual_ref[:, own] + projected_ref[d].astype(jnp.float32)
    normed = rms_rows(residual_ref[...], gain_ref[...])
    normed_ref[...] = normed
    groups = send_ref.shape[0]
    local_experts = EXPERTS // groups
    for g in range(groups):
        first = pl.multiple_of((g * local_experts + own_ref[0]) * CAP, CAP)
        picking = turned_ref[pl.ds(first, CAP), :].astype(jnp.bfloat16)
        send_ref[g] = dot(picking, normed).astype(jnp.bfloat16)


def gate_kernel(normed_ref, router_ref, select_ref, chosen_ref, out_ref):
    logits = dot(normed_ref[...], router_ref[...])
    gates = jnp.zeros(select_ref.shape[1:], jnp.float32)
    for c in range(TOPK):
        logit = jnp.sum(chosen_ref[c][:, :EXPERTS] * logits, axis=-1, keepdims=True)
        gates = gates + jax.nn.sigmoid(logit) * select_ref[c]
    out_ref[...] = gates


def expert_kernel(rows_ref, in_ref, down_ref, out_ref):
    groups, slots, width = rows_ref.shape
    rows = rows_ref[...].reshape(groups * slots, width)
    gate = dot(rows, in_ref[0, 0], ROWS_BY_ROWS)
    up = dot(rows, in_ref[1, 0], ROWS_BY_ROWS)
    hidden = (jax.nn.gelu(gate, approximate=True) * up).astype(jnp.bfloat16)
    out_ref[...] = dot(hidden, down_ref[0])


def final_kernel(gates_ref, returned_ref, residual_ref, out_ref):
    requests, steps, width = out_ref.shape
    returned = returned_ref[...]
    moe = sum(dot(part, returned) for part in split(gates_ref[...], 2))
    total = residual_ref[...] + moe
    for r in range(requests):
        out_ref[r] = total[r * steps : (r + 1) * steps].astype(jnp.bfloat16)


def shape(dims, dtype):
    return jax.ShapeDtypeStruct(dims, dtype)


def body(
    tokens,
    attn_gain,
    w_qkv,
    window_cache,
    sink_cache,
    lengths,
    w_out,
    moe_gain,
    router,
    expert_ids,
    slot_order,
    expert_in,
    expert_down,
):
    requests, steps, width = tokens.shape
    rows = requests * steps
    seq_index = lax.axis_index("seq")
    seq_count = lax.axis_size("seq")
    groups = lax.axis_size("exp")
    local_experts = EXPERTS // groups
    sharers = seq_count // local_experts
    own_expert = (seq_index // sharers).astype(jnp.int32).reshape(1)
    place = seq_index.astype(jnp.int32).reshape(1)
    span = window_cache.shape[2]
    share = w_qkv.shape[0]
    slots = EXPERTS * CAP
    f32, bf16 = jnp.float32, jnp.bfloat16

    local_mix = pl.pallas_call(
        qkv_kernel,
        out_shape=shape((rows, share), bf16),
        scratch_shapes=[pltpu.VMEM((rows, width), f32)],
        compiler_params=params(),
        name="qkv",
    )(tokens, attn_gain.reshape(1, width), w_qkv)
    mixed = lax.all_gather(local_mix, "seq", axis=0)

    padded = width + LANES
    part = pl.pallas_call(
        attention_kernel,
        grid_spec=pltpu.PrefetchScalarGridSpec(
            num_scalar_prefetch=2,
            grid=(requests,),
            in_specs=[
                pl.BlockSpec((seq_count, rows, share), lambda i, *_: (0, 0, 0)),
                pl.BlockSpec((1, 1, span, width), lambda i, *_: (0, i, 0, 0)),
                pl.BlockSpec((1, 1, span, width), lambda i, *_: (1, i, 0, 0)),
                pl.BlockSpec(sink_cache.shape, lambda i, *_: (0, 0, 0, 0)),
            ],
            out_specs=pl.BlockSpec((rows, padded), lambda i, *_: (0, 0)),
            scratch_shapes=[
                pltpu.VMEM((rows, 3 * width), f32),
                pltpu.VMEM((requests, steps, width), f32),
                pltpu.VMEM((2, requests, SINKS + steps, width), f32),
                pltpu.VMEM((requests, steps, padded), f32),
            ],
        ),
        out_shape=shape((rows, padded), bf16),
        compiler_params=params(),
        name="attention",
    )(lengths, place, mixed, window_cache, window_cache, sink_cache)
    parts = lax.all_gather(part, "seq", axis=0)

    local_proj = pl.pallas_call(
        project_kernel,
        out_shape=shape((rows, w_out.shape[0]), bf16),
        compiler_params=params(),
        name="project",
    )(parts, w_out)
    projected = lax.all_gather(local_proj, "seq", axis=0)

    select, turned, chosen = pl.pallas_call(
        routing_kernel,
        out_shape=(
            shape((TOPK, rows, slots), f32),
            shape((slots, rows), f32),
            shape((TOPK, rows, LANES), f32),
        ),
        scratch_shapes=[pltpu.VMEM((rows, TOPK), jnp.int32)],
        compiler_params=params(),
        name="routing",
    )(expert_ids, slot_order)

    smem = pl.BlockSpec(memory_space=pltpu.SMEM)
    vmem = pl.BlockSpec(memory_space=pltpu.VMEM)
    normed, residual, send = pl.pallas_call(
        residual_kernel,
        in_specs=[smem] + [vmem] * 4,
        out_shape=(
            shape((rows, width), bf16),
            shape((rows, width), f32),
            shape((groups, CAP, width), bf16),
        ),
        compiler_params=params(),
        name="residual",
    )(own_expert, projected, tokens, moe_gain.reshape(1, width), turned)
    received = lax.all_to_all(send, "exp", split_axis=0, concat_axis=0, tiled=True)

    gates = pl.pallas_call(
        gate_kernel,
        out_shape=shape((rows, slots), f32),
        compiler_params=params(),
        name="gate",
    )(normed, router, select, chosen)

    outputs = pl.pallas_call(
        expert_kernel,
        out_shape=shape((groups * CAP, width), f32),
        compiler_params=params(),
        name="expert",
    )(received, expert_in, expert_down)

    reach = 1
    while reach < sharers:
        other = lax.ppermute(outputs, "seq", [(i, i ^ reach) for i in range(seq_count)])
        outputs = outputs + other
        reach *= 2
    returned = lax.all_to_all(
        outputs.astype(bf16).reshape(groups, CAP, width),
        "exp",
        split_axis=0,
        concat_axis=0,
        tiled=True,
    )
    gathered = lax.all_gather(returned, "seq", axis=0)[::sharers]
    everyone = gathered.transpose(1, 0, 2, 3).reshape(slots, width)

    return pl.pallas_call(
        final_kernel,
        out_shape=shape((requests, steps, width), bf16),
        compiler_params=params(),
        name="final",
    )(gates, everyone, residual)


def solution(mesh):
    in_specs = (
        P("exp", None, None),
        P(),
        P("seq", None),
        P(None, "exp", "seq", None),
        P(None, "exp", None, None),
        P("exp"),
        P("seq", None),
        P(),
        P(),
        P("exp", None, None),
        P("exp", None),
        P(None, "exp", "seq", None),
        P("exp", "seq", None),
    )
    out_specs = P("exp", None, None)
    return jax.shard_map(body, mesh=mesh, in_specs=in_specs, out_specs=out_specs, check_vma=False)
```

```python
import functools

import jax
import jax.numpy as jnp
from jax import lax
from jax.experimental import pallas as pl
from jax.experimental.pallas import tpu as pltpu
from jax.sharding import PartitionSpec as P

HEADS = 16
HD = 64
EXPERTS = 16
TOPK = 2
SINKS = 4
WIN = 4096
CAP = 8
LANES = 128
PIECES = 3
BLOCK = 256
BLOCK_HEADS = BLOCK // HD

EPSILON = 1e-06
MASKED = -1e30
MIB = 1 << 20
ROWS_BY_ROWS = (((1,), (1,)), ((), ()))
ROWS_BY_COLS = (((1,), (0,)), ((), ()))


def dot(a, b, dims=ROWS_BY_COLS):
    return lax.dot_general(a, b, dims, preferred_element_type=jnp.float32)


def params(limit_mib=32):
    return pltpu.CompilerParams(vmem_limit_bytes=limit_mib * MIB)


def split(value, count):
    parts = []
    for _ in range(count):
        part = value.astype(jnp.bfloat16)
        parts.append(part)
        value = value - part.astype(jnp.float32)
    return parts


def rms_rows(widened, gain_row):
    inverse = lax.rsqrt(jnp.mean(widened * widened, axis=-1, keepdims=True) + EPSILON)
    return (widened * inverse * gain_row).astype(jnp.bfloat16)


def copy_rows(source_ref, rows_ref):
    requests, steps, _ = source_ref.shape
    for r in range(requests):
        rows_ref[r * steps : (r + 1) * steps, :] = source_ref[r].astype(rows_ref.dtype)


def qkv_kernel(tokens_ref, gain_ref, weight_ref, out_ref, token_buf, gain_buf, weight_buf, rows_ref, sems):
    copies = [
        pltpu.make_async_copy(source, target, sems.at[i])
        for i, (source, target) in enumerate(
            ((tokens_ref, token_buf), (gain_ref, gain_buf), (weight_ref, weight_buf))
        )
    ]
    for copy in copies:
        copy.start()
    for copy in copies:
        copy.wait()
    copy_rows(token_buf, rows_ref)
    normed = rms_rows(rows_ref[...], gain_buf[...])
    out_ref[...] = dot(normed, weight_buf[...], ROWS_BY_ROWS).astype(jnp.bfloat16)


def in_order(place, near_ref, far_ref, ordered_ref):
    for j in range(near_ref.shape[0]):
        ordered_ref[jnp.bitwise_xor(place, 2 * j)] = near_ref[j]
        ordered_ref[jnp.bitwise_xor(place, 2 * j + 1)] = far_ref[j]


def head_masks(rows, width, steps):
    row_head = lax.broadcasted_iota(jnp.int32, (rows, width), 0) // steps % BLOCK_HEADS
    col_head = lax.broadcasted_iota(jnp.int32, (rows, width), 1) // HD % BLOCK_HEADS
    return (row_head == col_head).astype(jnp.float32)


def attention_kernel(
    place_ref, lengths_ref, near_ref, far_ref, window_ref, out_ref, ordered_ref, flat_ref, query_ref
):
    devices, rows, share = ordered_ref.shape
    _, requests, span, width = window_ref.shape
    steps = rows // requests
    block_rows = BLOCK_HEADS * steps
    place = place_ref[0]
    in_order(place, near_ref, far_ref, ordered_ref)
    for d in range(devices):
        if d * share < width:
            flat_ref[:, d * share : (d + 1) * share] = ordered_ref[d].astype(jnp.float32)
    own_head = head_masks(block_rows, width, steps)
    for r in range(requests):
        queries = flat_ref[r * steps : (r + 1) * steps, 0:width]
        query_ref[r] = (jnp.concatenate([queries] * BLOCK_HEADS, axis=0) * own_head).astype(
            jnp.bfloat16
        )
    base = place * span
    scale = HD ** (-0.5)
    pair = 2 * steps
    tiles = HEADS * steps // pair
    slot = base + lax.broadcasted_iota(jnp.int32, (pair, span), 1)
    step = lax.broadcasted_iota(jnp.int32, (pair, span), 0) % steps
    stat_lane = lax.broadcasted_iota(jnp.int32, (HEADS * steps, LANES), 1)
    stat_head = lax.broadcasted_iota(jnp.int32, (HEADS * steps, LANES), 0) // steps
    cols = [slice(c, c + BLOCK) for c in range(0, width, BLOCK)]

    def score(r):
        return jnp.concatenate(
            [dot(query_ref[r, :, c], window_ref[0, r, :, c], ROWS_BY_ROWS) for c in cols], axis=0
        )

    scores = score(0)
    for r in range(requests):
        following = score(r + 1) if r + 1 < requests else None
        length = lengths_ref[r]
        age = jnp.bitwise_and(slot - (length - SINKS), WIN - 1)
        live = ((slot < jnp.minimum(WIN, length - SINKS)) & (age > step))[None]
        scores = jnp.where(live, scores.reshape(tiles, pair, span) * scale, MASKED)
        peak = jnp.max(scores, axis=-1, keepdims=True)
        weight = jnp.where(live, jnp.exp(scores - peak), 0.0)
        total = jnp.sum(weight, axis=-1, keepdims=True)
        weight = weight.reshape(HEADS * steps, span).astype(jnp.bfloat16)
        outs = []
        for b, c in enumerate(cols):
            own = slice(b * block_rows, (b + 1) * block_rows)
            mixed = dot(weight[own], window_ref[1, r, :, c]) * own_head[:, c]
            mixed = sum(mixed[i : i + pair] for i in range(0, block_rows, pair))
            outs.append(mixed[:steps] + mixed[steps:])
        stats = jnp.zeros((HEADS * steps, LANES), jnp.float32)
        parts = split(peak.reshape(HEADS * steps, 1), PIECES)
        parts = parts + split(total.reshape(HEADS * steps, 1), PIECES)
        for i, part in enumerate(parts):
            stats = jnp.where(
                stat_lane == stat_head + i * HEADS, part.astype(jnp.float32), stats
            )
        stats = jnp.sum(stats.reshape(tiles, pair, LANES), axis=0)
        outs.append(stats[:steps] + stats[steps:])
        flat_ref[r * steps : (r + 1) * steps, :] = jnp.concatenate(outs, axis=1)
        scores = following
    out_ref[...] = flat_ref[...].astype(jnp.bfloat16)


def extra_kernel(
    place_ref, near_ref, far_ref, sinks_ref, out_ref, stats_ref, ordered_ref, flat_ref, query_ref, keys_ref
):
    devices, rows, share = ordered_ref.shape
    _, requests, sinks, width = sinks_ref.shape
    steps = rows // requests
    block_rows = BLOCK_HEADS * steps
    count = sinks + steps
    in_order(place_ref[0], near_ref, far_ref, ordered_ref)
    for d in range(devices):
        flat_ref[:, d * share : (d + 1) * share] = ordered_ref[d].astype(jnp.float32)
    own_head = head_masks(block_rows, width, steps)
    for r in range(requests):
        own = slice(r * steps, (r + 1) * steps)
        queries = jnp.concatenate([flat_ref[own, 0:width]] * BLOCK_HEADS, axis=0) * own_head
        query_ref[r * block_rows : (r + 1) * block_rows, :] = queries
        for p in range(2):
            keys_ref[p, r * count : r * count + sinks] = sinks_ref[p, r].astype(jnp.float32)
            keys_ref[p, r * count + sinks : (r + 1) * count] = flat_ref[
                own, (p + 1) * width : (p + 2) * width
            ]
    all_rows = requests * block_rows
    all_keys = requests * count
    row = lax.broadcasted_iota(jnp.int32, (all_rows, all_keys), 0)
    key = lax.broadcasted_iota(jnp.int32, (all_rows, all_keys), 1)
    live = (row // block_rows == key // count) & (key % count - sinks <= row % steps)
    stat_lane = lax.broadcasted_iota(jnp.int32, (all_rows, LANES), 1)
    stat_head = lax.broadcasted_iota(jnp.int32, (all_rows, LANES), 0) % block_rows // steps
    whole_mask = jnp.concatenate([own_head[:, :BLOCK]] * requests, axis=0)
    stats = jnp.zeros((all_rows, LANES), jnp.float32)
    pair = 2 * steps

    def by_request(values):
        values = jnp.sum(values.reshape(requests, block_rows // pair, pair, values.shape[-1]), axis=1)
        return values[:, :steps] + values[:, steps:]

    for b in range(width // BLOCK):
        c = slice(b * BLOCK, (b + 1) * BLOCK)
        scores = dot(
            query_ref[:, c].astype(jnp.bfloat16), keys_ref[0, :, c].astype(jnp.bfloat16), ROWS_BY_ROWS
        )
        scores = jnp.where(live, scores * HD ** (-0.5), MASKED)
        peak = jnp.max(scores, axis=-1, keepdims=True)
        weight = jnp.where(live, jnp.exp(scores - peak), 0.0)
        total = jnp.sum(weight, axis=-1, keepdims=True)
        mixed = dot(weight.astype(jnp.bfloat16), keys_ref[1, :, c].astype(jnp.bfloat16))
        mixed = by_request(mixed * whole_mask)
        for r in range(requests):
            out_ref[r * steps : (r + 1) * steps, c] = mixed[r]
        stats = jnp.where(stat_lane == stat_head + b * BLOCK_HEADS, peak, stats)
        stats = jnp.where(stat_lane == stat_head + b * BLOCK_HEADS + HEADS, total, stats)
    stats = by_request(stats)
    for r in range(requests):
        stats_ref[r * steps : (r + 1) * steps, :] = stats[r]


def project_kernel(
    place_ref, near_ref, far_ref, extra_ref, extra_stats_ref, weight_ref, out_ref, ordered_ref
):
    devices, rows, padded = ordered_ref.shape
    width = padded - LANES
    in_order(place_ref[0], near_ref, far_ref, ordered_ref)
    stats = [ordered_ref[d][:, width:].astype(jnp.float32) for d in range(devices)]

    def joined(stat, first):
        return sum(
            stat[:, (first + i) * HEADS : (first + i + 1) * HEADS] for i in range(PIECES)
        )

    peaks = [joined(stat, 0) for stat in stats] + [extra_stats_ref[:, :HEADS]]
    totals = [joined(stat, PIECES) for stat in stats] + [extra_stats_ref[:, HEADS : 2 * HEADS]]
    overall = functools.reduce(jnp.maximum, peaks)
    factors = [jnp.exp(peak - overall) for peak in peaks]
    total = sum(f * t for f, t in zip(factors, totals))
    inverse = 1.0 / total
    head_of_row = lax.broadcasted_iota(jnp.int32, (HEADS, width), 0)
    head_of_col = lax.broadcasted_iota(jnp.int32, (HEADS, width), 1) // HD
    expand = (head_of_row == head_of_col).astype(jnp.bfloat16)

    def spread(factor):
        return sum(dot(part, expand) for part in split(factor * inverse, 2))

    attended = spread(factors[-1]) * extra_ref[...]
    for d in range(devices):
        attended = attended + spread(factors[d]) * ordered_ref[d][:, :width].astype(jnp.float32)
    out_ref[...] = dot(attended.astype(jnp.bfloat16), weight_ref[...], ROWS_BY_ROWS).astype(
        jnp.bfloat16
    )


def routing_kernel(ids_ref, order_ref, select_ref, turned_ref, chosen_ref, rows_ref):
    requests, steps, _ = ids_ref.shape
    rows = requests * steps
    for r in range(requests):
        rows_ref[r * steps : (r + 1) * steps, :] = ids_ref[r]
    lane = lax.broadcasted_iota(jnp.int32, (rows, LANES), 1)
    chosen = [rows_ref[:, c : c + 1] for c in range(TOPK)]
    onehot = [(lane == ids).astype(jnp.float32) for ids in chosen]
    across = order_ref[...]
    square_row = lax.broadcasted_iota(jnp.int32, (rows, rows), 0)
    square_col = lax.broadcasted_iota(jnp.int32, (rows, rows), 1)
    order_wide = jnp.broadcast_to(across, (rows, rows))
    down = jnp.sum(
        jnp.where(square_row == square_col, order_wide, 0).astype(jnp.float32),
        axis=1,
        keepdims=True,
    )
    earlier = (order_wide.astype(jnp.float32) < down).astype(jnp.bfloat16)
    counts = dot(earlier, sum(onehot).astype(jnp.bfloat16))
    slot = lax.broadcasted_iota(jnp.int32, (rows, EXPERTS * CAP), 1)
    both = jnp.zeros((rows, EXPERTS * CAP), jnp.float32)
    for c in range(TOPK):
        position = jnp.sum(onehot[c] * counts, axis=-1, keepdims=True).astype(jnp.int32)
        column = chosen[c] * CAP + position
        select = ((column == slot) & (position < CAP)).astype(jnp.float32)
        select_ref[c] = select
        chosen_ref[c] = onehot[c]
        both = both + select
    turned_ref[...] = jnp.transpose(both)


def residual_kernel(
    place_ref,
    own_ref,
    near_ref,
    far_ref,
    tokens_ref,
    gain_ref,
    turned_ref,
    normed_ref,
    residual_ref,
    send_ref,
    ordered_ref,
):
    devices, rows, share = ordered_ref.shape
    in_order(place_ref[0], near_ref, far_ref, ordered_ref)
    copy_rows(tokens_ref, residual_ref)
    for d in range(devices):
        own = slice(d * share, (d + 1) * share)
        residual_ref[:, own] = residual_ref[:, own] + ordered_ref[d].astype(jnp.float32)
    normed = rms_rows(residual_ref[...], gain_ref[...])
    normed_ref[...] = normed
    groups = send_ref.shape[0]
    local_experts = EXPERTS // groups
    for g in range(groups):
        first = pl.multiple_of((g * local_experts + own_ref[0]) * CAP, CAP)
        picking = turned_ref[pl.ds(first, CAP), :].astype(jnp.bfloat16)
        send_ref[g] = dot(picking, normed).astype(jnp.bfloat16)


def gate_kernel(normed_ref, router_ref, select_ref, chosen_ref, out_ref):
    logits = dot(normed_ref[...], router_ref[...])
    gates = jnp.zeros(select_ref.shape[1:], jnp.float32)
    for c in range(TOPK):
        logit = jnp.sum(chosen_ref[c][:, :EXPERTS] * logits, axis=-1, keepdims=True)
        gates = gates + jax.nn.sigmoid(logit) * select_ref[c]
    out_ref[...] = gates


def expert_kernel(odd_ref, rows_ref, in_ref, down_ref, keep_ref, send_ref):
    groups, slots, width = rows_ref.shape
    rows = rows_ref[...].reshape(groups * slots, width)
    gate = dot(rows, in_ref[0, 0], ROWS_BY_ROWS)
    up = dot(rows, in_ref[1, 0], ROWS_BY_ROWS)
    hidden = (jax.nn.gelu(gate, approximate=True) * up).astype(jnp.bfloat16)
    outputs = dot(hidden, down_ref[0])
    half = width // 2
    odd = odd_ref[0] == 1
    keep_ref[...] = jnp.where(odd, outputs[:, half:], outputs[:, :half])
    send_ref[...] = jnp.where(odd, outputs[:, :half], outputs[:, half:])


def column_block(sharer, sharers):
    block = 0
    while sharers > 1:
        sharers //= 2
        block += (sharer & 1) * sharers
        sharer >>= 1
    return block


def final_kernel(gates_ref, returned_ref, residual_ref, out_ref, table_ref):
    requests, steps, width = out_ref.shape
    devices, groups, slots, part = returned_ref.shape
    local_experts = EXPERTS // groups
    sharers = devices // local_experts
    for s in range(devices):
        first = column_block(s % sharers, sharers) * part
        for x in range(groups):
            row = (x * local_experts + s // sharers) * slots
            table_ref[row : row + slots, first : first + part] = returned_ref[s, x].astype(jnp.float32)
    table = table_ref[...].astype(jnp.bfloat16)
    moe = sum(dot(part, table) for part in split(gates_ref[...], 2))
    total = residual_ref[...] + moe
    for r in range(requests):
        out_ref[r] = total[r * steps : (r + 1) * steps].astype(jnp.bfloat16)


def gather_seq(values):
    count = lax.axis_size("seq")
    others = [
        lax.ppermute(values, "seq", [(i, i ^ k) for i in range(count)]) for k in range(2, count, 2)
    ]
    near = jnp.stack([values] + others)
    far = lax.ppermute(near, "seq", [(i, i ^ 1) for i in range(count)])
    return near, far


def shape(dims, dtype):
    return jax.ShapeDtypeStruct(dims, dtype)


def body(
    tokens,
    attn_gain,
    w_qkv,
    window_cache,
    sink_cache,
    lengths,
    w_out,
    moe_gain,
    router,
    expert_ids,
    slot_order,
    expert_in,
    expert_down,
):
    requests, steps, width = tokens.shape
    rows = requests * steps
    seq_index = lax.axis_index("seq")
    seq_count = lax.axis_size("seq")
    groups = lax.axis_size("exp")
    local_experts = EXPERTS // groups
    sharers = seq_count // local_experts
    own_expert = (seq_index // sharers).astype(jnp.int32).reshape(1)
    place = seq_index.astype(jnp.int32).reshape(1)
    span = window_cache.shape[2]
    share = w_qkv.shape[0]
    slots = EXPERTS * CAP
    f32, bf16 = jnp.float32, jnp.bfloat16

    smem = pl.BlockSpec(memory_space=pltpu.SMEM)
    vmem = pl.BlockSpec(memory_space=pltpu.VMEM)
    anywhere = pl.BlockSpec(memory_space=pl.ANY)

    gain_row = attn_gain.reshape(1, width)
    local_mix = pl.pallas_call(
        qkv_kernel,
        in_specs=[anywhere] * 3,
        out_shape=shape((rows, share), bf16),
        scratch_shapes=[
            pltpu.VMEM(tokens.shape, bf16),
            pltpu.VMEM(gain_row.shape, f32),
            pltpu.VMEM(w_qkv.shape, bf16),
            pltpu.VMEM((rows, width), f32),
            pltpu.SemaphoreType.DMA((3,)),
        ],
        compiler_params=params(4),
        name="qkv",
    )(tokens, gain_row, w_qkv)
    near_mix, far_mix = gather_seq(local_mix)

    padded = width + LANES
    part = pl.pallas_call(
        attention_kernel,
        in_specs=[smem, smem, vmem, vmem, vmem],
        out_shape=shape((rows, padded), bf16),
        scratch_shapes=[
            pltpu.VMEM((seq_count, rows, share), bf16),
            pltpu.VMEM((rows, padded), f32),
            pltpu.VMEM((requests, BLOCK_HEADS * steps, width), bf16),
        ],
        compiler_params=params(8),
        name="attention",
    )(place, lengths, near_mix, far_mix, window_cache)
    near_part, far_part = gather_seq(part)

    extra, extra_stats = pl.pallas_call(
        extra_kernel,
        in_specs=[smem, vmem, vmem, vmem],
        out_shape=(shape((rows, width), f32), shape((rows, LANES), f32)),
        scratch_shapes=[
            pltpu.VMEM((seq_count, rows, share), bf16),
            pltpu.VMEM((rows, 3 * width), f32),
            pltpu.VMEM((rows * BLOCK_HEADS, width), f32),
            pltpu.VMEM((2, requests * (SINKS + steps), width), f32),
        ],
        compiler_params=params(8),
        name="extra",
    )(place, near_mix, far_mix, sink_cache)

    local_proj = pl.pallas_call(
        project_kernel,
        in_specs=[smem] + [vmem] * 5,
        out_shape=shape((rows, w_out.shape[0]), bf16),
        scratch_shapes=[pltpu.VMEM((seq_count, rows, padded), bf16)],
        compiler_params=params(8),
        name="project",
    )(place, near_part, far_part, extra, extra_stats, w_out)
    near_proj, far_proj = gather_seq(local_proj)

    select, turned, chosen = pl.pallas_call(
        routing_kernel,
        out_shape=(
            shape((TOPK, rows, slots), f32),
            shape((slots, rows), f32),
            shape((TOPK, rows, LANES), f32),
        ),
        scratch_shapes=[pltpu.VMEM((rows, TOPK), jnp.int32)],
        compiler_params=params(8),
        name="routing",
    )(expert_ids, slot_order)

    normed, residual, send = pl.pallas_call(
        residual_kernel,
        in_specs=[smem, smem] + [vmem] * 5,
        out_shape=(
            shape((rows, width), bf16),
            shape((rows, width), f32),
            shape((groups, CAP, width), bf16),
        ),
        scratch_shapes=[pltpu.VMEM((seq_count, rows, w_out.shape[0]), bf16)],
        compiler_params=params(8),
        name="residual",
    )(place, own_expert, near_proj, far_proj, tokens, moe_gain.reshape(1, width), turned)
    received = lax.all_to_all(send, "exp", split_axis=0, concat_axis=0, tiled=True)

    gates = pl.pallas_call(
        gate_kernel,
        out_shape=shape((rows, slots), f32),
        compiler_params=params(8),
        name="gate",
    )(normed, router, select, chosen)

    odd = jnp.bitwise_and(place, 1)
    kept, sent = pl.pallas_call(
        expert_kernel,
        in_specs=[smem] + [vmem] * 3,
        out_shape=(
            shape((groups * CAP, width // 2), f32),
            shape((groups * CAP, width // 2), f32),
        ),
        compiler_params=params(8),
        name="expert",
    )(odd, received, expert_in, expert_down)

    reach = 1
    while True:
        kept = kept + lax.ppermute(sent, "seq", [(i, i ^ reach) for i in range(seq_count)])
        reach *= 2
        if reach >= sharers:
            break
        upper = (seq_index // reach) % 2 == 1
        low, high = jnp.split(kept, 2, axis=1)
        kept, sent = jnp.where(upper, high, low), jnp.where(upper, low, high)
    columns = kept.shape[1]
    outgoing = kept.astype(bf16).reshape(1, groups, CAP, columns)
    outgoing = jnp.broadcast_to(outgoing, (seq_count, groups, CAP, columns))
    returned = lax.all_to_all(
        outgoing.reshape(seq_count * groups, CAP, columns),
        ("seq", "exp"),
        split_axis=0,
        concat_axis=0,
        tiled=True,
    ).reshape(seq_count, groups, CAP, columns)

    return pl.pallas_call(
        final_kernel,
        out_shape=shape((requests, steps, width), bf16),
        scratch_shapes=[pltpu.VMEM((slots, width), f32)],
        compiler_params=params(8),
        name="final",
    )(gates, returned, residual)


def solution(mesh):
    in_specs = (
        P("exp", None, None),
        P(),
        P("seq", None),
        P(None, "exp", "seq", None),
        P(None, "exp", None, None),
        P("exp"),
        P("seq", None),
        P(),
        P(),
        P("exp", None, None),
        P("exp", None),
        P(None, "exp", "seq", None),
        P("exp", "seq", None),
    )
    out_specs = P("exp", None, None)
    return jax.shard_map(body, mesh=mesh, in_specs=in_specs, out_specs=out_specs, check_vma=False)
```

```python
import functools

import jax
import jax.numpy as jnp
from jax import lax
from jax.experimental import pallas as pl
from jax.experimental.pallas import tpu as pltpu
from jax.sharding import PartitionSpec as P

HEADS = 16
HD = 64
EXPERTS = 16
TOPK = 2
SINKS = 4
WIN = 4096
CAP = 8
LANES = 128
PIECES = 3
EARLY = 3
BLOCK = 256
BLOCK_HEADS = BLOCK // HD

EPSILON = 1e-06
MASKED = -1e30
MIB = 1 << 20
ROWS_BY_ROWS = (((1,), (1,)), ((), ()))
ROWS_BY_COLS = (((1,), (0,)), ((), ()))


def dot(a, b, dims=ROWS_BY_COLS):
    return lax.dot_general(a, b, dims, preferred_element_type=jnp.float32)


def params(limit_mib=32):
    return pltpu.CompilerParams(vmem_limit_bytes=limit_mib * MIB)


def moving(count):
    return pl.CostEstimate(flops=0, bytes_accessed=count, transcendentals=0)


def in_hbm(value):
    return pltpu.with_memory_space_constraint(value, pltpu.HBM)


def split(value, count):
    parts = []
    for _ in range(count):
        part = value.astype(jnp.bfloat16)
        parts.append(part)
        value = value - part.astype(jnp.float32)
    return parts


def rms_rows(widened, gain_row):
    inverse = lax.rsqrt(jnp.mean(widened * widened, axis=-1, keepdims=True) + EPSILON)
    return (widened * inverse * gain_row).astype(jnp.bfloat16)


def copy_rows(source_ref, rows_ref):
    requests, steps, _ = source_ref.shape
    for r in range(requests):
        rows_ref[r * steps : (r + 1) * steps, :] = source_ref[r].astype(rows_ref.dtype)


def qkv_kernel(tokens_ref, gain_ref, weight_ref, out_ref, token_buf, gain_buf, weight_buf, rows_ref, sems):
    copies = [
        pltpu.make_async_copy(source, target, sems.at[i])
        for i, (source, target) in enumerate(
            ((tokens_ref, token_buf), (gain_ref, gain_buf), (weight_ref, weight_buf))
        )
    ]
    for copy in copies:
        copy.start()
    for copy in copies:
        copy.wait()
    copy_rows(token_buf, rows_ref)
    normed = rms_rows(rows_ref[...], gain_buf[...])
    out_ref[...] = dot(normed, weight_buf[...], ROWS_BY_ROWS).astype(jnp.bfloat16)


def in_order(place, near_ref, far_ref, ordered_ref):
    for j in range(near_ref.shape[0]):
        ordered_ref[jnp.bitwise_xor(place, 2 * j)] = near_ref[j]
        ordered_ref[jnp.bitwise_xor(place, 2 * j + 1)] = far_ref[j]


def head_masks(rows, width, steps):
    row_head = lax.broadcasted_iota(jnp.int32, (rows, width), 0) // steps % BLOCK_HEADS
    col_head = lax.broadcasted_iota(jnp.int32, (rows, width), 1) // HD % BLOCK_HEADS
    return (row_head == col_head).astype(jnp.float32)


def fetch_window_kernel(
    early, sent_ref, window_ref, lengths_ref, held_ref, keys_ref, values_ref, spans_ref, numbers_ref, sems
):
    copies = [
        pltpu.make_async_copy(lengths_ref, numbers_ref, sems.at[0]),
        pltpu.make_async_copy(window_ref.at[0], keys_ref, sems.at[1]),
        pltpu.make_async_copy(window_ref.at[1, pl.ds(0, early)], values_ref, sems.at[2]),
    ]
    for copy in copies:
        copy.start()
    held_ref[...] = sent_ref[...]
    copies[0].wait()
    for r in range(spans_ref.shape[0]):
        spans_ref[r : r + 1, :] = jnp.full((1, LANES), numbers_ref[r], jnp.int32)
    copies[1].wait()
    copies[2].wait()


def fetch_experts_kernel(sent_ref, in_ref, down_ref, held_ref, in_out, down_out, sems):
    copies = [
        pltpu.make_async_copy(in_ref, in_out, sems.at[0]),
        pltpu.make_async_copy(down_ref, down_out, sems.at[1]),
    ]
    for copy in copies:
        copy.start()
    held_ref[...] = sent_ref[...]
    for copy in copies:
        copy.wait()


def attention_kernel(
    place_ref,
    spans_ref,
    near_ref,
    far_ref,
    keys_ref,
    values_ref,
    window_ref,
    out_ref,
    ordered_ref,
    flat_ref,
    query_ref,
    late_ref,
    sems,
):
    devices, rows, share = ordered_ref.shape
    requests, span, width = keys_ref.shape
    early = values_ref.shape[0]
    late = [
        pltpu.make_async_copy(window_ref.at[1, r], late_ref.at[r - early], sems.at[r - early])
        for r in range(early, requests)
    ]
    for copy in late:
        copy.start()
    steps = rows // requests
    block_rows = BLOCK_HEADS * steps
    place = place_ref[0]
    in_order(place, near_ref, far_ref, ordered_ref)
    for d in range(devices):
        if d * share < width:
            flat_ref[:, d * share : (d + 1) * share] = ordered_ref[d].astype(jnp.float32)
    own_head = head_masks(block_rows, width, steps)
    for r in range(requests):
        queries = flat_ref[r * steps : (r + 1) * steps, 0:width]
        query_ref[r] = (jnp.concatenate([queries] * BLOCK_HEADS, axis=0) * own_head).astype(
            jnp.bfloat16
        )
    base = place * span
    scale = HD ** (-0.5)
    pair = 2 * steps
    tiles = HEADS * steps // pair
    slot = base + lax.broadcasted_iota(jnp.int32, (pair, span), 1)
    step = lax.broadcasted_iota(jnp.int32, (pair, span), 0) % steps
    stat_lane = lax.broadcasted_iota(jnp.int32, (HEADS * steps, LANES), 1)
    stat_head = lax.broadcasted_iota(jnp.int32, (HEADS * steps, LANES), 0) // steps
    cols = [slice(c, c + BLOCK) for c in range(0, width, BLOCK)]

    def score(r):
        return jnp.concatenate(
            [dot(query_ref[r, :, c], keys_ref[r, :, c], ROWS_BY_ROWS) for c in cols], axis=0
        )

    scores = score(0)
    for r in range(requests):
        following = score(r + 1) if r + 1 < requests else None
        length = spans_ref[r : r + 1, 0:1]
        age = jnp.bitwise_and(slot - (length - SINKS), WIN - 1)
        live = ((slot < jnp.minimum(WIN, length - SINKS)) & (age > step))[None]
        scores = jnp.where(live, scores.reshape(tiles, pair, span) * scale, MASKED)
        peak = jnp.max(scores, axis=-1, keepdims=True)
        weight = jnp.where(live, jnp.exp(scores - peak), 0.0)
        total = jnp.sum(weight, axis=-1, keepdims=True)
        weight = weight.reshape(HEADS * steps, span).astype(jnp.bfloat16)
        if r >= early:
            late[r - early].wait()
        values = values_ref.at[r] if r < early else late_ref.at[r - early]
        outs = []
        for b, c in enumerate(cols):
            own = slice(b * block_rows, (b + 1) * block_rows)
            mixed = dot(weight[own], values[:, c]) * own_head[:, c]
            mixed = sum(mixed[i : i + pair] for i in range(0, block_rows, pair))
            outs.append(mixed[:steps] + mixed[steps:])
        stats = jnp.zeros((HEADS * steps, LANES), jnp.float32)
        parts = split(peak.reshape(HEADS * steps, 1), PIECES)
        parts = parts + split(total.reshape(HEADS * steps, 1), PIECES)
        for i, part in enumerate(parts):
            stats = jnp.where(
                stat_lane == stat_head + i * HEADS, part.astype(jnp.float32), stats
            )
        stats = jnp.sum(stats.reshape(tiles, pair, LANES), axis=0)
        outs.append(stats[:steps] + stats[steps:])
        flat_ref[r * steps : (r + 1) * steps, :] = jnp.concatenate(outs, axis=1)
        scores = following
    out_ref[...] = flat_ref[...].astype(jnp.bfloat16)


def extra_kernel(
    place_ref, near_ref, far_ref, sinks_ref, out_ref, stats_ref, ordered_ref, flat_ref, query_ref, keys_ref
):
    devices, rows, share = ordered_ref.shape
    _, requests, sinks, width = sinks_ref.shape
    steps = rows // requests
    block_rows = BLOCK_HEADS * steps
    count = sinks + steps
    in_order(place_ref[0], near_ref, far_ref, ordered_ref)
    for d in range(devices):
        flat_ref[:, d * share : (d + 1) * share] = ordered_ref[d].astype(jnp.float32)
    own_head = head_masks(block_rows, width, steps)
    for r in range(requests):
        own = slice(r * steps, (r + 1) * steps)
        queries = jnp.concatenate([flat_ref[own, 0:width]] * BLOCK_HEADS, axis=0) * own_head
        query_ref[r * block_rows : (r + 1) * block_rows, :] = queries
        for p in range(2):
            keys_ref[p, r * count : r * count + sinks] = sinks_ref[p, r].astype(jnp.float32)
            keys_ref[p, r * count + sinks : (r + 1) * count] = flat_ref[
                own, (p + 1) * width : (p + 2) * width
            ]
    all_rows = requests * block_rows
    all_keys = requests * count
    row = lax.broadcasted_iota(jnp.int32, (all_rows, all_keys), 0)
    key = lax.broadcasted_iota(jnp.int32, (all_rows, all_keys), 1)
    live = (row // block_rows == key // count) & (key % count - sinks <= row % steps)
    stat_lane = lax.broadcasted_iota(jnp.int32, (all_rows, LANES), 1)
    stat_head = lax.broadcasted_iota(jnp.int32, (all_rows, LANES), 0) % block_rows // steps
    whole_mask = jnp.concatenate([own_head[:, :BLOCK]] * requests, axis=0)
    stats = jnp.zeros((all_rows, LANES), jnp.float32)
    pair = 2 * steps

    def by_request(values):
        values = jnp.sum(values.reshape(requests, block_rows // pair, pair, values.shape[-1]), axis=1)
        return values[:, :steps] + values[:, steps:]

    for b in range(width // BLOCK):
        c = slice(b * BLOCK, (b + 1) * BLOCK)
        scores = dot(
            query_ref[:, c].astype(jnp.bfloat16), keys_ref[0, :, c].astype(jnp.bfloat16), ROWS_BY_ROWS
        )
        scores = jnp.where(live, scores * HD ** (-0.5), MASKED)
        peak = jnp.max(scores, axis=-1, keepdims=True)
        weight = jnp.where(live, jnp.exp(scores - peak), 0.0)
        total = jnp.sum(weight, axis=-1, keepdims=True)
        mixed = dot(weight.astype(jnp.bfloat16), keys_ref[1, :, c].astype(jnp.bfloat16))
        mixed = by_request(mixed * whole_mask)
        for r in range(requests):
            out_ref[r * steps : (r + 1) * steps, c] = mixed[r]
        stats = jnp.where(stat_lane == stat_head + b * BLOCK_HEADS, peak, stats)
        stats = jnp.where(stat_lane == stat_head + b * BLOCK_HEADS + HEADS, total, stats)
    stats = by_request(stats)
    for r in range(requests):
        stats_ref[r * steps : (r + 1) * steps, :] = stats[r]


def project_kernel(
    place_ref, near_ref, far_ref, extra_ref, extra_stats_ref, weight_ref, out_ref, ordered_ref
):
    devices, rows, padded = ordered_ref.shape
    width = padded - LANES
    in_order(place_ref[0], near_ref, far_ref, ordered_ref)
    stats = [ordered_ref[d][:, width:].astype(jnp.float32) for d in range(devices)]

    def joined(stat, first):
        return sum(
            stat[:, (first + i) * HEADS : (first + i + 1) * HEADS] for i in range(PIECES)
        )

    peaks = [joined(stat, 0) for stat in stats] + [extra_stats_ref[:, :HEADS]]
    totals = [joined(stat, PIECES) for stat in stats] + [extra_stats_ref[:, HEADS : 2 * HEADS]]
    overall = functools.reduce(jnp.maximum, peaks)
    factors = [jnp.exp(peak - overall) for peak in peaks]
    total = sum(f * t for f, t in zip(factors, totals))
    inverse = 1.0 / total
    head_of_row = lax.broadcasted_iota(jnp.int32, (HEADS, width), 0)
    head_of_col = lax.broadcasted_iota(jnp.int32, (HEADS, width), 1) // HD
    expand = (head_of_row == head_of_col).astype(jnp.bfloat16)

    def spread(factor):
        return sum(dot(part, expand) for part in split(factor * inverse, 2))

    attended = spread(factors[-1]) * extra_ref[...]
    for d in range(devices):
        attended = attended + spread(factors[d]) * ordered_ref[d][:, :width].astype(jnp.float32)
    out_ref[...] = dot(attended.astype(jnp.bfloat16), weight_ref[...], ROWS_BY_ROWS).astype(
        jnp.bfloat16
    )


def routing_kernel(ids_ref, order_ref, select_ref, turned_ref, chosen_ref, rows_ref):
    requests, steps, _ = ids_ref.shape
    rows = requests * steps
    for r in range(requests):
        rows_ref[r * steps : (r + 1) * steps, :] = ids_ref[r]
    lane = lax.broadcasted_iota(jnp.int32, (rows, LANES), 1)
    chosen = [rows_ref[:, c : c + 1] for c in range(TOPK)]
    onehot = [(lane == ids).astype(jnp.float32) for ids in chosen]
    across = order_ref[...]
    square_row = lax.broadcasted_iota(jnp.int32, (rows, rows), 0)
    square_col = lax.broadcasted_iota(jnp.int32, (rows, rows), 1)
    order_wide = jnp.broadcast_to(across, (rows, rows))
    down = jnp.sum(
        jnp.where(square_row == square_col, order_wide, 0).astype(jnp.float32),
        axis=1,
        keepdims=True,
    )
    earlier = (order_wide.astype(jnp.float32) < down).astype(jnp.bfloat16)
    counts = dot(earlier, sum(onehot).astype(jnp.bfloat16))
    slot = lax.broadcasted_iota(jnp.int32, (rows, EXPERTS * CAP), 1)
    both = jnp.zeros((rows, EXPERTS * CAP), jnp.float32)
    for c in range(TOPK):
        position = jnp.sum(onehot[c] * counts, axis=-1, keepdims=True).astype(jnp.int32)
        column = chosen[c] * CAP + position
        select = ((column == slot) & (position < CAP)).astype(jnp.float32)
        select_ref[c] = select
        chosen_ref[c] = onehot[c]
        both = both + select
    turned_ref[...] = jnp.transpose(both)


def residual_kernel(
    place_ref,
    own_ref,
    near_ref,
    far_ref,
    tokens_ref,
    gain_ref,
    turned_ref,
    normed_ref,
    residual_ref,
    *send_and_ordered_refs,
):
    *send_refs, ordered_ref = send_and_ordered_refs
    devices, rows, share = ordered_ref.shape
    in_order(place_ref[0], near_ref, far_ref, ordered_ref)
    copy_rows(tokens_ref, residual_ref)
    for d in range(devices):
        own = slice(d * share, (d + 1) * share)
        residual_ref[:, own] = residual_ref[:, own] + ordered_ref[d].astype(jnp.float32)
    normed = rms_rows(residual_ref[...], gain_ref[...])
    normed_ref[...] = normed
    local_experts = EXPERTS // len(send_refs)
    for k, send_ref in enumerate(send_refs):
        expert = jnp.bitwise_xor(own_ref[1], k) * local_experts + own_ref[0]
        picking = turned_ref[pl.ds(pl.multiple_of(expert * CAP, CAP), CAP), :].astype(jnp.bfloat16)
        send_ref[...] = dot(picking, normed).astype(jnp.bfloat16)


def gate_kernel(normed_ref, router_ref, select_ref, chosen_ref, out_ref):
    logits = dot(normed_ref[...], router_ref[...])
    gates = jnp.zeros(select_ref.shape[1:], jnp.float32)
    for c in range(TOPK):
        logit = jnp.sum(chosen_ref[c][:, :EXPERTS] * logits, axis=-1, keepdims=True)
        gates = gates + jax.nn.sigmoid(logit) * select_ref[c]
    out_ref[...] = gates


def expert_kernel(place_ref, own_ref, in_ref, down_ref, *refs):
    *received_refs, keep_ref, send_ref, rows_ref = refs
    groups, slots, width = rows_ref.shape
    for k, received_ref in enumerate(received_refs):
        rows_ref[jnp.bitwise_xor(own_ref[1], k)] = received_ref[...].astype(jnp.float32)
    rows = rows_ref[...].reshape(groups * slots, width).astype(jnp.bfloat16)
    gate = dot(rows, in_ref[0, 0], ROWS_BY_ROWS)
    up = dot(rows, in_ref[1, 0], ROWS_BY_ROWS)
    hidden = (jax.nn.gelu(gate, approximate=True) * up).astype(jnp.bfloat16)
    outputs = dot(hidden, down_ref[0])
    half = width // 2
    odd = jnp.bitwise_and(place_ref[0], 1) == 1
    keep_ref[...] = jnp.where(odd, outputs[:, half:], outputs[:, :half])
    send_ref[...] = jnp.where(odd, outputs[:, :half], outputs[:, half:])


def spread_kernel(kept_ref, other_ref, out_ref):
    slots = out_ref.shape[1]
    groups = kept_ref.shape[0] // slots
    outputs = kept_ref[...] + other_ref[...]
    for block in range(out_ref.shape[0]):
        first = block % groups * slots
        out_ref[block] = outputs[first : first + slots].astype(jnp.bfloat16)


def column_block(sharer, sharers):
    block = 0
    while sharers > 1:
        sharers //= 2
        block += (sharer & 1) * sharers
        sharer >>= 1
    return block


def final_kernel(gates_ref, returned_ref, residual_ref, out_ref, table_ref):
    requests, steps, width = out_ref.shape
    devices, groups, slots, part = returned_ref.shape
    local_experts = EXPERTS // groups
    sharers = devices // local_experts
    for s in range(devices):
        first = column_block(s % sharers, sharers) * part
        for x in range(groups):
            row = (x * local_experts + s // sharers) * slots
            table_ref[row : row + slots, first : first + part] = returned_ref[s, x].astype(jnp.float32)
    table = table_ref[...].astype(jnp.bfloat16)
    moe = sum(dot(part, table) for part in split(gates_ref[...], 2))
    total = residual_ref[...] + moe
    for r in range(requests):
        out_ref[r] = total[r * steps : (r + 1) * steps].astype(jnp.bfloat16)


def gather_seq(values, meanwhile=None):
    count = lax.axis_size("seq")
    others = [
        lax.ppermute(values, "seq", [(i, i ^ k) for i in range(count)]) for k in range(2, count, 2)
    ]
    if meanwhile is not None:
        values = meanwhile(values)
    near = jnp.stack([values] + others)
    far = lax.ppermute(near, "seq", [(i, i ^ 1) for i in range(count)])
    return near, far


def shape(dims, dtype):
    return jax.ShapeDtypeStruct(dims, dtype)


def body(
    tokens,
    attn_gain,
    w_qkv,
    window_cache,
    sink_cache,
    lengths,
    w_out,
    moe_gain,
    router,
    expert_ids,
    slot_order,
    expert_in,
    expert_down,
):
    requests, steps, width = tokens.shape
    rows = requests * steps
    seq_index = lax.axis_index("seq")
    seq_count = lax.axis_size("seq")
    groups = lax.axis_size("exp")
    local_experts = EXPERTS // groups
    sharers = seq_count // local_experts
    own_expert = jnp.stack([seq_index // sharers, lax.axis_index("exp")]).astype(jnp.int32)
    place = seq_index.astype(jnp.int32).reshape(1)
    span = window_cache.shape[2]
    share = w_qkv.shape[0]
    slots = EXPERTS * CAP
    f32, bf16 = jnp.float32, jnp.bfloat16

    smem = pl.BlockSpec(memory_space=pltpu.SMEM)
    vmem = pl.BlockSpec(memory_space=pltpu.VMEM)
    hbm = pl.BlockSpec(memory_space=pltpu.HBM)

    gain_row = attn_gain.reshape(1, width)
    local_mix = pl.pallas_call(
        qkv_kernel,
        in_specs=[hbm] * 3,
        out_shape=shape((rows, share), bf16),
        scratch_shapes=[
            pltpu.VMEM(tokens.shape, bf16),
            pltpu.VMEM(gain_row.shape, f32),
            pltpu.VMEM(w_qkv.shape, bf16),
            pltpu.VMEM((rows, width), f32),
            pltpu.SemaphoreType.DMA((3,)),
        ],
        compiler_params=params(4),
        name="qkv",
    )(in_hbm(tokens), in_hbm(gain_row), in_hbm(w_qkv))
    early = min(EARLY, requests - 1)
    fetched = {}

    def fetch_window(values):
        held, *fetched["window"] = pl.pallas_call(
            functools.partial(fetch_window_kernel, early),
            in_specs=[vmem, hbm, hbm],
            out_shape=(
                shape(values.shape, bf16),
                shape((requests, span, width), bf16),
                shape((early, span, width), bf16),
                shape((requests, LANES), jnp.int32),
            ),
            scratch_shapes=[pltpu.SMEM((requests,), jnp.int32), pltpu.SemaphoreType.DMA((3,))],
            compiler_params=params(8),
            cost_estimate=moving(window_cache.size),
            name="fetch_window",
        )(values, in_hbm(window_cache), in_hbm(lengths))
        return held

    def fetch_experts(values):
        held, *fetched["experts"] = pl.pallas_call(
            fetch_experts_kernel,
            in_specs=[vmem, hbm, hbm],
            out_shape=(
                shape(values.shape, bf16),
                shape(expert_in.shape, bf16),
                shape(expert_down.shape, bf16),
            ),
            scratch_shapes=[pltpu.SemaphoreType.DMA((2,))],
            compiler_params=params(8),
            cost_estimate=moving(2 * (expert_in.size + expert_down.size)),
            name="fetch_experts",
        )(values, in_hbm(expert_in), in_hbm(expert_down))
        return held

    near_mix, far_mix = gather_seq(local_mix, fetch_window)
    keys, values, spans = fetched["window"]

    padded = width + LANES
    part = pl.pallas_call(
        attention_kernel,
        in_specs=[smem] + [vmem] * 5 + [hbm],
        out_shape=shape((rows, padded), bf16),
        scratch_shapes=[
            pltpu.VMEM((seq_count, rows, share), bf16),
            pltpu.VMEM((rows, padded), f32),
            pltpu.VMEM((requests, BLOCK_HEADS * steps, width), bf16),
            pltpu.VMEM((requests - early, span, width), bf16),
            pltpu.SemaphoreType.DMA((requests - early,)),
        ],
        compiler_params=params(20),
        name="attention",
    )(place, spans, near_mix, far_mix, keys, values, in_hbm(window_cache))
    near_part, far_part = gather_seq(part, fetch_experts)
    local_in, local_down = fetched["experts"]

    extra, extra_stats = pl.pallas_call(
        extra_kernel,
        in_specs=[smem, vmem, vmem, vmem],
        out_shape=(shape((rows, width), f32), shape((rows, LANES), f32)),
        scratch_shapes=[
            pltpu.VMEM((seq_count, rows, share), bf16),
            pltpu.VMEM((rows, 3 * width), f32),
            pltpu.VMEM((rows * BLOCK_HEADS, width), f32),
            pltpu.VMEM((2, requests * (SINKS + steps), width), f32),
        ],
        compiler_params=params(8),
        name="extra",
    )(place, near_mix, far_mix, sink_cache)

    local_proj = pl.pallas_call(
        project_kernel,
        in_specs=[smem] + [vmem] * 5,
        out_shape=shape((rows, w_out.shape[0]), bf16),
        scratch_shapes=[pltpu.VMEM((seq_count, rows, padded), bf16)],
        compiler_params=params(8),
        name="project",
    )(place, near_part, far_part, extra, extra_stats, w_out)
    near_proj, far_proj = gather_seq(local_proj)

    select, turned, chosen = pl.pallas_call(
        routing_kernel,
        out_shape=(
            shape((TOPK, rows, slots), f32),
            shape((slots, rows), f32),
            shape((TOPK, rows, LANES), f32),
        ),
        scratch_shapes=[pltpu.VMEM((rows, TOPK), jnp.int32)],
        compiler_params=params(8),
        name="routing",
    )(expert_ids, slot_order)

    normed, residual, *send = pl.pallas_call(
        residual_kernel,
        in_specs=[smem, smem] + [vmem] * 5,
        out_shape=(
            shape((rows, width), bf16),
            shape((rows, width), f32),
            *[shape((CAP, width), bf16)] * groups,
        ),
        scratch_shapes=[pltpu.VMEM((seq_count, rows, w_out.shape[0]), bf16)],
        compiler_params=params(8),
        name="residual",
    )(place, own_expert, near_proj, far_proj, tokens, moe_gain.reshape(1, width), turned)
    received = [
        lax.ppermute(block, "exp", [(i, i ^ k) for i in range(groups)]) if k else block
        for k, block in enumerate(send)
    ]

    gates = pl.pallas_call(
        gate_kernel,
        out_shape=shape((rows, slots), f32),
        compiler_params=params(8),
        name="gate",
    )(normed, router, select, chosen)

    kept, sent = pl.pallas_call(
        expert_kernel,
        in_specs=[smem, smem] + [vmem] * (2 + groups),
        out_shape=(
            shape((groups * CAP, width // 2), f32),
            shape((groups * CAP, width // 2), f32),
        ),
        scratch_shapes=[pltpu.VMEM((groups, CAP, width), f32)],
        compiler_params=params(8),
        name="expert",
    )(place, own_expert, local_in, local_down, *received)

    reach = 1
    while True:
        other = lax.ppermute(sent, "seq", [(i, i ^ reach) for i in range(seq_count)])
        reach *= 2
        if reach >= sharers:
            break
        upper = (seq_index // reach) % 2 == 1
        low, high = jnp.split(kept + other, 2, axis=1)
        kept, sent = jnp.where(upper, high, low), jnp.where(upper, low, high)
    columns = kept.shape[1]
    outgoing = pl.pallas_call(
        spread_kernel,
        out_shape=shape((seq_count * groups, CAP, columns), bf16),
        compiler_params=params(8),
        name="spread",
    )(kept, other)
    returned = lax.all_to_all(
        outgoing,
        ("seq", "exp"),
        split_axis=0,
        concat_axis=0,
        tiled=True,
    ).reshape(seq_count, groups, CAP, columns)

    return pl.pallas_call(
        final_kernel,
        out_shape=shape((requests, steps, width), bf16),
        scratch_shapes=[pltpu.VMEM((slots, width), f32)],
        compiler_params=params(8),
        name="final",
    )(gates, returned, residual)


def solution(mesh):
    in_specs = (
        P("exp", None, None),
        P(),
        P("seq", None),
        P(None, "exp", "seq", None),
        P(None, "exp", None, None),
        P("exp"),
        P("seq", None),
        P(),
        P(),
        P("exp", None, None),
        P("exp", None),
        P(None, "exp", "seq", None),
        P("exp", "seq", None),
    )
    out_specs = P("exp", None, None)
    return jax.shard_map(body, mesh=mesh, in_specs=in_specs, out_specs=out_specs, check_vma=False)
```

```python
import functools

import jax
import jax.numpy as jnp
from jax import lax
from jax.experimental import pallas as pl
from jax.experimental.pallas import tpu as pltpu
from jax.sharding import PartitionSpec as P

HEADS = 16
HD = 64
EXPERTS = 16
TOPK = 2
SINKS = 4
WIN = 4096
CAP = 8
LANES = 128
PIECES = 3
EARLY = 3
BLOCK = 256
BLOCK_HEADS = BLOCK // HD

EPSILON = 1e-06
MASKED = -1e30
MIB = 1 << 20
ROWS_BY_ROWS = (((1,), (1,)), ((), ()))
ROWS_BY_COLS = (((1,), (0,)), ((), ()))


def dot(a, b, dims=ROWS_BY_COLS):
    return lax.dot_general(a, b, dims, preferred_element_type=jnp.float32)


def params(limit_mib=32):
    return pltpu.CompilerParams(vmem_limit_bytes=limit_mib * MIB)


def moving(count):
    return pl.CostEstimate(flops=0, bytes_accessed=count, transcendentals=0)


def in_hbm(value):
    return pltpu.with_memory_space_constraint(value, pltpu.HBM)


def split(value, count):
    parts = []
    for _ in range(count):
        part = value.astype(jnp.bfloat16)
        parts.append(part)
        value = value - part.astype(jnp.float32)
    return parts


def rms_rows(widened, gain_row):
    inverse = lax.rsqrt(jnp.mean(widened * widened, axis=-1, keepdims=True) + EPSILON)
    return (widened * inverse * gain_row).astype(jnp.bfloat16)


def copy_rows(source_ref, rows_ref):
    requests, steps, _ = source_ref.shape
    for r in range(requests):
        rows_ref[r * steps : (r + 1) * steps, :] = source_ref[r].astype(rows_ref.dtype)


def qkv_kernel(tokens_ref, gain_ref, weight_ref, out_ref, token_buf, gain_buf, weight_buf, rows_ref, sems):
    copies = [
        pltpu.make_async_copy(source, target, sems.at[i])
        for i, (source, target) in enumerate(
            ((tokens_ref, token_buf), (gain_ref, gain_buf), (weight_ref, weight_buf))
        )
    ]
    for copy in copies:
        copy.start()
    for copy in copies:
        copy.wait()
    copy_rows(token_buf, rows_ref)
    normed = rms_rows(rows_ref[...], gain_buf[...])
    out_ref[...] = dot(normed, weight_buf[...], ROWS_BY_ROWS).astype(jnp.bfloat16)


def in_order(sent_refs, ordered_ref):
    place = lax.axis_index("seq")
    for k, sent_ref in enumerate(sent_refs):
        ordered_ref[jnp.bitwise_xor(place, k)] = sent_ref[...]


def head_masks(rows, width, steps):
    row_head = lax.broadcasted_iota(jnp.int32, (rows, width), 0) // steps % BLOCK_HEADS
    col_head = lax.broadcasted_iota(jnp.int32, (rows, width), 1) // HD % BLOCK_HEADS
    return (row_head == col_head).astype(jnp.float32)


def fetch_window_kernel(
    early, sent_ref, window_ref, lengths_ref, held_ref, keys_ref, values_ref, spans_ref, numbers_ref, sems
):
    copies = [
        pltpu.make_async_copy(lengths_ref, numbers_ref, sems.at[0]),
        pltpu.make_async_copy(window_ref.at[0], keys_ref, sems.at[1]),
        pltpu.make_async_copy(window_ref.at[1, pl.ds(0, early)], values_ref, sems.at[2]),
    ]
    for copy in copies:
        copy.start()
    held_ref[...] = sent_ref[...]
    copies[0].wait()
    for r in range(spans_ref.shape[0]):
        spans_ref[r : r + 1, :] = jnp.full((1, LANES), numbers_ref[r], jnp.int32)
    copies[1].wait()
    copies[2].wait()


def fetch_experts_kernel(sent_ref, in_ref, down_ref, held_ref, in_out, down_out, sems):
    copies = [
        pltpu.make_async_copy(in_ref, in_out, sems.at[0]),
        pltpu.make_async_copy(down_ref, down_out, sems.at[1]),
    ]
    for copy in copies:
        copy.start()
    held_ref[...] = sent_ref[...]
    for copy in copies:
        copy.wait()


def attention_kernel(*refs):
    *mixed_refs, spans_ref, keys_ref, values_ref, window_ref = refs[:-6]
    out_ref, ordered_ref, flat_ref, query_ref, late_ref, sems = refs[-6:]
    devices, rows, share = ordered_ref.shape
    requests, span, width = keys_ref.shape
    early = values_ref.shape[0]
    late = [
        pltpu.make_async_copy(window_ref.at[1, r], late_ref.at[r - early], sems.at[r - early])
        for r in range(early, requests)
    ]
    for copy in late:
        copy.start()
    steps = rows // requests
    block_rows = BLOCK_HEADS * steps
    place = lax.axis_index("seq")
    in_order(mixed_refs, ordered_ref)
    for d in range(devices):
        if d * share < width:
            flat_ref[:, d * share : (d + 1) * share] = ordered_ref[d].astype(jnp.float32)
    own_head = head_masks(block_rows, width, steps)
    for r in range(requests):
        queries = flat_ref[r * steps : (r + 1) * steps, 0:width]
        query_ref[r] = (jnp.concatenate([queries] * BLOCK_HEADS, axis=0) * own_head).astype(
            jnp.bfloat16
        )
    base = place * span
    scale = HD ** (-0.5)
    pair = 2 * steps
    tiles = HEADS * steps // pair
    slot = base + lax.broadcasted_iota(jnp.int32, (pair, span), 1)
    step = lax.broadcasted_iota(jnp.int32, (pair, span), 0) % steps
    stat_lane = lax.broadcasted_iota(jnp.int32, (HEADS * steps, LANES), 1)
    stat_head = lax.broadcasted_iota(jnp.int32, (HEADS * steps, LANES), 0) // steps
    cols = [slice(c, c + BLOCK) for c in range(0, width, BLOCK)]

    def score(r):
        return jnp.concatenate(
            [dot(query_ref[r, :, c], keys_ref[r, :, c], ROWS_BY_ROWS) for c in cols], axis=0
        )

    scores = score(0)
    for r in range(requests):
        following = score(r + 1) if r + 1 < requests else None
        length = spans_ref[r : r + 1, 0:1]
        age = jnp.bitwise_and(slot - (length - SINKS), WIN - 1)
        live = ((slot < jnp.minimum(WIN, length - SINKS)) & (age > step))[None]
        scores = jnp.where(live, scores.reshape(tiles, pair, span) * scale, MASKED)
        peak = jnp.max(scores, axis=-1, keepdims=True)
        weight = jnp.where(live, jnp.exp(scores - peak), 0.0)
        total = jnp.sum(weight, axis=-1, keepdims=True)
        weight = weight.reshape(HEADS * steps, span).astype(jnp.bfloat16)
        if r >= early:
            late[r - early].wait()
        values = values_ref.at[r] if r < early else late_ref.at[r - early]
        outs = []
        for b, c in enumerate(cols):
            own = slice(b * block_rows, (b + 1) * block_rows)
            mixed = dot(weight[own], values[:, c]) * own_head[:, c]
            mixed = sum(mixed[i : i + pair] for i in range(0, block_rows, pair))
            outs.append(mixed[:steps] + mixed[steps:])
        stats = jnp.zeros((HEADS * steps, LANES), jnp.float32)
        parts = split(peak.reshape(HEADS * steps, 1), PIECES)
        parts = parts + split(total.reshape(HEADS * steps, 1), PIECES)
        for i, part in enumerate(parts):
            stats = jnp.where(
                stat_lane == stat_head + i * HEADS, part.astype(jnp.float32), stats
            )
        stats = jnp.sum(stats.reshape(tiles, pair, LANES), axis=0)
        outs.append(stats[:steps] + stats[steps:])
        flat_ref[r * steps : (r + 1) * steps, :] = jnp.concatenate(outs, axis=1)
        scores = following
    out_ref[...] = flat_ref[...].astype(jnp.bfloat16)


def extra_kernel(*refs):
    *mixed_refs, sinks_ref = refs[:-6]
    out_ref, stats_ref, ordered_ref, flat_ref, query_ref, keys_ref = refs[-6:]
    devices, rows, share = ordered_ref.shape
    _, requests, sinks, width = sinks_ref.shape
    steps = rows // requests
    block_rows = BLOCK_HEADS * steps
    count = sinks + steps
    in_order(mixed_refs, ordered_ref)
    for d in range(devices):
        flat_ref[:, d * share : (d + 1) * share] = ordered_ref[d].astype(jnp.float32)
    own_head = head_masks(block_rows, width, steps)
    for r in range(requests):
        own = slice(r * steps, (r + 1) * steps)
        queries = jnp.concatenate([flat_ref[own, 0:width]] * BLOCK_HEADS, axis=0) * own_head
        query_ref[r * block_rows : (r + 1) * block_rows, :] = queries
        for p in range(2):
            keys_ref[p, r * count : r * count + sinks] = sinks_ref[p, r].astype(jnp.float32)
            keys_ref[p, r * count + sinks : (r + 1) * count] = flat_ref[
                own, (p + 1) * width : (p + 2) * width
            ]
    all_rows = requests * block_rows
    all_keys = requests * count
    row = lax.broadcasted_iota(jnp.int32, (all_rows, all_keys), 0)
    key = lax.broadcasted_iota(jnp.int32, (all_rows, all_keys), 1)
    live = (row // block_rows == key // count) & (key % count - sinks <= row % steps)
    stat_lane = lax.broadcasted_iota(jnp.int32, (all_rows, LANES), 1)
    stat_head = lax.broadcasted_iota(jnp.int32, (all_rows, LANES), 0) % block_rows // steps
    whole_mask = jnp.concatenate([own_head[:, :BLOCK]] * requests, axis=0)
    stats = jnp.zeros((all_rows, LANES), jnp.float32)
    pair = 2 * steps

    def by_request(values):
        values = jnp.sum(values.reshape(requests, block_rows // pair, pair, values.shape[-1]), axis=1)
        return values[:, :steps] + values[:, steps:]

    for b in range(width // BLOCK):
        c = slice(b * BLOCK, (b + 1) * BLOCK)
        scores = dot(
            query_ref[:, c].astype(jnp.bfloat16), keys_ref[0, :, c].astype(jnp.bfloat16), ROWS_BY_ROWS
        )
        scores = jnp.where(live, scores * HD ** (-0.5), MASKED)
        peak = jnp.max(scores, axis=-1, keepdims=True)
        weight = jnp.where(live, jnp.exp(scores - peak), 0.0)
        total = jnp.sum(weight, axis=-1, keepdims=True)
        mixed = dot(weight.astype(jnp.bfloat16), keys_ref[1, :, c].astype(jnp.bfloat16))
        mixed = by_request(mixed * whole_mask)
        for r in range(requests):
            out_ref[r * steps : (r + 1) * steps, c] = mixed[r]
        stats = jnp.where(stat_lane == stat_head + b * BLOCK_HEADS, peak, stats)
        stats = jnp.where(stat_lane == stat_head + b * BLOCK_HEADS + HEADS, total, stats)
    stats = by_request(stats)
    for r in range(requests):
        stats_ref[r * steps : (r + 1) * steps, :] = stats[r]


def project_kernel(*refs):
    *part_refs, extra_ref, extra_stats_ref, weight_ref, out_ref, ordered_ref = refs
    devices, rows, padded = ordered_ref.shape
    width = padded - LANES
    in_order(part_refs, ordered_ref)
    stats = [ordered_ref[d][:, width:].astype(jnp.float32) for d in range(devices)]

    def joined(stat, first):
        return sum(
            stat[:, (first + i) * HEADS : (first + i + 1) * HEADS] for i in range(PIECES)
        )

    peaks = [joined(stat, 0) for stat in stats] + [extra_stats_ref[:, :HEADS]]
    totals = [joined(stat, PIECES) for stat in stats] + [extra_stats_ref[:, HEADS : 2 * HEADS]]
    overall = functools.reduce(jnp.maximum, peaks)
    factors = [jnp.exp(peak - overall) for peak in peaks]
    total = sum(f * t for f, t in zip(factors, totals))
    inverse = 1.0 / total
    head_of_row = lax.broadcasted_iota(jnp.int32, (HEADS, width), 0)
    head_of_col = lax.broadcasted_iota(jnp.int32, (HEADS, width), 1) // HD
    expand = (head_of_row == head_of_col).astype(jnp.bfloat16)

    def spread(factor):
        return sum(dot(part, expand) for part in split(factor * inverse, 2))

    attended = spread(factors[-1]) * extra_ref[...]
    for d in range(devices):
        attended = attended + spread(factors[d]) * ordered_ref[d][:, :width].astype(jnp.float32)
    out_ref[...] = dot(attended.astype(jnp.bfloat16), weight_ref[...], ROWS_BY_ROWS).astype(
        jnp.bfloat16
    )


def routing_kernel(ids_ref, order_ref, select_ref, turned_ref, chosen_ref):
    steps, _, requests = ids_ref.shape
    rows = requests * steps
    lane = lax.broadcasted_iota(jnp.int32, (rows, LANES), 1)
    own_row = lax.broadcasted_iota(jnp.int32, (rows, requests), 0)
    own_request = lax.broadcasted_iota(jnp.int32, (rows, requests), 1) == own_row // steps
    chosen = []
    for c in range(TOPK):
        ids = jnp.zeros((rows, requests), jnp.int32)
        for t in range(steps):
            ids = jnp.where(own_request & (own_row % steps == t), ids_ref[t, c : c + 1, :], ids)
        chosen.append(jnp.sum(ids.astype(jnp.float32), axis=1, keepdims=True).astype(jnp.int32))
    onehot = [(lane == ids).astype(jnp.float32) for ids in chosen]
    across = order_ref[...]
    square_row = lax.broadcasted_iota(jnp.int32, (rows, rows), 0)
    square_col = lax.broadcasted_iota(jnp.int32, (rows, rows), 1)
    order_wide = jnp.broadcast_to(across, (rows, rows))
    down = jnp.sum(
        jnp.where(square_row == square_col, order_wide, 0).astype(jnp.float32),
        axis=1,
        keepdims=True,
    )
    earlier = (order_wide.astype(jnp.float32) < down).astype(jnp.bfloat16)
    counts = dot(earlier, sum(onehot).astype(jnp.bfloat16))
    slot = lax.broadcasted_iota(jnp.int32, (rows, EXPERTS * CAP), 1)
    both = jnp.zeros((rows, EXPERTS * CAP), jnp.float32)
    for c in range(TOPK):
        position = jnp.sum(onehot[c] * counts, axis=-1, keepdims=True).astype(jnp.int32)
        column = chosen[c] * CAP + position
        select = ((column == slot) & (position < CAP)).astype(jnp.float32)
        select_ref[c] = select
        chosen_ref[c] = onehot[c]
        both = both + select
    turned_ref[...] = jnp.transpose(both)


def residual_kernel(devices, *refs):
    projected_refs, refs = refs[:devices], refs[devices:]
    tokens_ref, gain_ref, turned_ref, normed_ref, residual_ref, *send_refs, ordered_ref = refs
    share = ordered_ref.shape[2]
    in_order(projected_refs, ordered_ref)
    copy_rows(tokens_ref, residual_ref)
    for d in range(devices):
        own = slice(d * share, (d + 1) * share)
        residual_ref[:, own] = residual_ref[:, own] + ordered_ref[d].astype(jnp.float32)
    normed = rms_rows(residual_ref[...], gain_ref[...])
    normed_ref[...] = normed
    local_experts = EXPERTS // len(send_refs)
    own = lax.axis_index("seq") // (devices // local_experts)
    for k, send_ref in enumerate(send_refs):
        expert = jnp.bitwise_xor(lax.axis_index("exp"), k) * local_experts + own
        picking = turned_ref[pl.ds(pl.multiple_of(expert * CAP, CAP), CAP), :].astype(jnp.bfloat16)
        send_ref[...] = dot(picking, normed).astype(jnp.bfloat16)


def gate_kernel(normed_ref, router_ref, select_ref, chosen_ref, out_ref):
    logits = dot(normed_ref[...], router_ref[...], ROWS_BY_ROWS)
    gates = jnp.zeros(select_ref.shape[1:], jnp.float32)
    for c in range(TOPK):
        logit = jnp.sum(chosen_ref[c][:, :EXPERTS] * logits, axis=-1, keepdims=True)
        gates = gates + jax.nn.sigmoid(logit) * select_ref[c]
    out_ref[...] = gates


def expert_kernel(in_ref, down_ref, *refs):
    *received_refs, keep_ref, send_ref, rows_ref = refs
    groups, slots, width = rows_ref.shape
    for k, received_ref in enumerate(received_refs):
        rows_ref[jnp.bitwise_xor(lax.axis_index("exp"), k)] = received_ref[...].astype(jnp.float32)
    rows = rows_ref[...].reshape(groups * slots, width).astype(jnp.bfloat16)
    gate = dot(rows, in_ref[0, 0], ROWS_BY_ROWS)
    up = dot(rows, in_ref[1, 0], ROWS_BY_ROWS)
    hidden = (jax.nn.gelu(gate, approximate=True) * up).astype(jnp.bfloat16)
    outputs = dot(hidden, down_ref[0])
    half = width // 2
    odd = lax.axis_index("seq") % 2 == 1
    keep_ref[...] = jnp.where(odd, outputs[:, half:], outputs[:, :half])
    send_ref[...] = jnp.where(odd, outputs[:, :half], outputs[:, half:])


def spread_kernel(kept_ref, other_ref, out_ref):
    slots = out_ref.shape[1]
    groups = kept_ref.shape[0] // slots
    outputs = kept_ref[...] + other_ref[...]
    for block in range(out_ref.shape[0]):
        first = block % groups * slots
        out_ref[block] = outputs[first : first + slots].astype(jnp.bfloat16)


def column_block(sharer, sharers):
    block = 0
    while sharers > 1:
        sharers //= 2
        block += (sharer & 1) * sharers
        sharer >>= 1
    return block


def final_kernel(gates_ref, returned_ref, residual_ref, out_ref, table_ref):
    requests, steps, width = out_ref.shape
    devices, groups, slots, part = returned_ref.shape
    local_experts = EXPERTS // groups
    sharers = devices // local_experts
    for s in range(devices):
        first = column_block(s % sharers, sharers) * part
        for x in range(groups):
            row = (x * local_experts + s // sharers) * slots
            table_ref[row : row + slots, first : first + part] = returned_ref[s, x].astype(jnp.float32)
    table = table_ref[...].astype(jnp.bfloat16)
    moe = sum(dot(part, table) for part in split(gates_ref[...], 2))
    total = residual_ref[...] + moe
    for r in range(requests):
        out_ref[r] = total[r * steps : (r + 1) * steps].astype(jnp.bfloat16)


def gather_seq(values, meanwhile=None):
    count = lax.axis_size("seq")

    def exchange(value, bits):
        return lax.ppermute(value, "seq", [(i, i ^ bits) for i in range(count)])

    near = [exchange(values, k) for k in range(2, count, 2)]
    if meanwhile is not None:
        values = meanwhile(values)
    near = [values] + near
    return [part for value in near for part in (value, exchange(value, 1))]


def shape(dims, dtype):
    return jax.ShapeDtypeStruct(dims, dtype)


def body(
    tokens,
    attn_gain,
    w_qkv,
    window_cache,
    sink_cache,
    lengths,
    w_out,
    moe_gain,
    router,
    expert_ids,
    slot_order,
    expert_in,
    expert_down,
):
    requests, steps, width = tokens.shape
    rows = requests * steps
    seq_index = lax.axis_index("seq")
    seq_count = lax.axis_size("seq")
    groups = lax.axis_size("exp")
    local_experts = EXPERTS // groups
    sharers = seq_count // local_experts
    span = window_cache.shape[2]
    share = w_qkv.shape[0]
    slots = EXPERTS * CAP
    f32, bf16 = jnp.float32, jnp.bfloat16

    vmem = pl.BlockSpec(memory_space=pltpu.VMEM)
    hbm = pl.BlockSpec(memory_space=pltpu.HBM)

    gain_row = attn_gain.reshape(1, width)
    local_mix = pl.pallas_call(
        qkv_kernel,
        in_specs=[hbm] * 3,
        out_shape=shape((rows, share), bf16),
        scratch_shapes=[
            pltpu.VMEM(tokens.shape, bf16),
            pltpu.VMEM(gain_row.shape, f32),
            pltpu.VMEM(w_qkv.shape, bf16),
            pltpu.VMEM((rows, width), f32),
            pltpu.SemaphoreType.DMA((3,)),
        ],
        compiler_params=params(4),
        name="qkv",
    )(in_hbm(tokens), in_hbm(gain_row), in_hbm(w_qkv))
    early = min(EARLY, requests - 1)
    fetched = {}

    def fetch_window(values):
        held, *fetched["window"] = pl.pallas_call(
            functools.partial(fetch_window_kernel, early),
            in_specs=[vmem, hbm, hbm],
            out_shape=(
                shape(values.shape, bf16),
                shape((requests, span, width), bf16),
                shape((early, span, width), bf16),
                shape((requests, LANES), jnp.int32),
            ),
            scratch_shapes=[pltpu.SMEM((requests,), jnp.int32), pltpu.SemaphoreType.DMA((3,))],
            compiler_params=params(8),
            cost_estimate=moving(window_cache.size),
            name="fetch_window",
        )(values, in_hbm(window_cache), in_hbm(lengths))
        return held

    def fetch_experts(values):
        held, *fetched["experts"] = pl.pallas_call(
            fetch_experts_kernel,
            in_specs=[vmem, hbm, hbm],
            out_shape=(
                shape(values.shape, bf16),
                shape(expert_in.shape, bf16),
                shape(expert_down.shape, bf16),
            ),
            scratch_shapes=[pltpu.SemaphoreType.DMA((2,))],
            compiler_params=params(8),
            cost_estimate=moving(2 * (expert_in.size + expert_down.size)),
            name="fetch_experts",
        )(values, in_hbm(expert_in), in_hbm(expert_down))
        return held

    mixed = gather_seq(local_mix, fetch_window)
    keys, values, spans = fetched["window"]

    padded = width + LANES
    part = pl.pallas_call(
        attention_kernel,
        in_specs=[vmem] * (seq_count + 3) + [hbm],
        out_shape=shape((rows, padded), bf16),
        scratch_shapes=[
            pltpu.VMEM((seq_count, rows, share), bf16),
            pltpu.VMEM((rows, padded), f32),
            pltpu.VMEM((requests, BLOCK_HEADS * steps, width), bf16),
            pltpu.VMEM((requests - early, span, width), bf16),
            pltpu.SemaphoreType.DMA((requests - early,)),
        ],
        compiler_params=params(20),
        name="attention",
    )(*mixed, spans, keys, values, in_hbm(window_cache))
    parts = gather_seq(part, fetch_experts)
    local_in, local_down = fetched["experts"]

    extra, extra_stats = pl.pallas_call(
        extra_kernel,
        out_shape=(shape((rows, width), f32), shape((rows, LANES), f32)),
        scratch_shapes=[
            pltpu.VMEM((seq_count, rows, share), bf16),
            pltpu.VMEM((rows, 3 * width), f32),
            pltpu.VMEM((rows * BLOCK_HEADS, width), f32),
            pltpu.VMEM((2, requests * (SINKS + steps), width), f32),
        ],
        compiler_params=params(8),
        name="extra",
    )(*mixed, sink_cache)

    local_proj = pl.pallas_call(
        project_kernel,
        out_shape=shape((rows, w_out.shape[0]), bf16),
        scratch_shapes=[pltpu.VMEM((seq_count, rows, padded), bf16)],
        compiler_params=params(8),
        name="project",
    )(*parts, extra, extra_stats, w_out)
    projected = gather_seq(local_proj)

    select, turned, chosen = pl.pallas_call(
        routing_kernel,
        out_shape=(
            shape((TOPK, rows, slots), f32),
            shape((slots, rows), f32),
            shape((TOPK, rows, LANES), f32),
        ),
        compiler_params=params(8),
        name="routing",
    )(expert_ids.transpose(1, 2, 0), slot_order)

    normed, residual, *send = pl.pallas_call(
        functools.partial(residual_kernel, seq_count),
        out_shape=(
            shape((rows, width), bf16),
            shape((rows, width), f32),
            *[shape((CAP, width), bf16)] * groups,
        ),
        scratch_shapes=[pltpu.VMEM((seq_count, rows, w_out.shape[0]), bf16)],
        compiler_params=params(8),
        name="residual",
    )(*projected, tokens, moe_gain.reshape(1, width), turned)
    received = [
        lax.ppermute(block, "exp", [(i, i ^ k) for i in range(groups)]) if k else block
        for k, block in enumerate(send)
    ]

    gates = pl.pallas_call(
        gate_kernel,
        out_shape=shape((rows, slots), f32),
        compiler_params=params(8),
        name="gate",
    )(normed, router.T, select, chosen)

    kept, sent = pl.pallas_call(
        expert_kernel,
        out_shape=(
            shape((groups * CAP, width // 2), f32),
            shape((groups * CAP, width // 2), f32),
        ),
        scratch_shapes=[pltpu.VMEM((groups, CAP, width), f32)],
        compiler_params=params(8),
        name="expert",
    )(local_in, local_down, *received)

    reach = 1
    while True:
        other = lax.ppermute(sent, "seq", [(i, i ^ reach) for i in range(seq_count)])
        reach *= 2
        if reach >= sharers:
            break
        upper = (seq_index // reach) % 2 == 1
        low, high = jnp.split(kept + other, 2, axis=1)
        kept, sent = jnp.where(upper, high, low), jnp.where(upper, low, high)
    columns = kept.shape[1]
    outgoing = pl.pallas_call(
        spread_kernel,
        out_shape=shape((seq_count * groups, CAP, columns), bf16),
        compiler_params=params(8),
        name="spread",
    )(kept, other)
    returned = lax.all_to_all(
        outgoing,
        ("seq", "exp"),
        split_axis=0,
        concat_axis=0,
        tiled=True,
    ).reshape(seq_count, groups, CAP, columns)

    return pl.pallas_call(
        final_kernel,
        out_shape=shape((requests, steps, width), bf16),
        scratch_shapes=[pltpu.VMEM((slots, width), f32)],
        compiler_params=params(8),
        name="final",
    )(gates, returned, residual)


def solution(mesh):
    in_specs = (
        P("exp", None, None),
        P(),
        P("seq", None),
        P(None, "exp", "seq", None),
        P(None, "exp", None, None),
        P("exp"),
        P("seq", None),
        P(),
        P(),
        P("exp", None, None),
        P("exp", None),
        P(None, "exp", "seq", None),
        P("exp", "seq", None),
    )
    out_specs = P("exp", None, None)
    return jax.shard_map(body, mesh=mesh, in_specs=in_specs, out_specs=out_specs, check_vma=False)
```

```python
import functools

import jax
import jax.numpy as jnp
from jax import lax
from jax.experimental import pallas as pl
from jax.experimental.pallas import tpu as pltpu
from jax.sharding import PartitionSpec as P

HEADS = 16
HD = 64
EXPERTS = 16
TOPK = 2
SINKS = 4
WIN = 4096
CAP = 8
LANES = 128
PIECES = 3
EARLY = 3
PIECE = 512
BLOCK = 256
BLOCK_HEADS = BLOCK // HD

EPSILON = 1e-06
MASKED = -1e30
MIB = 1 << 20
ROWS_BY_ROWS = (((1,), (1,)), ((), ()))
ROWS_BY_COLS = (((1,), (0,)), ((), ()))


def dot(a, b, dims=ROWS_BY_COLS):
    return lax.dot_general(a, b, dims, preferred_element_type=jnp.float32)


def params(limit_mib=32):
    return pltpu.CompilerParams(vmem_limit_bytes=limit_mib * MIB)


def moving(count):
    return pl.CostEstimate(flops=0, bytes_accessed=count, transcendentals=0)


def in_hbm(value):
    return pltpu.with_memory_space_constraint(value, pltpu.HBM)


def split(value, count):
    parts = []
    for _ in range(count):
        part = value.astype(jnp.bfloat16)
        parts.append(part)
        value = value - part.astype(jnp.float32)
    return parts


def rms_rows(widened, gain_row):
    inverse = lax.rsqrt(jnp.mean(widened * widened, axis=-1, keepdims=True) + EPSILON)
    return (widened * inverse * gain_row).astype(jnp.bfloat16)


def copy_rows(source_ref, rows_ref):
    requests, steps, _ = source_ref.shape
    for r in range(requests):
        rows_ref[r * steps : (r + 1) * steps, :] = source_ref[r].astype(rows_ref.dtype)


def started(pairs, sems):
    copies = [pltpu.make_async_copy(*pair, sems.at[i]) for i, pair in enumerate(pairs)]
    for copy in copies:
        copy.start()
    return copies


def route(ids_ref, order_ref, select_ref, chosen_ref):
    steps, _, requests = ids_ref.shape
    rows = requests * steps
    lane = lax.broadcasted_iota(jnp.int32, (rows, LANES), 1)
    own_row = lax.broadcasted_iota(jnp.int32, (rows, requests), 0)
    own_request = lax.broadcasted_iota(jnp.int32, (rows, requests), 1) == own_row // steps
    chosen = []
    for c in range(TOPK):
        ids = jnp.zeros((rows, requests), jnp.int32)
        for t in range(steps):
            ids = jnp.where(own_request & (own_row % steps == t), ids_ref[t, c : c + 1, :], ids)
        chosen.append(jnp.sum(ids.astype(jnp.float32), axis=1, keepdims=True).astype(jnp.int32))
    onehot = [(lane == ids).astype(jnp.float32) for ids in chosen]
    square_row = lax.broadcasted_iota(jnp.int32, (rows, rows), 0)
    square_col = lax.broadcasted_iota(jnp.int32, (rows, rows), 1)
    order_wide = jnp.broadcast_to(order_ref[...], (rows, rows))
    down = jnp.sum(
        jnp.where(square_row == square_col, order_wide, 0).astype(jnp.float32),
        axis=1,
        keepdims=True,
    )
    earlier = (order_wide.astype(jnp.float32) < down).astype(jnp.bfloat16)
    counts = dot(earlier, sum(onehot).astype(jnp.bfloat16))
    slot = lax.broadcasted_iota(jnp.int32, (rows, EXPERTS * CAP), 1)
    both = jnp.zeros((rows, EXPERTS * CAP), jnp.float32)
    for c in range(TOPK):
        position = jnp.sum(onehot[c] * counts, axis=-1, keepdims=True).astype(jnp.int32)
        column = chosen[c] * CAP + position
        select = ((column == slot) & (position < CAP)).astype(jnp.float32)
        select_ref[c] = select
        chosen_ref[c] = onehot[c]
        both = both + select
    return jnp.transpose(both)


def qkv_kernel(tokens_ref, gain_ref, weight_ref, out_ref, token_buf, gain_buf, weight_buf, rows_ref, sems):
    copies = started(
        ((tokens_ref, token_buf), (gain_ref, gain_buf), (weight_ref, weight_buf)), sems
    )
    for copy in copies:
        copy.wait()
    copy_rows(token_buf, rows_ref)
    normed = rms_rows(rows_ref[...], gain_buf[...])
    out_ref[...] = dot(normed, weight_buf[...], ROWS_BY_ROWS).astype(jnp.bfloat16)


def in_order(sent_refs, ordered_ref):
    place = lax.axis_index("seq")
    for k, sent_ref in enumerate(sent_refs):
        ordered_ref[jnp.bitwise_xor(place, k)] = sent_ref[...]


def head_masks(rows, width, steps):
    row_head = lax.broadcasted_iota(jnp.int32, (rows, width), 0) // steps % BLOCK_HEADS
    col_head = lax.broadcasted_iota(jnp.int32, (rows, width), 1) // HD % BLOCK_HEADS
    return (row_head == col_head).astype(jnp.float32)


def fetch_window_kernel(
    sent_ref,
    window_ref,
    lengths_ref,
    ids_ref,
    order_ref,
    held_ref,
    keys_ref,
    values_ref,
    spans_ref,
    select_ref,
    chosen_ref,
    turned_ref,
    numbers_ref,
    ids_buf,
    order_buf,
    sems,
):
    copies = started(
        (
            (ids_ref, ids_buf),
            (order_ref, order_buf),
            (lengths_ref, numbers_ref),
            (window_ref.at[0], keys_ref),
            (window_ref.at[1, pl.ds(0, values_ref.shape[0])], values_ref),
        ),
        sems,
    )
    held_ref[...] = sent_ref[...]
    for copy in copies[:3]:
        copy.wait()
    turned_ref[...] = route(ids_buf, order_buf, select_ref, chosen_ref)
    for r in range(spans_ref.shape[0]):
        spans_ref[r : r + 1, :] = jnp.full((1, LANES), numbers_ref[r], jnp.int32)
    for copy in copies[3:]:
        copy.wait()


def attention_kernel(*refs):
    *mixed_refs, spans_ref, keys_ref, values_ref, window_ref = refs[:-6]
    out_ref, ordered_ref, flat_ref, query_ref, late_ref, sems = refs[-6:]
    devices, rows, share = ordered_ref.shape
    requests, span, width = keys_ref.shape
    early = values_ref.shape[0]
    late = [
        pltpu.make_async_copy(window_ref.at[1, r], late_ref.at[r - early], sems.at[r - early])
        for r in range(early, requests)
    ]
    for copy in late:
        copy.start()
    steps = rows // requests
    block_rows = BLOCK_HEADS * steps
    place = lax.axis_index("seq")
    in_order(mixed_refs, ordered_ref)
    for d in range(devices):
        if d * share < width:
            flat_ref[:, d * share : (d + 1) * share] = ordered_ref[d].astype(jnp.float32)
    own_head = head_masks(block_rows, width, steps)
    for r in range(requests):
        queries = flat_ref[r * steps : (r + 1) * steps, 0:width]
        query_ref[r] = (jnp.concatenate([queries] * BLOCK_HEADS, axis=0) * own_head).astype(
            jnp.bfloat16
        )
    base = place * span
    scale = HD ** (-0.5)
    pair = 2 * steps
    tiles = HEADS * steps // pair
    slot = base + lax.broadcasted_iota(jnp.int32, (pair, span), 1)
    step = lax.broadcasted_iota(jnp.int32, (pair, span), 0) % steps
    stat_lane = lax.broadcasted_iota(jnp.int32, (HEADS * steps, LANES), 1)
    stat_head = lax.broadcasted_iota(jnp.int32, (HEADS * steps, LANES), 0) // steps
    cols = [slice(c, c + BLOCK) for c in range(0, width, BLOCK)]

    def score(r):
        return jnp.concatenate(
            [dot(query_ref[r, :, c], keys_ref[r, :, c], ROWS_BY_ROWS) for c in cols], axis=0
        )

    scores = score(0)
    for r in range(requests):
        following = score(r + 1) if r + 1 < requests else None
        length = spans_ref[r : r + 1, 0:1]
        age = jnp.bitwise_and(slot - (length - SINKS), WIN - 1)
        live = ((slot < jnp.minimum(WIN, length - SINKS)) & (age > step))[None]
        scores = jnp.where(live, scores.reshape(tiles, pair, span) * scale, MASKED)
        peak = jnp.max(scores, axis=-1, keepdims=True)
        weight = jnp.where(live, jnp.exp(scores - peak), 0.0)
        total = jnp.sum(weight, axis=-1, keepdims=True)
        weight = weight.reshape(HEADS * steps, span).astype(jnp.bfloat16)
        if r >= early:
            late[r - early].wait()
        values = values_ref.at[r] if r < early else late_ref.at[r - early]
        outs = []
        for b, c in enumerate(cols):
            own = slice(b * block_rows, (b + 1) * block_rows)
            mixed = dot(weight[own], values[:, c]) * own_head[:, c]
            mixed = sum(mixed[i : i + pair] for i in range(0, block_rows, pair))
            outs.append(mixed[:steps] + mixed[steps:])
        stats = jnp.zeros((HEADS * steps, LANES), jnp.float32)
        parts = split(peak.reshape(HEADS * steps, 1), PIECES)
        parts = parts + split(total.reshape(HEADS * steps, 1), PIECES)
        for i, part in enumerate(parts):
            stats = jnp.where(
                stat_lane == stat_head + i * HEADS, part.astype(jnp.float32), stats
            )
        stats = jnp.sum(stats.reshape(tiles, pair, LANES), axis=0)
        outs.append(stats[:steps] + stats[steps:])
        flat_ref[r * steps : (r + 1) * steps, :] = jnp.concatenate(outs, axis=1)
        scores = following
    out_ref[...] = flat_ref[...].astype(jnp.bfloat16)


def extra_kernel(*refs):
    *mixed_refs, sinks_ref = refs[:-6]
    out_ref, stats_ref, ordered_ref, flat_ref, query_ref, keys_ref = refs[-6:]
    devices, rows, share = ordered_ref.shape
    _, requests, sinks, width = sinks_ref.shape
    steps = rows // requests
    block_rows = BLOCK_HEADS * steps
    count = sinks + steps
    in_order(mixed_refs, ordered_ref)
    for d in range(devices):
        flat_ref[:, d * share : (d + 1) * share] = ordered_ref[d].astype(jnp.float32)
    own_head = head_masks(block_rows, width, steps)
    for r in range(requests):
        own = slice(r * steps, (r + 1) * steps)
        queries = jnp.concatenate([flat_ref[own, 0:width]] * BLOCK_HEADS, axis=0) * own_head
        query_ref[r * block_rows : (r + 1) * block_rows, :] = queries
        for p in range(2):
            keys_ref[p, r * count : r * count + sinks] = sinks_ref[p, r].astype(jnp.float32)
            keys_ref[p, r * count + sinks : (r + 1) * count] = flat_ref[
                own, (p + 1) * width : (p + 2) * width
            ]
    all_rows = requests * block_rows
    all_keys = requests * count
    row = lax.broadcasted_iota(jnp.int32, (all_rows, all_keys), 0)
    key = lax.broadcasted_iota(jnp.int32, (all_rows, all_keys), 1)
    live = (row // block_rows == key // count) & (key % count - sinks <= row % steps)
    stat_lane = lax.broadcasted_iota(jnp.int32, (all_rows, LANES), 1)
    stat_head = lax.broadcasted_iota(jnp.int32, (all_rows, LANES), 0) % block_rows // steps
    whole_mask = jnp.concatenate([own_head[:, :BLOCK]] * requests, axis=0)
    stats = jnp.zeros((all_rows, LANES), jnp.float32)
    pair = 2 * steps

    def by_request(values):
        values = jnp.sum(values.reshape(requests, block_rows // pair, pair, values.shape[-1]), axis=1)
        return values[:, :steps] + values[:, steps:]

    for b in range(width // BLOCK):
        c = slice(b * BLOCK, (b + 1) * BLOCK)
        scores = dot(
            query_ref[:, c].astype(jnp.bfloat16), keys_ref[0, :, c].astype(jnp.bfloat16), ROWS_BY_ROWS
        )
        scores = jnp.where(live, scores * HD ** (-0.5), MASKED)
        peak = jnp.max(scores, axis=-1, keepdims=True)
        weight = jnp.where(live, jnp.exp(scores - peak), 0.0)
        total = jnp.sum(weight, axis=-1, keepdims=True)
        mixed = dot(weight.astype(jnp.bfloat16), keys_ref[1, :, c].astype(jnp.bfloat16))
        mixed = by_request(mixed * whole_mask)
        for r in range(requests):
            out_ref[r * steps : (r + 1) * steps, c] = mixed[r]
        stats = jnp.where(stat_lane == stat_head + b * BLOCK_HEADS, peak, stats)
        stats = jnp.where(stat_lane == stat_head + b * BLOCK_HEADS + HEADS, total, stats)
    stats = by_request(stats)
    for r in range(requests):
        stats_ref[r * steps : (r + 1) * steps, :] = stats[r]


def project_kernel(*refs):
    *part_refs, extra_ref, extra_stats_ref, weight_ref, tokens_ref, turned_ref = refs[:-4]
    out_ref, residual_ref, ordered_ref, rows_ref = refs[-4:]
    devices, rows, padded = ordered_ref.shape
    width = padded - LANES
    in_order(part_refs, ordered_ref)
    stats = [ordered_ref[d][:, width:].astype(jnp.float32) for d in range(devices)]

    def joined(stat, first):
        return sum(
            stat[:, (first + i) * HEADS : (first + i + 1) * HEADS] for i in range(PIECES)
        )

    peaks = [joined(stat, 0) for stat in stats] + [extra_stats_ref[:, :HEADS]]
    totals = [joined(stat, PIECES) for stat in stats] + [extra_stats_ref[:, HEADS : 2 * HEADS]]
    overall = functools.reduce(jnp.maximum, peaks)
    factors = [jnp.exp(peak - overall) for peak in peaks]
    total = sum(f * t for f, t in zip(factors, totals))
    inverse = 1.0 / total
    head_of_row = lax.broadcasted_iota(jnp.int32, (HEADS, width), 0)
    head_of_col = lax.broadcasted_iota(jnp.int32, (HEADS, width), 1) // HD
    expand = (head_of_row == head_of_col).astype(jnp.bfloat16)

    def spread(factor):
        return sum(dot(part, expand) for part in split(factor * inverse, 2))

    attended = spread(factors[-1]) * extra_ref[...]
    for d in range(devices):
        attended = attended + spread(factors[d]) * ordered_ref[d][:, :width].astype(jnp.float32)
    projected = dot(attended.astype(jnp.bfloat16), weight_ref[...], ROWS_BY_ROWS).astype(jnp.bfloat16)
    copy_rows(tokens_ref, rows_ref)
    share = weight_ref.shape[0]
    feature = lax.broadcasted_iota(jnp.int32, (width, share), 0)
    column = lax.broadcasted_iota(jnp.int32, (width, share), 1)
    own = (feature == column + lax.axis_index("seq") * share).astype(jnp.bfloat16)
    residual = dot(rows_ref[...].astype(jnp.bfloat16), own) + projected.astype(jnp.float32)
    residual_ref[...] = residual
    turned = turned_ref[...].astype(jnp.bfloat16)
    table = sum(dot(turned, part) for part in split(residual, PIECES))
    groups = lax.axis_size("exp")
    local_experts = EXPERTS // groups
    for s in range(devices):
        for x in range(groups):
            row = (x * local_experts + s // (devices // local_experts)) * CAP
            out_ref[s * groups + x] = table[row : row + CAP]


def home_kernel(devices, *refs):
    residual_refs, refs = refs[:devices], refs[devices:]
    gain_ref, router_ref, select_ref, chosen_ref, residual_ref, gates_ref, ordered_ref = refs
    in_order(residual_refs, ordered_ref)
    residual = jnp.concatenate([ordered_ref[d] for d in range(devices)], axis=1)
    residual_ref[...] = residual
    normed = rms_rows(residual, gain_ref[...])
    logits = dot(normed, router_ref[...], ROWS_BY_ROWS)
    gates = jnp.zeros(select_ref.shape[1:], jnp.float32)
    for c in range(TOPK):
        logit = jnp.sum(chosen_ref[c][:, :EXPERTS] * logits, axis=-1, keepdims=True)
        gates = gates + jax.nn.sigmoid(logit) * select_ref[c]
    gates_ref[...] = gates


def expert_kernel(
    received_ref, gain_ref, in_ref, down_ref, keep_ref, send_ref, in_buf, down_buf, sems
):
    hidden_units, width = down_buf.shape
    pieces = [
        slice(at, min(at + PIECE, hidden_units)) for at in range(0, hidden_units, PIECE)
    ]
    pairs = []
    for piece in pieces:
        rows = pl.ds(piece.start, piece.stop - piece.start)
        pairs += [(in_ref.at[p, 0, rows], in_buf.at[p, rows]) for p in range(2)]
    copies = started(pairs + [(down_ref.at[0], down_buf)], sems)
    devices = lax.axis_size("seq")
    groups = lax.axis_size("exp")
    columns = []
    for s in range(devices):
        columns.append(
            jnp.concatenate([received_ref[s * groups + g] for g in range(groups)], axis=0)
        )
    rows = rms_rows(jnp.concatenate(columns, axis=1), gain_ref[...])
    hidden = []
    for i, piece in enumerate(pieces):
        copies[2 * i].wait()
        gate = dot(rows, in_buf[0, piece], ROWS_BY_ROWS)
        copies[2 * i + 1].wait()
        up = dot(rows, in_buf[1, piece], ROWS_BY_ROWS)
        hidden.append((jax.nn.gelu(gate, approximate=True) * up).astype(jnp.bfloat16))
    copies[-1].wait()
    outputs = dot(jnp.concatenate(hidden, axis=1), down_buf[...])
    half = width // 2
    odd = lax.axis_index("seq") % 2 == 1
    keep_ref[...] = jnp.where(odd, outputs[:, half:], outputs[:, :half])
    send_ref[...] = jnp.where(odd, outputs[:, :half], outputs[:, half:])


def spread_kernel(kept_ref, other_ref, out_ref):
    slots = out_ref.shape[1]
    groups = kept_ref.shape[0] // slots
    outputs = kept_ref[...] + other_ref[...]
    for block in range(out_ref.shape[0]):
        first = block % groups * slots
        out_ref[block] = outputs[first : first + slots].astype(jnp.bfloat16)


def column_block(sharer, sharers):
    block = 0
    while sharers > 1:
        sharers //= 2
        block += (sharer & 1) * sharers
        sharer >>= 1
    return block


def final_kernel(gates_ref, returned_ref, residual_ref, out_ref, table_ref):
    requests, steps, width = out_ref.shape
    devices, groups, slots, part = returned_ref.shape
    local_experts = EXPERTS // groups
    sharers = devices // local_experts
    for s in range(devices):
        first = column_block(s % sharers, sharers) * part
        for x in range(groups):
            row = (x * local_experts + s // sharers) * slots
            table_ref[row : row + slots, first : first + part] = returned_ref[s, x].astype(jnp.float32)
    table = table_ref[...].astype(jnp.bfloat16)
    moe = sum(dot(part, table) for part in split(gates_ref[...], 2))
    total = residual_ref[...] + moe
    for r in range(requests):
        out_ref[r] = total[r * steps : (r + 1) * steps].astype(jnp.bfloat16)


def gather_seq(values, meanwhile=None):
    count = lax.axis_size("seq")

    def exchange(value, bits):
        return lax.ppermute(value, "seq", [(i, i ^ bits) for i in range(count)])

    near = [exchange(values, k) for k in range(2, count, 2)]
    if meanwhile is not None:
        values = meanwhile(values)
    near = [values] + near
    return [part for value in near for part in (value, exchange(value, 1))]


def shape(dims, dtype):
    return jax.ShapeDtypeStruct(dims, dtype)


def body(
    tokens,
    attn_gain,
    w_qkv,
    window_cache,
    sink_cache,
    lengths,
    w_out,
    moe_gain,
    router,
    expert_ids,
    slot_order,
    expert_in,
    expert_down,
):
    requests, steps, width = tokens.shape
    rows = requests * steps
    seq_index = lax.axis_index("seq")
    seq_count = lax.axis_size("seq")
    groups = lax.axis_size("exp")
    local_experts = EXPERTS // groups
    sharers = seq_count // local_experts
    span = window_cache.shape[2]
    share = w_qkv.shape[0]
    slots = EXPERTS * CAP
    f32, bf16 = jnp.float32, jnp.bfloat16

    vmem = pl.BlockSpec(memory_space=pltpu.VMEM)
    hbm = pl.BlockSpec(memory_space=pltpu.HBM)

    gain_row = attn_gain.reshape(1, width)
    local_mix = pl.pallas_call(
        qkv_kernel,
        in_specs=[hbm] * 3,
        out_shape=shape((rows, share), bf16),
        scratch_shapes=[
            pltpu.VMEM(tokens.shape, bf16),
            pltpu.VMEM(gain_row.shape, f32),
            pltpu.VMEM(w_qkv.shape, bf16),
            pltpu.VMEM((rows, width), f32),
            pltpu.SemaphoreType.DMA((3,)),
        ],
        compiler_params=params(4),
        name="qkv",
    )(in_hbm(tokens), in_hbm(gain_row), in_hbm(w_qkv))
    early = min(EARLY, requests - 1)

    fetched = []

    def fetch_window(values):
        held, *outputs = pl.pallas_call(
            fetch_window_kernel,
            in_specs=[vmem] + [hbm] * 4,
            out_shape=(
                shape(values.shape, bf16),
                shape((requests, span, width), bf16),
                shape((early, span, width), bf16),
                shape((requests, LANES), jnp.int32),
                shape((TOPK, rows, slots), f32),
                shape((TOPK, rows, LANES), f32),
                shape((slots, rows), f32),
            ),
            scratch_shapes=[
                pltpu.SMEM((requests,), jnp.int32),
                pltpu.VMEM((steps, TOPK, requests), jnp.int32),
                pltpu.VMEM(slot_order.shape, jnp.int32),
                pltpu.SemaphoreType.DMA((5,)),
            ],
            compiler_params=params(8),
            cost_estimate=moving(window_cache.size),
            name="fetch_window",
        )(
            values,
            in_hbm(window_cache),
            in_hbm(lengths),
            in_hbm(expert_ids.transpose(1, 2, 0)),
            in_hbm(slot_order),
        )
        fetched.extend(outputs)
        return held

    mixed = gather_seq(local_mix, fetch_window)
    keys, values, spans, select, chosen, turned = fetched

    padded = width + LANES
    part = pl.pallas_call(
        attention_kernel,
        in_specs=[vmem] * (seq_count + 3) + [hbm],
        out_shape=shape((rows, padded), bf16),
        scratch_shapes=[
            pltpu.VMEM((seq_count, rows, share), bf16),
            pltpu.VMEM((rows, padded), f32),
            pltpu.VMEM((requests, BLOCK_HEADS * steps, width), bf16),
            pltpu.VMEM((requests - early, span, width), bf16),
            pltpu.SemaphoreType.DMA((requests - early,)),
        ],
        compiler_params=params(20),
        name="attention",
    )(*mixed, spans, keys, values, in_hbm(window_cache))
    parts = gather_seq(part)

    extra, extra_stats = pl.pallas_call(
        extra_kernel,
        out_shape=(shape((rows, width), f32), shape((rows, LANES), f32)),
        scratch_shapes=[
            pltpu.VMEM((seq_count, rows, share), bf16),
            pltpu.VMEM((rows, 3 * width), f32),
            pltpu.VMEM((rows * BLOCK_HEADS, width), f32),
            pltpu.VMEM((2, requests * (SINKS + steps), width), f32),
        ],
        compiler_params=params(8),
        name="extra",
    )(*mixed, sink_cache)

    outgoing, residual_columns = pl.pallas_call(
        project_kernel,
        out_shape=(
            shape((seq_count * groups, CAP, w_out.shape[0]), f32),
            shape((rows, w_out.shape[0]), f32),
        ),
        scratch_shapes=[
            pltpu.VMEM((seq_count, rows, padded), bf16),
            pltpu.VMEM((rows, width), f32),
        ],
        compiler_params=params(8),
        name="project",
    )(*parts, extra, extra_stats, w_out, tokens, turned)
    received = lax.all_to_all(outgoing, ("seq", "exp"), split_axis=0, concat_axis=0, tiled=True)
    columns = gather_seq(residual_columns)

    moe_row = moe_gain.reshape(1, width)
    hidden_units = expert_down.shape[1]
    kept, sent = pl.pallas_call(
        expert_kernel,
        in_specs=[vmem, vmem, hbm, hbm],
        out_shape=(
            shape((groups * CAP, width // 2), f32),
            shape((groups * CAP, width // 2), f32),
        ),
        scratch_shapes=[
            pltpu.VMEM((2, hidden_units, width), bf16),
            pltpu.VMEM((hidden_units, width), bf16),
            pltpu.SemaphoreType.DMA((2 * pl.cdiv(hidden_units, PIECE) + 1,)),
        ],
        compiler_params=params(20),
        name="expert",
    )(received, moe_row, in_hbm(expert_in), in_hbm(expert_down))

    reach = 1
    while True:
        other = lax.ppermute(sent, "seq", [(i, i ^ reach) for i in range(seq_count)])
        reach *= 2
        if reach >= sharers:
            break
        upper = (seq_index // reach) % 2 == 1
        low, high = jnp.split(kept + other, 2, axis=1)
        kept, sent = jnp.where(upper, high, low), jnp.where(upper, low, high)
    part_width = kept.shape[1]
    outgoing = pl.pallas_call(
        spread_kernel,
        out_shape=shape((seq_count * groups, CAP, part_width), bf16),
        compiler_params=params(8),
        name="spread",
    )(kept, other)
    returned = lax.all_to_all(
        outgoing,
        ("seq", "exp"),
        split_axis=0,
        concat_axis=0,
        tiled=True,
    ).reshape(seq_count, groups, CAP, part_width)

    columns, _ = lax.optimization_barrier((columns, outgoing))
    residual, gates = pl.pallas_call(
        functools.partial(home_kernel, seq_count),
        out_shape=(shape((rows, width), f32), shape((rows, slots), f32)),
        scratch_shapes=[pltpu.VMEM((seq_count, rows, w_out.shape[0]), f32)],
        compiler_params=params(8),
        name="home",
    )(*columns, moe_row, router.T, select, chosen)

    return pl.pallas_call(
        final_kernel,
        out_shape=shape((requests, steps, width), bf16),
        scratch_shapes=[pltpu.VMEM((slots, width), f32)],
        compiler_params=params(8),
        name="final",
    )(gates, returned, residual)


def solution(mesh):
    in_specs = (
        P("exp", None, None),
        P(),
        P("seq", None),
        P(None, "exp", "seq", None),
        P(None, "exp", None, None),
        P("exp"),
        P("seq", None),
        P(),
        P(),
        P("exp", None, None),
        P("exp", None),
        P(None, "exp", "seq", None),
        P("exp", "seq", None),
    )
    out_specs = P("exp", None, None)
    return jax.shard_map(body, mesh=mesh, in_specs=in_specs, out_specs=out_specs, check_vma=False)
```

```python
import functools

import jax
import jax.numpy as jnp
from jax import lax
from jax.experimental import pallas as pl
from jax.experimental.pallas import tpu as pltpu
from jax.sharding import PartitionSpec as P

HEADS = 16
HD = 64
EXPERTS = 16
TOPK = 2
SINKS = 4
WIN = 4096
CAP = 8
LANES = 128
PIECES = 3
FIRST_KEYS = 2
SECOND_KEYS = 8
SECOND_VALUES = 3
PIECE = 512
BLOCK = 256
BLOCK_HEADS = BLOCK // HD

EPSILON = 1e-06
MASKED = -1e30
MIB = 1 << 20
ROWS_BY_ROWS = (((1,), (1,)), ((), ()))
ROWS_BY_COLS = (((1,), (0,)), ((), ()))


def dot(a, b, dims=ROWS_BY_COLS):
    return lax.dot_general(a, b, dims, preferred_element_type=jnp.float32)


def params(limit_mib=32):
    return pltpu.CompilerParams(vmem_limit_bytes=limit_mib * MIB)


def moving(count):
    return pl.CostEstimate(flops=0, bytes_accessed=count, transcendentals=0)


def in_hbm(value):
    return pltpu.with_memory_space_constraint(value, pltpu.HBM)


def split(value, count):
    parts = []
    for _ in range(count):
        part = value.astype(jnp.bfloat16)
        parts.append(part)
        value = value - part.astype(jnp.float32)
    return parts


def rms_rows(widened, gain_row):
    inverse = lax.rsqrt(jnp.mean(widened * widened, axis=-1, keepdims=True) + EPSILON)
    return (widened * inverse * gain_row).astype(jnp.bfloat16)


def copy_rows(source_ref, rows_ref):
    requests, steps, _ = source_ref.shape
    for r in range(requests):
        rows_ref[r * steps : (r + 1) * steps, :] = source_ref[r].astype(rows_ref.dtype)


def started(pairs, sems):
    copies = [pltpu.make_async_copy(*pair, sems.at[i]) for i, pair in enumerate(pairs)]
    for copy in copies:
        copy.start()
    return copies


def route(ids_ref, order_ref, select_ref, chosen_ref):
    steps, _, requests = ids_ref.shape
    rows = requests * steps
    lane = lax.broadcasted_iota(jnp.int32, (rows, LANES), 1)
    own_row = lax.broadcasted_iota(jnp.int32, (rows, requests), 0)
    own_request = lax.broadcasted_iota(jnp.int32, (rows, requests), 1) == own_row // steps
    chosen = []
    for c in range(TOPK):
        ids = jnp.zeros((rows, requests), jnp.int32)
        for t in range(steps):
            ids = jnp.where(own_request & (own_row % steps == t), ids_ref[t, c : c + 1, :], ids)
        chosen.append(jnp.sum(ids.astype(jnp.float32), axis=1, keepdims=True).astype(jnp.int32))
    onehot = [(lane == ids).astype(jnp.float32) for ids in chosen]
    square_row = lax.broadcasted_iota(jnp.int32, (rows, rows), 0)
    square_col = lax.broadcasted_iota(jnp.int32, (rows, rows), 1)
    order_wide = jnp.broadcast_to(order_ref[...], (rows, rows))
    down = jnp.sum(
        jnp.where(square_row == square_col, order_wide, 0).astype(jnp.float32),
        axis=1,
        keepdims=True,
    )
    earlier = (order_wide.astype(jnp.float32) < down).astype(jnp.bfloat16)
    counts = dot(earlier, sum(onehot).astype(jnp.bfloat16))
    slot = lax.broadcasted_iota(jnp.int32, (rows, EXPERTS * CAP), 1)
    both = jnp.zeros((rows, EXPERTS * CAP), jnp.float32)
    for c in range(TOPK):
        position = jnp.sum(onehot[c] * counts, axis=-1, keepdims=True).astype(jnp.int32)
        column = chosen[c] * CAP + position
        select = ((column == slot) & (position < CAP)).astype(jnp.float32)
        select_ref[c] = select
        chosen_ref[c] = onehot[c]
        both = both + select
    return jnp.transpose(both)


def qkv_kernel(
    tokens_ref,
    gain_ref,
    weight_ref,
    window_ref,
    out_ref,
    keys_ref,
    token_buf,
    gain_buf,
    weight_buf,
    rows_ref,
    sems,
):
    copies = started(
        (
            (tokens_ref, token_buf),
            (gain_ref, gain_buf),
            (weight_ref, weight_buf),
            (window_ref.at[0, pl.ds(0, keys_ref.shape[0])], keys_ref),
        ),
        sems,
    )
    for copy in copies[:3]:
        copy.wait()
    copy_rows(token_buf, rows_ref)
    normed = rms_rows(rows_ref[...], gain_buf[...])
    out_ref[...] = dot(normed, weight_buf[...], ROWS_BY_ROWS).astype(jnp.bfloat16)
    copies[3].wait()


def in_order(sent_refs, ordered_ref):
    place = lax.axis_index("seq")
    for k, sent_ref in enumerate(sent_refs):
        ordered_ref[jnp.bitwise_xor(place, k)] = sent_ref[...]


def head_masks(rows, width, steps):
    row_head = lax.broadcasted_iota(jnp.int32, (rows, width), 0) // steps % BLOCK_HEADS
    col_head = lax.broadcasted_iota(jnp.int32, (rows, width), 1) // HD % BLOCK_HEADS
    return (row_head == col_head).astype(jnp.float32)


def fetch_window_kernel(
    first,
    sent_ref,
    window_ref,
    lengths_ref,
    ids_ref,
    order_ref,
    held_ref,
    keys_ref,
    values_ref,
    spans_ref,
    select_ref,
    chosen_ref,
    turned_ref,
    numbers_ref,
    ids_buf,
    order_buf,
    sems,
):
    copies = started(
        (
            (ids_ref, ids_buf),
            (order_ref, order_buf),
            (lengths_ref, numbers_ref),
            (window_ref.at[0, pl.ds(first, keys_ref.shape[0])], keys_ref),
            (window_ref.at[1, pl.ds(0, values_ref.shape[0])], values_ref),
        ),
        sems,
    )
    held_ref[...] = sent_ref[...]
    for copy in copies[:3]:
        copy.wait()
    turned_ref[...] = route(ids_buf, order_buf, select_ref, chosen_ref)
    for r in range(spans_ref.shape[0]):
        spans_ref[r : r + 1, :] = jnp.full((1, LANES), numbers_ref[r], jnp.int32)
    for copy in copies[3:]:
        copy.wait()


def fetch_expert_kernel(sent_ref, in_ref, held_ref, piece_ref, sems):
    copies = started([(in_ref.at[p, 0, pl.ds(0, piece_ref.shape[1])], piece_ref.at[p]) for p in range(2)], sems)
    held_ref[...] = sent_ref[...]
    for copy in copies:
        copy.wait()


def attention_kernel(*refs):
    *mixed_refs, spans_ref, first_ref, keys_ref, values_ref, window_ref = refs[:-6]
    out_ref, ordered_ref, flat_ref, query_ref, late_ref, sems = refs[-6:]
    devices, rows, share = ordered_ref.shape
    _, requests, span, width = window_ref.shape
    held = {(0, r): first_ref.at[r] for r in range(first_ref.shape[0])}
    held |= {(0, r + first_ref.shape[0]): keys_ref.at[r] for r in range(keys_ref.shape[0])}
    held |= {(1, r): values_ref.at[r] for r in range(values_ref.shape[0])}
    needed = [(p, r) for i in range(requests + 1) for p, r in ((0, i), (1, i - 1))]
    needed = [at for at in needed if 0 <= at[1] < requests and at not in held]
    late = {at: late_ref.at[i] for i, at in enumerate(needed)}
    copies = started([(window_ref.at[p, r], late[p, r]) for p, r in needed], sems)
    waits = dict(zip(needed, copies))

    def window(p, r):
        if (p, r) in held:
            return held[p, r]
        waits[p, r].wait()
        return late[p, r]

    steps = rows // requests
    block_rows = BLOCK_HEADS * steps
    place = lax.axis_index("seq")
    in_order(mixed_refs, ordered_ref)
    for d in range(devices):
        if d * share < width:
            flat_ref[:, d * share : (d + 1) * share] = ordered_ref[d].astype(jnp.float32)
    own_head = head_masks(block_rows, width, steps)
    for r in range(requests):
        queries = flat_ref[r * steps : (r + 1) * steps, 0:width]
        query_ref[r] = (jnp.concatenate([queries] * BLOCK_HEADS, axis=0) * own_head).astype(
            jnp.bfloat16
        )
    base = place * span
    scale = HD ** (-0.5)
    pair = 2 * steps
    tiles = HEADS * steps // pair
    slot = base + lax.broadcasted_iota(jnp.int32, (pair, span), 1)
    step = lax.broadcasted_iota(jnp.int32, (pair, span), 0) % steps
    stat_lane = lax.broadcasted_iota(jnp.int32, (HEADS * steps, LANES), 1)
    stat_head = lax.broadcasted_iota(jnp.int32, (HEADS * steps, LANES), 0) // steps
    cols = [slice(c, c + BLOCK) for c in range(0, width, BLOCK)]

    def score(r):
        keys = window(0, r)
        return jnp.concatenate(
            [dot(query_ref[r, :, c], keys[:, c], ROWS_BY_ROWS) for c in cols], axis=0
        )

    scores = score(0)
    for r in range(requests):
        following = score(r + 1) if r + 1 < requests else None
        length = spans_ref[r : r + 1, 0:1]
        age = jnp.bitwise_and(slot - (length - SINKS), WIN - 1)
        live = ((slot < jnp.minimum(WIN, length - SINKS)) & (age > step))[None]
        scores = jnp.where(live, scores.reshape(tiles, pair, span) * scale, MASKED)
        peak = jnp.max(scores, axis=-1, keepdims=True)
        weight = jnp.where(live, jnp.exp(scores - peak), 0.0)
        total = jnp.sum(weight, axis=-1, keepdims=True)
        weight = weight.reshape(HEADS * steps, span).astype(jnp.bfloat16)
        values = window(1, r)
        outs = []
        for b, c in enumerate(cols):
            own = slice(b * block_rows, (b + 1) * block_rows)
            mixed = dot(weight[own], values[:, c]) * own_head[:, c]
            mixed = sum(mixed[i : i + pair] for i in range(0, block_rows, pair))
            outs.append(mixed[:steps] + mixed[steps:])
        stats = jnp.zeros((HEADS * steps, LANES), jnp.float32)
        parts = split(peak.reshape(HEADS * steps, 1), PIECES)
        parts = parts + split(total.reshape(HEADS * steps, 1), PIECES)
        for i, part in enumerate(parts):
            stats = jnp.where(
                stat_lane == stat_head + i * HEADS, part.astype(jnp.float32), stats
            )
        stats = jnp.sum(stats.reshape(tiles, pair, LANES), axis=0)
        outs.append(stats[:steps] + stats[steps:])
        flat_ref[r * steps : (r + 1) * steps, :] = jnp.concatenate(outs, axis=1)
        scores = following
    out_ref[...] = flat_ref[...].astype(jnp.bfloat16)


def extra_kernel(*refs):
    *mixed_refs, sinks_ref = refs[:-6]
    out_ref, stats_ref, ordered_ref, flat_ref, query_ref, keys_ref = refs[-6:]
    devices, rows, share = ordered_ref.shape
    _, requests, sinks, width = sinks_ref.shape
    steps = rows // requests
    block_rows = BLOCK_HEADS * steps
    count = sinks + steps
    in_order(mixed_refs, ordered_ref)
    for d in range(devices):
        flat_ref[:, d * share : (d + 1) * share] = ordered_ref[d].astype(jnp.float32)
    own_head = head_masks(block_rows, width, steps)
    for r in range(requests):
        own = slice(r * steps, (r + 1) * steps)
        queries = jnp.concatenate([flat_ref[own, 0:width]] * BLOCK_HEADS, axis=0) * own_head
        query_ref[r * block_rows : (r + 1) * block_rows, :] = queries
        for p in range(2):
            keys_ref[p, r * count : r * count + sinks] = sinks_ref[p, r].astype(jnp.float32)
            keys_ref[p, r * count + sinks : (r + 1) * count] = flat_ref[
                own, (p + 1) * width : (p + 2) * width
            ]
    all_rows = requests * block_rows
    all_keys = requests * count
    row = lax.broadcasted_iota(jnp.int32, (all_rows, all_keys), 0)
    key = lax.broadcasted_iota(jnp.int32, (all_rows, all_keys), 1)
    live = (row // block_rows == key // count) & (key % count - sinks <= row % steps)
    stat_lane = lax.broadcasted_iota(jnp.int32, (all_rows, LANES), 1)
    stat_head = lax.broadcasted_iota(jnp.int32, (all_rows, LANES), 0) % block_rows // steps
    whole_mask = jnp.concatenate([own_head[:, :BLOCK]] * requests, axis=0)
    stats = jnp.zeros((all_rows, LANES), jnp.float32)
    pair = 2 * steps

    def by_request(values):
        values = jnp.sum(values.reshape(requests, block_rows // pair, pair, values.shape[-1]), axis=1)
        return values[:, :steps] + values[:, steps:]

    for b in range(width // BLOCK):
        c = slice(b * BLOCK, (b + 1) * BLOCK)
        scores = dot(
            query_ref[:, c].astype(jnp.bfloat16), keys_ref[0, :, c].astype(jnp.bfloat16), ROWS_BY_ROWS
        )
        scores = jnp.where(live, scores * HD ** (-0.5), MASKED)
        peak = jnp.max(scores, axis=-1, keepdims=True)
        weight = jnp.where(live, jnp.exp(scores - peak), 0.0)
        total = jnp.sum(weight, axis=-1, keepdims=True)
        mixed = dot(weight.astype(jnp.bfloat16), keys_ref[1, :, c].astype(jnp.bfloat16))
        mixed = by_request(mixed * whole_mask)
        for r in range(requests):
            out_ref[r * steps : (r + 1) * steps, c] = mixed[r]
        stats = jnp.where(stat_lane == stat_head + b * BLOCK_HEADS, peak, stats)
        stats = jnp.where(stat_lane == stat_head + b * BLOCK_HEADS + HEADS, total, stats)
    stats = by_request(stats)
    for r in range(requests):
        stats_ref[r * steps : (r + 1) * steps, :] = stats[r]


def project_kernel(*refs):
    *part_refs, extra_ref, extra_stats_ref, weight_ref, tokens_ref, turned_ref = refs[:-4]
    out_ref, residual_ref, ordered_ref, rows_ref = refs[-4:]
    devices, rows, padded = ordered_ref.shape
    width = padded - LANES
    in_order(part_refs, ordered_ref)
    stats = [ordered_ref[d][:, width:].astype(jnp.float32) for d in range(devices)]

    def joined(stat, first):
        return sum(
            stat[:, (first + i) * HEADS : (first + i + 1) * HEADS] for i in range(PIECES)
        )

    peaks = [joined(stat, 0) for stat in stats] + [extra_stats_ref[:, :HEADS]]
    totals = [joined(stat, PIECES) for stat in stats] + [extra_stats_ref[:, HEADS : 2 * HEADS]]
    overall = functools.reduce(jnp.maximum, peaks)
    factors = [jnp.exp(peak - overall) for peak in peaks]
    total = sum(f * t for f, t in zip(factors, totals))
    inverse = 1.0 / total
    head_of_row = lax.broadcasted_iota(jnp.int32, (HEADS, width), 0)
    head_of_col = lax.broadcasted_iota(jnp.int32, (HEADS, width), 1) // HD
    expand = (head_of_row == head_of_col).astype(jnp.bfloat16)

    spread = jnp.concatenate([factor * inverse for factor in factors], axis=0)
    spread = sum(dot(part, expand) for part in split(spread, 2))
    attended = spread[devices * rows :] * extra_ref[...]
    for d in range(devices):
        share = spread[d * rows : (d + 1) * rows]
        attended = attended + share * ordered_ref[d][:, :width].astype(jnp.float32)
    projected = dot(attended.astype(jnp.bfloat16), weight_ref[...], ROWS_BY_ROWS).astype(jnp.bfloat16)
    copy_rows(tokens_ref, rows_ref)
    share = weight_ref.shape[0]
    feature = lax.broadcasted_iota(jnp.int32, (width, share), 0)
    column = lax.broadcasted_iota(jnp.int32, (width, share), 1)
    own = (feature == column + lax.axis_index("seq") * share).astype(jnp.bfloat16)
    residual = dot(rows_ref[...].astype(jnp.bfloat16), own) + projected.astype(jnp.float32)
    residual_ref[...] = residual
    turned = turned_ref[...].astype(jnp.bfloat16)
    table = sum(dot(turned, part) for part in split(residual, PIECES))
    groups = lax.axis_size("exp")
    local_experts = EXPERTS // groups
    for s in range(devices):
        for x in range(groups):
            row = (x * local_experts + s // (devices // local_experts)) * CAP
            out_ref[s * groups + x] = table[row : row + CAP]


def home_kernel(devices, *refs):
    residual_refs, refs = refs[:devices], refs[devices:]
    gain_ref, router_ref, select_ref, chosen_ref, residual_ref, gates_ref, ordered_ref = refs
    in_order(residual_refs, ordered_ref)
    residual = jnp.concatenate([ordered_ref[d] for d in range(devices)], axis=1)
    residual_ref[...] = residual
    normed = rms_rows(residual, gain_ref[...])
    logits = dot(normed, router_ref[...], ROWS_BY_ROWS)
    gates = jnp.zeros(select_ref.shape[1:], jnp.float32)
    for c in range(TOPK):
        logit = jnp.sum(chosen_ref[c][:, :EXPERTS] * logits, axis=-1, keepdims=True)
        gates = gates + jax.nn.sigmoid(logit) * select_ref[c]
    gates_ref[...] = gates


def expert_kernel(
    received_ref, gain_ref, piece_ref, in_ref, down_ref, keep_ref, send_ref, in_buf, down_buf, sems
):
    hidden_units, width = down_buf.shape
    held = piece_ref.shape[1]
    pieces = [(at, min(PIECE, hidden_units - at)) for at in range(held, hidden_units, PIECE)]
    pairs = []
    for at, count in pieces:
        for p in range(2):
            pairs.append(
                (in_ref.at[p, 0, pl.ds(at, count)], in_buf.at[p, pl.ds(at - held, count)])
            )
    copies = started(pairs + [(down_ref.at[0], down_buf)], sems)
    devices = lax.axis_size("seq")
    groups = lax.axis_size("exp")
    columns = []
    for s in range(devices):
        columns.append(
            jnp.concatenate([received_ref[s * groups + g] for g in range(groups)], axis=0)
        )
    rows = rms_rows(jnp.concatenate(columns, axis=1), gain_ref[...])

    def layer(gate_weight, up_weight):
        gate = dot(rows, gate_weight, ROWS_BY_ROWS)
        up = dot(rows, up_weight, ROWS_BY_ROWS)
        return (jax.nn.gelu(gate, approximate=True) * up).astype(jnp.bfloat16)

    hidden = [layer(piece_ref[0], piece_ref[1])]
    for i, (at, count) in enumerate(pieces):
        copies[2 * i].wait()
        copies[2 * i + 1].wait()
        own = slice(at - held, at - held + count)
        hidden.append(layer(in_buf[0, own], in_buf[1, own]))
    copies[-1].wait()
    outputs = dot(jnp.concatenate(hidden, axis=1), down_buf[...])
    half = width // 2
    odd = lax.axis_index("seq") % 2 == 1
    keep_ref[...] = jnp.where(odd, outputs[:, half:], outputs[:, :half])
    send_ref[...] = jnp.where(odd, outputs[:, :half], outputs[:, half:])


def spread_kernel(kept_ref, other_ref, out_ref):
    slots = out_ref.shape[1]
    groups = kept_ref.shape[0] // slots
    outputs = kept_ref[...] + other_ref[...]
    for block in range(out_ref.shape[0]):
        first = block % groups * slots
        out_ref[block] = outputs[first : first + slots].astype(jnp.bfloat16)


def column_block(sharer, sharers):
    block = 0
    while sharers > 1:
        sharers //= 2
        block += (sharer & 1) * sharers
        sharer >>= 1
    return block


def final_kernel(gates_ref, returned_ref, residual_ref, out_ref, table_ref):
    requests, steps, width = out_ref.shape
    devices, groups, slots, part = returned_ref.shape
    local_experts = EXPERTS // groups
    sharers = devices // local_experts
    for s in range(devices):
        first = column_block(s % sharers, sharers) * part
        for x in range(groups):
            row = (x * local_experts + s // sharers) * slots
            table_ref[row : row + slots, first : first + part] = returned_ref[s, x].astype(jnp.float32)
    table = table_ref[...].astype(jnp.bfloat16)
    moe = sum(dot(part, table) for part in split(gates_ref[...], 2))
    total = residual_ref[...] + moe
    for r in range(requests):
        out_ref[r] = total[r * steps : (r + 1) * steps].astype(jnp.bfloat16)


def gather_seq(values, meanwhile=None):
    count = lax.axis_size("seq")

    def exchange(value, bits):
        return lax.ppermute(value, "seq", [(i, i ^ bits) for i in range(count)])

    near = [exchange(values, k) for k in range(2, count, 2)]
    if meanwhile is not None:
        values = meanwhile(values)
    near = [values] + near
    return [part for value in near for part in (value, exchange(value, 1))]


def shape(dims, dtype):
    return jax.ShapeDtypeStruct(dims, dtype)


def body(
    tokens,
    attn_gain,
    w_qkv,
    window_cache,
    sink_cache,
    lengths,
    w_out,
    moe_gain,
    router,
    expert_ids,
    slot_order,
    expert_in,
    expert_down,
):
    requests, steps, width = tokens.shape
    rows = requests * steps
    seq_index = lax.axis_index("seq")
    seq_count = lax.axis_size("seq")
    groups = lax.axis_size("exp")
    local_experts = EXPERTS // groups
    sharers = seq_count // local_experts
    span = window_cache.shape[2]
    share = w_qkv.shape[0]
    slots = EXPERTS * CAP
    f32, bf16 = jnp.float32, jnp.bfloat16

    vmem = pl.BlockSpec(memory_space=pltpu.VMEM)
    hbm = pl.BlockSpec(memory_space=pltpu.HBM)

    gain_row = attn_gain.reshape(1, width)
    first_keys = min(FIRST_KEYS, requests)
    second_keys = min(SECOND_KEYS, requests - first_keys)
    second_values = min(SECOND_VALUES, requests)
    late = 2 * requests - first_keys - second_keys - second_values
    local_mix, first = pl.pallas_call(
        qkv_kernel,
        in_specs=[hbm] * 4,
        out_shape=(shape((rows, share), bf16), shape((first_keys, span, width), bf16)),
        scratch_shapes=[
            pltpu.VMEM(tokens.shape, bf16),
            pltpu.VMEM(gain_row.shape, f32),
            pltpu.VMEM(w_qkv.shape, bf16),
            pltpu.VMEM((rows, width), f32),
            pltpu.SemaphoreType.DMA((4,)),
        ],
        compiler_params=params(4),
        name="qkv",
    )(in_hbm(tokens), in_hbm(gain_row), in_hbm(w_qkv), in_hbm(window_cache))

    fetched = []

    def fetch_window(values):
        held, *outputs = pl.pallas_call(
            functools.partial(fetch_window_kernel, first_keys),
            in_specs=[vmem] + [hbm] * 4,
            out_shape=(
                shape(values.shape, bf16),
                shape((second_keys, span, width), bf16),
                shape((second_values, span, width), bf16),
                shape((requests, LANES), jnp.int32),
                shape((TOPK, rows, slots), f32),
                shape((TOPK, rows, LANES), f32),
                shape((slots, rows), f32),
            ),
            scratch_shapes=[
                pltpu.SMEM((requests,), jnp.int32),
                pltpu.VMEM((steps, TOPK, requests), jnp.int32),
                pltpu.VMEM(slot_order.shape, jnp.int32),
                pltpu.SemaphoreType.DMA((5,)),
            ],
            compiler_params=params(8),
            cost_estimate=moving(window_cache.size),
            name="fetch_window",
        )(
            values,
            in_hbm(window_cache),
            in_hbm(lengths),
            in_hbm(expert_ids.transpose(1, 2, 0)),
            in_hbm(slot_order),
        )
        fetched.extend(outputs)
        return held

    mixed = gather_seq(local_mix, fetch_window)
    keys, values, spans, select, chosen, turned = fetched

    padded = width + LANES
    part = pl.pallas_call(
        attention_kernel,
        in_specs=[vmem] * (seq_count + 4) + [hbm],
        out_shape=shape((rows, padded), bf16),
        scratch_shapes=[
            pltpu.VMEM((seq_count, rows, share), bf16),
            pltpu.VMEM((rows, padded), f32),
            pltpu.VMEM((requests, BLOCK_HEADS * steps, width), bf16),
            pltpu.VMEM((late, span, width), bf16),
            pltpu.SemaphoreType.DMA((late,)),
        ],
        compiler_params=params(24),
        name="attention",
    )(*mixed, spans, first, keys, values, in_hbm(window_cache))
    hidden_units = expert_down.shape[1]
    held_units = min(PIECE, hidden_units)
    late_units = max(hidden_units - held_units, 16)

    def fetch_expert(values):
        held, piece = pl.pallas_call(
            fetch_expert_kernel,
            in_specs=[vmem, hbm],
            out_shape=(shape(values.shape, bf16), shape((2, held_units, width), bf16)),
            scratch_shapes=[pltpu.SemaphoreType.DMA((2,))],
            compiler_params=params(8),
            cost_estimate=moving(4 * held_units * width),
            name="fetch_expert",
        )(values, in_hbm(expert_in))
        fetched.append(piece)
        return held

    parts = gather_seq(part, fetch_expert)
    piece = fetched[-1]

    extra, extra_stats = pl.pallas_call(
        extra_kernel,
        out_shape=(shape((rows, width), f32), shape((rows, LANES), f32)),
        scratch_shapes=[
            pltpu.VMEM((seq_count, rows, share), bf16),
            pltpu.VMEM((rows, 3 * width), f32),
            pltpu.VMEM((rows * BLOCK_HEADS, width), f32),
            pltpu.VMEM((2, requests * (SINKS + steps), width), f32),
        ],
        compiler_params=params(8),
        name="extra",
    )(*mixed, sink_cache)

    outgoing, residual_columns = pl.pallas_call(
        project_kernel,
        out_shape=(
            shape((seq_count * groups, CAP, w_out.shape[0]), f32),
            shape((rows, w_out.shape[0]), f32),
        ),
        scratch_shapes=[
            pltpu.VMEM((seq_count, rows, padded), bf16),
            pltpu.VMEM((rows, width), f32),
        ],
        compiler_params=params(16),
        name="project",
    )(*parts, extra, extra_stats, w_out, tokens, turned)
    received = lax.all_to_all(outgoing, ("seq", "exp"), split_axis=0, concat_axis=0, tiled=True)
    columns = gather_seq(residual_columns)

    moe_row = moe_gain.reshape(1, width)
    kept, sent = pl.pallas_call(
        expert_kernel,
        in_specs=[vmem, vmem, vmem, hbm, hbm],
        out_shape=(
            shape((groups * CAP, width // 2), f32),
            shape((groups * CAP, width // 2), f32),
        ),
        scratch_shapes=[
            pltpu.VMEM((2, late_units, width), bf16),
            pltpu.VMEM((hidden_units, width), bf16),
            pltpu.SemaphoreType.DMA((2 * pl.cdiv(hidden_units, PIECE) + 1,)),
        ],
        compiler_params=params(20),
        name="expert",
    )(received, moe_row, piece, in_hbm(expert_in), in_hbm(expert_down))

    reach = 1
    while True:
        other = lax.ppermute(sent, "seq", [(i, i ^ reach) for i in range(seq_count)])
        reach *= 2
        if reach >= sharers:
            break
        upper = (seq_index // reach) % 2 == 1
        low, high = jnp.split(kept + other, 2, axis=1)
        kept, sent = jnp.where(upper, high, low), jnp.where(upper, low, high)
    part_width = kept.shape[1]
    outgoing = pl.pallas_call(
        spread_kernel,
        out_shape=shape((seq_count * groups, CAP, part_width), bf16),
        compiler_params=params(8),
        name="spread",
    )(kept, other)
    returned = lax.all_to_all(
        outgoing,
        ("seq", "exp"),
        split_axis=0,
        concat_axis=0,
        tiled=True,
    ).reshape(seq_count, groups, CAP, part_width)

    columns, _ = lax.optimization_barrier((columns, outgoing))
    residual, gates = pl.pallas_call(
        functools.partial(home_kernel, seq_count),
        out_shape=(shape((rows, width), f32), shape((rows, slots), f32)),
        scratch_shapes=[pltpu.VMEM((seq_count, rows, w_out.shape[0]), f32)],
        compiler_params=params(8),
        name="home",
    )(*columns, moe_row, router.T, select, chosen)

    return pl.pallas_call(
        final_kernel,
        out_shape=shape((requests, steps, width), bf16),
        scratch_shapes=[pltpu.VMEM((slots, width), f32)],
        compiler_params=params(8),
        name="final",
    )(gates, returned, residual)


def solution(mesh):
    in_specs = (
        P("exp", None, None),
        P(),
        P("seq", None),
        P(None, "exp", "seq", None),
        P(None, "exp", None, None),
        P("exp"),
        P("seq", None),
        P(),
        P(),
        P("exp", None, None),
        P("exp", None),
        P(None, "exp", "seq", None),
        P("exp", "seq", None),
    )
    out_specs = P("exp", None, None)
    return jax.shard_map(body, mesh=mesh, in_specs=in_specs, out_specs=out_specs, check_vma=False)
```

```python
import functools

import jax
import jax.numpy as jnp
from jax import lax
from jax.experimental import pallas as pl
from jax.experimental.pallas import tpu as pltpu
from jax.sharding import PartitionSpec as P

HEADS = 16
HD = 64
EXPERTS = 16
TOPK = 2
SINKS = 4
WIN = 4096
CAP = 8
LANES = 128
PIECES = 3
FIRST_KEYS = 2
SECOND_KEYS = 8
SECOND_VALUES = 3
PIECE = 512
BLOCK = 256
BLOCK_HEADS = BLOCK // HD

EPSILON = 1e-06
MASKED = -1e30
MIB = 1 << 20
ROWS_BY_ROWS = (((1,), (1,)), ((), ()))
ROWS_BY_COLS = (((1,), (0,)), ((), ()))


def dot(a, b, dims=ROWS_BY_COLS):
    return lax.dot_general(a, b, dims, preferred_element_type=jnp.float32)


def params(limit_mib=32):
    return pltpu.CompilerParams(vmem_limit_bytes=limit_mib * MIB)


def moving(count):
    return pl.CostEstimate(flops=0, bytes_accessed=count, transcendentals=0)


def in_hbm(value):
    return pltpu.with_memory_space_constraint(value, pltpu.HBM)


def split(value, count):
    parts = []
    for _ in range(count):
        part = value.astype(jnp.bfloat16)
        parts.append(part)
        value = value - part.astype(jnp.float32)
    return parts


def rms_rows(widened, gain_row):
    inverse = lax.rsqrt(jnp.mean(widened * widened, axis=-1, keepdims=True) + EPSILON)
    return (widened * inverse * gain_row).astype(jnp.bfloat16)


def copy_rows(source_ref, rows_ref):
    requests, steps, _ = source_ref.shape
    for r in range(requests):
        rows_ref[r * steps : (r + 1) * steps, :] = source_ref[r].astype(rows_ref.dtype)


def started(pairs, sems):
    copies = [pltpu.make_async_copy(*pair, sems.at[i]) for i, pair in enumerate(pairs)]
    for copy in copies:
        copy.start()
    return copies


def route(ids_ref, order_ref, select_ref, chosen_ref):
    steps, _, requests = ids_ref.shape
    rows = requests * steps
    lane = lax.broadcasted_iota(jnp.int32, (rows, LANES), 1)
    own_row = lax.broadcasted_iota(jnp.int32, (rows, requests), 0)
    own_request = lax.broadcasted_iota(jnp.int32, (rows, requests), 1) == own_row // steps
    chosen = []
    for c in range(TOPK):
        ids = jnp.zeros((rows, requests), jnp.int32)
        for t in range(steps):
            ids = jnp.where(own_request & (own_row % steps == t), ids_ref[t, c : c + 1, :], ids)
        chosen.append(jnp.sum(ids.astype(jnp.float32), axis=1, keepdims=True).astype(jnp.int32))
    onehot = [(lane == ids).astype(jnp.float32) for ids in chosen]
    square_row = lax.broadcasted_iota(jnp.int32, (rows, rows), 0)
    square_col = lax.broadcasted_iota(jnp.int32, (rows, rows), 1)
    order_wide = jnp.broadcast_to(order_ref[...], (rows, rows))
    down = jnp.sum(
        jnp.where(square_row == square_col, order_wide, 0).astype(jnp.float32),
        axis=1,
        keepdims=True,
    )
    earlier = (order_wide.astype(jnp.float32) < down).astype(jnp.bfloat16)
    counts = dot(earlier, sum(onehot).astype(jnp.bfloat16))
    slot = lax.broadcasted_iota(jnp.int32, (rows, EXPERTS * CAP), 1)
    both = jnp.zeros((rows, EXPERTS * CAP), jnp.float32)
    for c in range(TOPK):
        position = jnp.sum(onehot[c] * counts, axis=-1, keepdims=True).astype(jnp.int32)
        column = chosen[c] * CAP + position
        select = ((column == slot) & (position < CAP)).astype(jnp.float32)
        select_ref[c] = select
        chosen_ref[c] = onehot[c]
        both = both + select
    return jnp.transpose(both)


def qkv_kernel(
    tokens_ref,
    gain_ref,
    weight_ref,
    window_ref,
    out_ref,
    token_buf,
    gain_buf,
    weight_buf,
    rows_ref,
    sems,
):
    copies = started(
        (
            (tokens_ref, token_buf),
            (gain_ref, gain_buf),
            (weight_ref, weight_buf),
        ),
        sems,
    )
    for copy in copies:
        copy.wait()
    copy_rows(token_buf, rows_ref)
    normed = rms_rows(rows_ref[...], gain_buf[...])
    out_ref[...] = dot(normed, weight_buf[...], ROWS_BY_ROWS).astype(jnp.bfloat16)


def in_order(sent_refs, ordered_ref):
    place = lax.axis_index("seq")
    for k, sent_ref in enumerate(sent_refs):
        ordered_ref[jnp.bitwise_xor(place, k)] = sent_ref[...]


def head_masks(rows, width, steps):
    row_head = lax.broadcasted_iota(jnp.int32, (rows, width), 0) // steps % BLOCK_HEADS
    col_head = lax.broadcasted_iota(jnp.int32, (rows, width), 1) // HD % BLOCK_HEADS
    return (row_head == col_head).astype(jnp.float32)


def routing_kernel(
    sent_ref,
    lengths_ref,
    ids_ref,
    order_ref,
    held_ref,
    spans_ref,
    select_ref,
    chosen_ref,
    turned_ref,
    numbers_ref,
    ids_buf,
    order_buf,
    sems,
):
    copies = started(
        (
            (ids_ref, ids_buf),
            (order_ref, order_buf),
            (lengths_ref, numbers_ref),
        ),
        sems,
    )
    held_ref[...] = sent_ref[...]
    for copy in copies:
        copy.wait()
    turned_ref[...] = route(ids_buf, order_buf, select_ref, chosen_ref)
    for r in range(spans_ref.shape[0]):
        spans_ref[r : r + 1, :] = jnp.full((1, LANES), numbers_ref[r], jnp.int32)


def fetch_expert_kernel(sent_ref, in_ref, held_ref, piece_ref, sems):
    copies = started([(in_ref.at[p, 0, pl.ds(0, piece_ref.shape[1])], piece_ref.at[p]) for p in range(2)], sems)
    held_ref[...] = sent_ref[...]
    for copy in copies:
        copy.wait()


def attention_kernel(*refs):
    *mixed_refs, spans_ref, window_ref = refs[:-4]
    out_ref, ordered_ref, flat_ref, query_ref = refs[-4:]
    devices, rows, share = ordered_ref.shape
    _, requests, span, width = window_ref.shape
    steps = rows // requests
    block_rows = BLOCK_HEADS * steps
    place = lax.axis_index("seq")
    in_order(mixed_refs, ordered_ref)
    for d in range(devices):
        if d * share < width:
            flat_ref[:, d * share : (d + 1) * share] = ordered_ref[d].astype(jnp.float32)
    own_head = head_masks(block_rows, width, steps)
    for r in range(requests):
        queries = flat_ref[r * steps : (r + 1) * steps, 0:width]
        query_ref[r] = (jnp.concatenate([queries] * BLOCK_HEADS, axis=0) * own_head).astype(
            jnp.bfloat16
        )
    base = place * span
    scale = HD ** (-0.5)
    pair = 2 * steps
    tiles = HEADS * steps // pair
    slot = base + lax.broadcasted_iota(jnp.int32, (pair, span), 1)
    step = lax.broadcasted_iota(jnp.int32, (pair, span), 0) % steps
    stat_lane = lax.broadcasted_iota(jnp.int32, (HEADS * steps, LANES), 1)
    stat_head = lax.broadcasted_iota(jnp.int32, (HEADS * steps, LANES), 0) // steps
    cols = [slice(c, c + BLOCK) for c in range(0, width, BLOCK)]

    def score(r):
        keys = window_ref.at[0, r]
        return jnp.concatenate(
            [dot(query_ref[r, :, c], keys[:, c], ROWS_BY_ROWS) for c in cols], axis=0
        )

    scores = score(0)
    for r in range(requests):
        following = score(r + 1) if r + 1 < requests else None
        length = spans_ref[r : r + 1, 0:1]
        age = jnp.bitwise_and(slot - (length - SINKS), WIN - 1)
        live = ((slot < jnp.minimum(WIN, length - SINKS)) & (age > step))[None]
        scores = jnp.where(live, scores.reshape(tiles, pair, span) * scale, MASKED)
        peak = jnp.max(scores, axis=-1, keepdims=True)
        weight = jnp.where(live, jnp.exp(scores - peak), 0.0)
        total = jnp.sum(weight, axis=-1, keepdims=True)
        weight = weight.reshape(HEADS * steps, span).astype(jnp.bfloat16)
        values = window_ref.at[1, r]
        outs = []
        for b, c in enumerate(cols):
            own = slice(b * block_rows, (b + 1) * block_rows)
            mixed = dot(weight[own], values[:, c]) * own_head[:, c]
            mixed = sum(mixed[i : i + pair] for i in range(0, block_rows, pair))
            outs.append(mixed[:steps] + mixed[steps:])
        stats = jnp.zeros((HEADS * steps, LANES), jnp.float32)
        parts = split(peak.reshape(HEADS * steps, 1), PIECES)
        parts = parts + split(total.reshape(HEADS * steps, 1), PIECES)
        for i, part in enumerate(parts):
            stats = jnp.where(
                stat_lane == stat_head + i * HEADS, part.astype(jnp.float32), stats
            )
        stats = jnp.sum(stats.reshape(tiles, pair, LANES), axis=0)
        outs.append(stats[:steps] + stats[steps:])
        flat_ref[r * steps : (r + 1) * steps, :] = jnp.concatenate(outs, axis=1)
        scores = following
    out_ref[...] = flat_ref[...].astype(jnp.bfloat16)


def extra_kernel(*refs):
    *mixed_refs, sinks_ref = refs[:-6]
    out_ref, stats_ref, ordered_ref, flat_ref, query_ref, keys_ref = refs[-6:]
    devices, rows, share = ordered_ref.shape
    _, requests, sinks, width = sinks_ref.shape
    steps = rows // requests
    block_rows = BLOCK_HEADS * steps
    count = sinks + steps
    in_order(mixed_refs, ordered_ref)
    for d in range(devices):
        flat_ref[:, d * share : (d + 1) * share] = ordered_ref[d].astype(jnp.float32)
    own_head = head_masks(block_rows, width, steps)
    for r in range(requests):
        own = slice(r * steps, (r + 1) * steps)
        queries = jnp.concatenate([flat_ref[own, 0:width]] * BLOCK_HEADS, axis=0) * own_head
        query_ref[r * block_rows : (r + 1) * block_rows, :] = queries
        for p in range(2):
            keys_ref[p, r * count : r * count + sinks] = sinks_ref[p, r].astype(jnp.float32)
            keys_ref[p, r * count + sinks : (r + 1) * count] = flat_ref[
                own, (p + 1) * width : (p + 2) * width
            ]
    all_rows = requests * block_rows
    all_keys = requests * count
    row = lax.broadcasted_iota(jnp.int32, (all_rows, all_keys), 0)
    key = lax.broadcasted_iota(jnp.int32, (all_rows, all_keys), 1)
    live = (row // block_rows == key // count) & (key % count - sinks <= row % steps)
    stat_lane = lax.broadcasted_iota(jnp.int32, (all_rows, LANES), 1)
    stat_head = lax.broadcasted_iota(jnp.int32, (all_rows, LANES), 0) % block_rows // steps
    whole_mask = jnp.concatenate([own_head[:, :BLOCK]] * requests, axis=0)
    stats = jnp.zeros((all_rows, LANES), jnp.float32)
    pair = 2 * steps

    def by_request(values):
        values = jnp.sum(values.reshape(requests, block_rows // pair, pair, values.shape[-1]), axis=1)
        return values[:, :steps] + values[:, steps:]

    for b in range(width // BLOCK):
        c = slice(b * BLOCK, (b + 1) * BLOCK)
        scores = dot(
            query_ref[:, c].astype(jnp.bfloat16), keys_ref[0, :, c].astype(jnp.bfloat16), ROWS_BY_ROWS
        )
        scores = jnp.where(live, scores * HD ** (-0.5), MASKED)
        peak = jnp.max(scores, axis=-1, keepdims=True)
        weight = jnp.where(live, jnp.exp(scores - peak), 0.0)
        total = jnp.sum(weight, axis=-1, keepdims=True)
        mixed = dot(weight.astype(jnp.bfloat16), keys_ref[1, :, c].astype(jnp.bfloat16))
        mixed = by_request(mixed * whole_mask)
        for r in range(requests):
            out_ref[r * steps : (r + 1) * steps, c] = mixed[r]
        stats = jnp.where(stat_lane == stat_head + b * BLOCK_HEADS, peak, stats)
        stats = jnp.where(stat_lane == stat_head + b * BLOCK_HEADS + HEADS, total, stats)
    stats = by_request(stats)
    for r in range(requests):
        stats_ref[r * steps : (r + 1) * steps, :] = stats[r]


def project_kernel(*refs):
    *part_refs, extra_ref, extra_stats_ref, weight_ref, tokens_ref, turned_ref = refs[:-4]
    out_ref, residual_ref, ordered_ref, rows_ref = refs[-4:]
    devices, rows, padded = ordered_ref.shape
    width = padded - LANES
    in_order(part_refs, ordered_ref)
    stats = [ordered_ref[d][:, width:].astype(jnp.float32) for d in range(devices)]

    def joined(stat, first):
        return sum(
            stat[:, (first + i) * HEADS : (first + i + 1) * HEADS] for i in range(PIECES)
        )

    peaks = [joined(stat, 0) for stat in stats] + [extra_stats_ref[:, :HEADS]]
    totals = [joined(stat, PIECES) for stat in stats] + [extra_stats_ref[:, HEADS : 2 * HEADS]]
    overall = functools.reduce(jnp.maximum, peaks)
    factors = [jnp.exp(peak - overall) for peak in peaks]
    total = sum(f * t for f, t in zip(factors, totals))
    inverse = 1.0 / total
    head_of_row = lax.broadcasted_iota(jnp.int32, (HEADS, width), 0)
    head_of_col = lax.broadcasted_iota(jnp.int32, (HEADS, width), 1) // HD
    expand = (head_of_row == head_of_col).astype(jnp.bfloat16)

    spread = jnp.concatenate([factor * inverse for factor in factors], axis=0)
    spread = sum(dot(part, expand) for part in split(spread, 2))
    attended = spread[devices * rows :] * extra_ref[...]
    for d in range(devices):
        share = spread[d * rows : (d + 1) * rows]
        attended = attended + share * ordered_ref[d][:, :width].astype(jnp.float32)
    projected = dot(attended.astype(jnp.bfloat16), weight_ref[...], ROWS_BY_ROWS).astype(jnp.bfloat16)
    copy_rows(tokens_ref, rows_ref)
    share = weight_ref.shape[0]
    feature = lax.broadcasted_iota(jnp.int32, (width, share), 0)
    column = lax.broadcasted_iota(jnp.int32, (width, share), 1)
    own = (feature == column + lax.axis_index("seq") * share).astype(jnp.bfloat16)
    residual = dot(rows_ref[...].astype(jnp.bfloat16), own) + projected.astype(jnp.float32)
    residual_ref[...] = residual
    turned = turned_ref[...].astype(jnp.bfloat16)
    table = sum(dot(turned, part) for part in split(residual, PIECES))
    groups = lax.axis_size("exp")
    local_experts = EXPERTS // groups
    for s in range(devices):
        for x in range(groups):
            row = (x * local_experts + s // (devices // local_experts)) * CAP
            out_ref[s * groups + x] = table[row : row + CAP]


def home_kernel(devices, *refs):
    residual_refs, refs = refs[:devices], refs[devices:]
    gain_ref, router_ref, select_ref, chosen_ref, residual_ref, gates_ref, ordered_ref = refs
    in_order(residual_refs, ordered_ref)
    residual = jnp.concatenate([ordered_ref[d] for d in range(devices)], axis=1)
    residual_ref[...] = residual
    normed = rms_rows(residual, gain_ref[...])
    logits = dot(normed, router_ref[...], ROWS_BY_ROWS)
    gates = jnp.zeros(select_ref.shape[1:], jnp.float32)
    for c in range(TOPK):
        logit = jnp.sum(chosen_ref[c][:, :EXPERTS] * logits, axis=-1, keepdims=True)
        gates = gates + jax.nn.sigmoid(logit) * select_ref[c]
    gates_ref[...] = gates


def expert_kernel(
    received_ref, gain_ref, piece_ref, in_ref, down_ref, keep_ref, send_ref, in_buf, down_buf, sems
):
    hidden_units, width = down_buf.shape
    held = piece_ref.shape[1]
    pieces = [(at, min(PIECE, hidden_units - at)) for at in range(held, hidden_units, PIECE)]
    pairs = []
    for at, count in pieces:
        for p in range(2):
            pairs.append(
                (in_ref.at[p, 0, pl.ds(at, count)], in_buf.at[p, pl.ds(at - held, count)])
            )
    copies = started(pairs + [(down_ref.at[0], down_buf)], sems)
    devices = lax.axis_size("seq")
    groups = lax.axis_size("exp")
    columns = []
    for s in range(devices):
        columns.append(
            jnp.concatenate([received_ref[s * groups + g] for g in range(groups)], axis=0)
        )
    rows = rms_rows(jnp.concatenate(columns, axis=1), gain_ref[...])

    def layer(gate_weight, up_weight):
        gate = dot(rows, gate_weight, ROWS_BY_ROWS)
        up = dot(rows, up_weight, ROWS_BY_ROWS)
        return (jax.nn.gelu(gate, approximate=True) * up).astype(jnp.bfloat16)

    hidden = [layer(piece_ref[0], piece_ref[1])]
    for i, (at, count) in enumerate(pieces):
        copies[2 * i].wait()
        copies[2 * i + 1].wait()
        own = slice(at - held, at - held + count)
        hidden.append(layer(in_buf[0, own], in_buf[1, own]))
    copies[-1].wait()
    outputs = dot(jnp.concatenate(hidden, axis=1), down_buf[...])
    half = width // 2
    odd = lax.axis_index("seq") % 2 == 1
    keep_ref[...] = jnp.where(odd, outputs[:, half:], outputs[:, :half])
    send_ref[...] = jnp.where(odd, outputs[:, :half], outputs[:, half:])


def spread_kernel(kept_ref, other_ref, out_ref):
    slots = out_ref.shape[1]
    groups = kept_ref.shape[0] // slots
    outputs = kept_ref[...] + other_ref[...]
    for block in range(out_ref.shape[0]):
        first = block % groups * slots
        out_ref[block] = outputs[first : first + slots].astype(jnp.bfloat16)


def column_block(sharer, sharers):
    block = 0
    while sharers > 1:
        sharers //= 2
        block += (sharer & 1) * sharers
        sharer >>= 1
    return block


def final_kernel(gates_ref, returned_ref, residual_ref, out_ref, table_ref):
    requests, steps, width = out_ref.shape
    devices, groups, slots, part = returned_ref.shape
    local_experts = EXPERTS // groups
    sharers = devices // local_experts
    for s in range(devices):
        first = column_block(s % sharers, sharers) * part
        for x in range(groups):
            row = (x * local_experts + s // sharers) * slots
            table_ref[row : row + slots, first : first + part] = returned_ref[s, x].astype(jnp.float32)
    table = table_ref[...].astype(jnp.bfloat16)
    moe = sum(dot(part, table) for part in split(gates_ref[...], 2))
    total = residual_ref[...] + moe
    for r in range(requests):
        out_ref[r] = total[r * steps : (r + 1) * steps].astype(jnp.bfloat16)


def gather_seq(values, meanwhile=None):
    count = lax.axis_size("seq")

    def exchange(value, bits):
        return lax.ppermute(value, "seq", [(i, i ^ bits) for i in range(count)])

    near = [exchange(values, k) for k in range(2, count, 2)]
    if meanwhile is not None:
        values = meanwhile(values)
    near = [values] + near
    return [part for value in near for part in (value, exchange(value, 1))]


def shape(dims, dtype):
    return jax.ShapeDtypeStruct(dims, dtype)


def body(
    tokens,
    attn_gain,
    w_qkv,
    window_cache,
    sink_cache,
    lengths,
    w_out,
    moe_gain,
    router,
    expert_ids,
    slot_order,
    expert_in,
    expert_down,
):
    requests, steps, width = tokens.shape
    rows = requests * steps
    seq_index = lax.axis_index("seq")
    seq_count = lax.axis_size("seq")
    groups = lax.axis_size("exp")
    local_experts = EXPERTS // groups
    sharers = seq_count // local_experts
    span = window_cache.shape[2]
    share = w_qkv.shape[0]
    slots = EXPERTS * CAP
    f32, bf16 = jnp.float32, jnp.bfloat16

    vmem = pl.BlockSpec(memory_space=pltpu.VMEM)
    hbm = pl.BlockSpec(memory_space=pltpu.HBM)

    gain_row = attn_gain.reshape(1, width)
    local_mix = pl.pallas_call(
        qkv_kernel,
        in_specs=[hbm] * 4,
        out_shape=shape((rows, share), bf16),
        scratch_shapes=[
            pltpu.VMEM(tokens.shape, bf16),
            pltpu.VMEM(gain_row.shape, f32),
            pltpu.VMEM(w_qkv.shape, bf16),
            pltpu.VMEM((rows, width), f32),
            pltpu.SemaphoreType.DMA((4,)),
        ],
        compiler_params=params(4),
        name="qkv",
    )(in_hbm(tokens), in_hbm(gain_row), in_hbm(w_qkv), in_hbm(window_cache))

    fetched = []

    def routing(values):
        held, *outputs = pl.pallas_call(
            routing_kernel,
            in_specs=[vmem] + [hbm] * 3,
            out_shape=(
                shape(values.shape, bf16),
                shape((requests, LANES), jnp.int32),
                shape((TOPK, rows, slots), f32),
                shape((TOPK, rows, LANES), f32),
                shape((slots, rows), f32),
            ),
            scratch_shapes=[
                pltpu.SMEM((requests,), jnp.int32),
                pltpu.VMEM((steps, TOPK, requests), jnp.int32),
                pltpu.VMEM(slot_order.shape, jnp.int32),
                pltpu.SemaphoreType.DMA((3,)),
            ],
            compiler_params=params(8),
            name="routing",
        )(
            values,
            in_hbm(lengths),
            in_hbm(expert_ids.transpose(1, 2, 0)),
            in_hbm(slot_order),
        )
        fetched.extend(outputs)
        return held

    mixed = gather_seq(local_mix, routing)
    spans, select, chosen, turned = fetched

    padded = width + LANES
    part = pl.pallas_call(
        attention_kernel,
        in_specs=[vmem] * (seq_count + 2),
        out_shape=shape((rows, padded), bf16),
        scratch_shapes=[
            pltpu.VMEM((seq_count, rows, share), bf16),
            pltpu.VMEM((rows, padded), f32),
            pltpu.VMEM((requests, BLOCK_HEADS * steps, width), bf16),
        ],
        compiler_params=params(8),
        name="attention",
    )(*mixed, spans, window_cache)
    hidden_units = expert_down.shape[1]
    held_units = min(PIECE, hidden_units)
    late_units = max(hidden_units - held_units, 16)

    def fetch_expert(values):
        held, piece = pl.pallas_call(
            fetch_expert_kernel,
            in_specs=[vmem, hbm],
            out_shape=(shape(values.shape, bf16), shape((2, held_units, width), bf16)),
            scratch_shapes=[pltpu.SemaphoreType.DMA((2,))],
            compiler_params=params(8),
            cost_estimate=moving(4 * held_units * width),
            name="fetch_expert",
        )(values, in_hbm(expert_in))
        fetched.append(piece)
        return held

    parts = gather_seq(part, fetch_expert)
    piece = fetched[-1]

    extra, extra_stats = pl.pallas_call(
        extra_kernel,
        out_shape=(shape((rows, width), f32), shape((rows, LANES), f32)),
        scratch_shapes=[
            pltpu.VMEM((seq_count, rows, share), bf16),
            pltpu.VMEM((rows, 3 * width), f32),
            pltpu.VMEM((rows * BLOCK_HEADS, width), f32),
            pltpu.VMEM((2, requests * (SINKS + steps), width), f32),
        ],
        compiler_params=params(8),
        name="extra",
    )(*mixed, sink_cache)

    outgoing, residual_columns = pl.pallas_call(
        project_kernel,
        out_shape=(
            shape((seq_count * groups, CAP, w_out.shape[0]), f32),
            shape((rows, w_out.shape[0]), f32),
        ),
        scratch_shapes=[
            pltpu.VMEM((seq_count, rows, padded), bf16),
            pltpu.VMEM((rows, width), f32),
        ],
        compiler_params=params(16),
        name="project",
    )(*parts, extra, extra_stats, w_out, tokens, turned)
    received = lax.all_to_all(outgoing, ("seq", "exp"), split_axis=0, concat_axis=0, tiled=True)
    columns = gather_seq(residual_columns)

    moe_row = moe_gain.reshape(1, width)
    kept, sent = pl.pallas_call(
        expert_kernel,
        in_specs=[vmem, vmem, vmem, hbm, hbm],
        out_shape=(
            shape((groups * CAP, width // 2), f32),
            shape((groups * CAP, width // 2), f32),
        ),
        scratch_shapes=[
            pltpu.VMEM((2, late_units, width), bf16),
            pltpu.VMEM((hidden_units, width), bf16),
            pltpu.SemaphoreType.DMA((2 * pl.cdiv(hidden_units, PIECE) + 1,)),
        ],
        compiler_params=params(20),
        name="expert",
    )(received, moe_row, piece, in_hbm(expert_in), in_hbm(expert_down))

    reach = 1
    while True:
        other = lax.ppermute(sent, "seq", [(i, i ^ reach) for i in range(seq_count)])
        reach *= 2
        if reach >= sharers:
            break
        upper = (seq_index // reach) % 2 == 1
        low, high = jnp.split(kept + other, 2, axis=1)
        kept, sent = jnp.where(upper, high, low), jnp.where(upper, low, high)
    part_width = kept.shape[1]
    outgoing = pl.pallas_call(
        spread_kernel,
        out_shape=shape((seq_count * groups, CAP, part_width), bf16),
        compiler_params=params(8),
        name="spread",
    )(kept, other)
    returned = lax.all_to_all(
        outgoing,
        ("seq", "exp"),
        split_axis=0,
        concat_axis=0,
        tiled=True,
    ).reshape(seq_count, groups, CAP, part_width)

    columns, _ = lax.optimization_barrier((columns, outgoing))
    residual, gates = pl.pallas_call(
        functools.partial(home_kernel, seq_count),
        out_shape=(shape((rows, width), f32), shape((rows, slots), f32)),
        scratch_shapes=[pltpu.VMEM((seq_count, rows, w_out.shape[0]), f32)],
        compiler_params=params(8),
        name="home",
    )(*columns, moe_row, router.T, select, chosen)

    return pl.pallas_call(
        final_kernel,
        out_shape=shape((requests, steps, width), bf16),
        scratch_shapes=[pltpu.VMEM((slots, width), f32)],
        compiler_params=params(8),
        name="final",
    )(gates, returned, residual)


def solution(mesh):
    in_specs = (
        P("exp", None, None),
        P(),
        P("seq", None),
        P(None, "exp", "seq", None),
        P(None, "exp", None, None),
        P("exp"),
        P("seq", None),
        P(),
        P(),
        P("exp", None, None),
        P("exp", None),
        P(None, "exp", "seq", None),
        P("exp", "seq", None),
    )
    out_specs = P("exp", None, None)
    return jax.shard_map(body, mesh=mesh, in_specs=in_specs, out_specs=out_specs, check_vma=False)
```

```python
import functools

import jax
import jax.numpy as jnp
from jax import lax
from jax.experimental import pallas as pl
from jax.experimental.pallas import tpu as pltpu
from jax.sharding import PartitionSpec as P

HEADS = 16
HD = 64
EXPERTS = 16
TOPK = 2
SINKS = 4
WIN = 4096
CAP = 8
LANES = 128
PIECES = 3
FIRST_KEYS = 2
SECOND_KEYS = 8
SECOND_VALUES = 3
HELD = 768
PIECE = 320
AHEAD = 10
BLOCK = 256
BLOCK_HEADS = BLOCK // HD

EPSILON = 1e-06
MASKED = -1e30
MIB = 1 << 20
ROWS_BY_ROWS = (((1,), (1,)), ((), ()))
ROWS_BY_COLS = (((1,), (0,)), ((), ()))


def dot(a, b, dims=ROWS_BY_COLS):
    return lax.dot_general(a, b, dims, preferred_element_type=jnp.float32)


def params(limit_mib=32):
    return pltpu.CompilerParams(vmem_limit_bytes=limit_mib * MIB)


def moving(count):
    return pl.CostEstimate(flops=0, bytes_accessed=count, transcendentals=0)


def in_hbm(value):
    return pltpu.with_memory_space_constraint(value, pltpu.HBM)


def split(value, count):
    parts = []
    for _ in range(count):
        part = value.astype(jnp.bfloat16)
        parts.append(part)
        value = value - part.astype(jnp.float32)
    return parts


def exact_dot(values, table):
    high, low = split(values, 2)
    both = dot(jnp.concatenate([high, low], axis=0), table)
    return both[: values.shape[0]] + both[values.shape[0] :]


def rms_rows(widened, gain_row):
    inverse = lax.rsqrt(jnp.mean(widened * widened, axis=-1, keepdims=True) + EPSILON)
    return (widened * inverse * gain_row).astype(jnp.bfloat16)


def copy_rows(source_ref, rows_ref):
    requests, steps, _ = source_ref.shape
    for r in range(requests):
        rows_ref[r * steps : (r + 1) * steps, :] = source_ref[r].astype(rows_ref.dtype)


def each(sems):
    return [sems.at[i] for i in range(sems.shape[0])]


def started(pairs, sems):
    copies = [pltpu.make_async_copy(*pair, sem) for pair, sem in zip(pairs, sems)]
    for copy in copies:
        copy.start()
    return copies


def route(ids_ref, order_ref, select_ref, chosen_ref):
    steps, _, requests = ids_ref.shape
    rows = requests * steps
    lane = lax.broadcasted_iota(jnp.int32, (rows, LANES), 1)
    own_row = lax.broadcasted_iota(jnp.int32, (rows, requests), 0)
    own_request = lax.broadcasted_iota(jnp.int32, (rows, requests), 1) == own_row // steps
    chosen = []
    for c in range(TOPK):
        ids = jnp.zeros((rows, requests), jnp.int32)
        for t in range(steps):
            ids = jnp.where(own_request & (own_row % steps == t), ids_ref[t, c : c + 1, :], ids)
        chosen.append(jnp.sum(ids.astype(jnp.float32), axis=1, keepdims=True).astype(jnp.int32))
    onehot = [(lane == ids).astype(jnp.float32) for ids in chosen]
    square_row = lax.broadcasted_iota(jnp.int32, (rows, rows), 0)
    square_col = lax.broadcasted_iota(jnp.int32, (rows, rows), 1)
    order_wide = jnp.broadcast_to(order_ref[...], (rows, rows))
    down = jnp.sum(
        jnp.where(square_row == square_col, order_wide, 0).astype(jnp.float32),
        axis=1,
        keepdims=True,
    )
    earlier = (order_wide.astype(jnp.float32) < down).astype(jnp.bfloat16)
    counts = dot(earlier, sum(onehot).astype(jnp.bfloat16))
    slot = lax.broadcasted_iota(jnp.int32, (rows, EXPERTS * CAP), 1)
    both = jnp.zeros((rows, EXPERTS * CAP), jnp.float32)
    for c in range(TOPK):
        position = jnp.sum(onehot[c] * counts, axis=-1, keepdims=True).astype(jnp.int32)
        column = chosen[c] * CAP + position
        select = ((column == slot) & (position < CAP)).astype(jnp.float32)
        select_ref[c] = select
        chosen_ref[c] = onehot[c]
        both = both + select
    return jnp.transpose(both)


def qkv_kernel(
    tokens_ref,
    gain_ref,
    weight_ref,
    window_ref,
    out_ref,
    token_buf,
    gain_buf,
    weight_buf,
    rows_ref,
    sems,
):
    copies = started(
        (
            (tokens_ref, token_buf),
            (gain_ref, gain_buf),
            (weight_ref, weight_buf),
        ),
        each(sems),
    )
    for copy in copies[:2]:
        copy.wait()
    copy_rows(token_buf, rows_ref)
    normed = rms_rows(rows_ref[...], gain_buf[...])
    copies[2].wait()
    out_ref[...] = dot(normed, weight_buf[...], ROWS_BY_ROWS).astype(jnp.bfloat16)


def in_order(sent_refs, ordered_ref):
    place = lax.axis_index("seq")
    for k, sent_ref in enumerate(sent_refs):
        ordered_ref[jnp.bitwise_xor(place, k)] = sent_ref[...]


def head_masks(rows, width, steps):
    row_head = lax.broadcasted_iota(jnp.int32, (rows, width), 0) // steps % BLOCK_HEADS
    col_head = lax.broadcasted_iota(jnp.int32, (rows, width), 1) // HD % BLOCK_HEADS
    return (row_head == col_head).astype(jnp.float32)


def routing_kernel(
    sent_ref,
    lengths_ref,
    ids_ref,
    order_ref,
    tokens_ref,
    held_ref,
    spans_ref,
    select_ref,
    chosen_ref,
    turned_ref,
    columns_ref,
    numbers_ref,
    ids_buf,
    order_buf,
    tokens_buf,
    rows_ref,
    sems,
):
    copies = started(
        (
            (ids_ref, ids_buf),
            (order_ref, order_buf),
            (lengths_ref, numbers_ref),
            (tokens_ref, tokens_buf),
        ),
        each(sems),
    )
    held_ref[...] = sent_ref[...]
    for copy in copies:
        copy.wait()
    turned_ref[...] = route(ids_buf, order_buf, select_ref, chosen_ref)
    for r in range(spans_ref.shape[0]):
        spans_ref[r : r + 1, :] = jnp.full((1, LANES), numbers_ref[r], jnp.int32)
    copy_rows(tokens_buf, rows_ref)
    width, share = rows_ref.shape[1], columns_ref.shape[1]
    feature = lax.broadcasted_iota(jnp.int32, (width, share), 0)
    column = lax.broadcasted_iota(jnp.int32, (width, share), 1)
    own = (feature == column + lax.axis_index("seq") * share).astype(jnp.bfloat16)
    columns_ref[...] = dot(rows_ref[...].astype(jnp.bfloat16), own)


def fetch_expert_kernel(sent_ref, in_ref, held_ref, piece_ref, sems):
    copies = started([(in_ref.at[p, 0, pl.ds(0, piece_ref.shape[1])], piece_ref.at[p]) for p in range(2)], each(sems))
    held_ref[...] = sent_ref[...]
    for copy in copies:
        copy.wait()


def attention_kernel(*refs):
    *mixed_refs, spans_ref, window_ref = refs[:-4]
    out_ref, ordered_ref, flat_ref, query_ref = refs[-4:]
    devices, rows, share = ordered_ref.shape
    _, requests, span, width = window_ref.shape
    steps = rows // requests
    block_rows = BLOCK_HEADS * steps
    place = lax.axis_index("seq")
    in_order(mixed_refs, ordered_ref)
    for d in range(devices):
        if d * share < width:
            flat_ref[:, d * share : (d + 1) * share] = ordered_ref[d].astype(jnp.float32)
    own_head = head_masks(block_rows, width, steps)
    for r in range(requests):
        queries = flat_ref[r * steps : (r + 1) * steps, 0:width]
        query_ref[r] = (jnp.concatenate([queries] * BLOCK_HEADS, axis=0) * own_head).astype(
            jnp.bfloat16
        )
    base = place * span
    scale = HD ** (-0.5)
    pair = 2 * steps
    tiles = HEADS * steps // pair
    slot = base + lax.broadcasted_iota(jnp.int32, (pair, span), 1)
    step = lax.broadcasted_iota(jnp.int32, (pair, span), 0) % steps
    stat_lane = lax.broadcasted_iota(jnp.int32, (HEADS * steps, LANES), 1)
    stat_head = lax.broadcasted_iota(jnp.int32, (HEADS * steps, LANES), 0) // steps
    cols = [slice(c, c + BLOCK) for c in range(0, width, BLOCK)]

    def score(r):
        keys = window_ref.at[0, r]
        return jnp.concatenate(
            [dot(query_ref[r, :, c], keys[:, c], ROWS_BY_ROWS) for c in cols], axis=0
        )

    scores = score(0)
    for r in range(requests):
        following = score(r + 1) if r + 1 < requests else None
        length = spans_ref[r : r + 1, 0:1]
        age = jnp.bitwise_and(slot - (length - SINKS), WIN - 1)
        live = ((slot < jnp.minimum(WIN, length - SINKS)) & (age > step))[None]
        scores = jnp.where(live, scores.reshape(tiles, pair, span) * scale, MASKED)
        peak = jnp.max(scores, axis=-1, keepdims=True)
        weight = jnp.where(live, jnp.exp(scores - peak), 0.0)
        total = jnp.sum(weight, axis=-1, keepdims=True)
        weight = weight.reshape(HEADS * steps, span).astype(jnp.bfloat16)
        values = window_ref.at[1, r]
        outs = []
        for b, c in enumerate(cols):
            own = slice(b * block_rows, (b + 1) * block_rows)
            mixed = dot(weight[own], values[:, c]) * own_head[:, c]
            mixed = sum(mixed[i : i + pair] for i in range(0, block_rows, pair))
            outs.append(mixed[:steps] + mixed[steps:])
        stats = jnp.where(stat_lane == stat_head, peak.reshape(HEADS * steps, 1), 0.0)
        stats = jnp.where(stat_lane == stat_head + HEADS, total.reshape(HEADS * steps, 1), stats)
        stats = jnp.sum(stats.reshape(tiles, pair, LANES), axis=0)
        outs.append(stats[:steps] + stats[steps:])
        flat_ref[r * steps : (r + 1) * steps, :] = jnp.concatenate(outs, axis=1)
        scores = following
    out_ref[:, :width] = flat_ref[:, :width].astype(jnp.bfloat16)
    parts = []
    for first in (0, HEADS):
        parts += split(flat_ref[:, width + first : width + first + HEADS], PIECES)
    blank = jnp.zeros((rows, LANES - 2 * PIECES * HEADS), jnp.float32)
    parts = [part.astype(jnp.float32) for part in parts] + [blank]
    out_ref[:, width:] = jnp.concatenate(parts, axis=1).astype(jnp.bfloat16)


def extra_kernel(*refs):
    *mixed_refs, sinks_ref = refs[:-6]
    out_ref, stats_ref, ordered_ref, flat_ref, query_ref, keys_ref = refs[-6:]
    devices, rows, share = ordered_ref.shape
    _, requests, sinks, width = sinks_ref.shape
    steps = rows // requests
    block_rows = BLOCK_HEADS * steps
    count = sinks + steps
    in_order(mixed_refs, ordered_ref)
    for d in range(devices):
        flat_ref[:, d * share : (d + 1) * share] = ordered_ref[d].astype(jnp.float32)
    own_head = head_masks(block_rows, width, steps)
    for r in range(requests):
        own = slice(r * steps, (r + 1) * steps)
        queries = jnp.concatenate([flat_ref[own, 0:width]] * BLOCK_HEADS, axis=0) * own_head
        query_ref[r * block_rows : (r + 1) * block_rows, :] = queries
        for p in range(2):
            keys_ref[p, r * count : r * count + sinks] = sinks_ref[p, r].astype(jnp.float32)
            keys_ref[p, r * count + sinks : (r + 1) * count] = flat_ref[
                own, (p + 1) * width : (p + 2) * width
            ]
    all_rows = requests * block_rows
    all_keys = requests * count
    row = lax.broadcasted_iota(jnp.int32, (all_rows, all_keys), 0)
    key = lax.broadcasted_iota(jnp.int32, (all_rows, all_keys), 1)
    live = (row // block_rows == key // count) & (key % count - sinks <= row % steps)
    stat_lane = lax.broadcasted_iota(jnp.int32, (all_rows, LANES), 1)
    stat_head = lax.broadcasted_iota(jnp.int32, (all_rows, LANES), 0) % block_rows // steps
    whole_mask = jnp.concatenate([own_head[:, :BLOCK]] * requests, axis=0)
    stats = jnp.zeros((all_rows, LANES), jnp.float32)
    pair = 2 * steps

    def by_request(values):
        values = jnp.sum(values.reshape(requests, block_rows // pair, pair, values.shape[-1]), axis=1)
        return values[:, :steps] + values[:, steps:]

    for b in range(width // BLOCK):
        c = slice(b * BLOCK, (b + 1) * BLOCK)
        scores = dot(
            query_ref[:, c].astype(jnp.bfloat16), keys_ref[0, :, c].astype(jnp.bfloat16), ROWS_BY_ROWS
        )
        scores = jnp.where(live, scores * HD ** (-0.5), MASKED)
        peak = jnp.max(scores, axis=-1, keepdims=True)
        weight = jnp.where(live, jnp.exp(scores - peak), 0.0)
        total = jnp.sum(weight, axis=-1, keepdims=True)
        mixed = dot(weight.astype(jnp.bfloat16), keys_ref[1, :, c].astype(jnp.bfloat16))
        mixed = by_request(mixed * whole_mask)
        for r in range(requests):
            out_ref[r * steps : (r + 1) * steps, c] = mixed[r]
        stats = jnp.where(stat_lane == stat_head + b * BLOCK_HEADS, peak, stats)
        stats = jnp.where(stat_lane == stat_head + b * BLOCK_HEADS + HEADS, total, stats)
    stats = by_request(stats)
    for r in range(requests):
        stats_ref[r * steps : (r + 1) * steps, :] = stats[r]


def project_kernel(*refs):
    *part_refs, extra_ref, extra_stats_ref, weight_ref, columns_ref, turned_ref = refs[:-2]
    out_ref, residual_ref = refs[-2:]
    devices = len(part_refs)
    rows, width = extra_ref.shape
    stats = [part_ref[:, width:].astype(jnp.float32) for part_ref in part_refs]

    def joined(stat, first):
        return sum(
            stat[:, (first + i) * HEADS : (first + i + 1) * HEADS] for i in range(PIECES)
        )

    peaks = [joined(stat, 0) for stat in stats] + [extra_stats_ref[:, :HEADS]]
    totals = [joined(stat, PIECES) for stat in stats] + [extra_stats_ref[:, HEADS : 2 * HEADS]]
    overall = functools.reduce(jnp.maximum, peaks)
    factors = [jnp.exp(peak - overall) for peak in peaks]
    total = sum(f * t for f, t in zip(factors, totals))
    inverse = 1.0 / total
    head_of_row = lax.broadcasted_iota(jnp.int32, (HEADS, width), 0)
    head_of_col = lax.broadcasted_iota(jnp.int32, (HEADS, width), 1) // HD
    expand = (head_of_row == head_of_col).astype(jnp.bfloat16)

    spread = jnp.concatenate([factor * inverse for factor in factors], axis=0)
    spread = exact_dot(spread, expand)
    attended = spread[devices * rows :] * extra_ref[...]
    for d in range(devices):
        share = spread[d * rows : (d + 1) * rows]
        attended = attended + share * part_refs[d][:, :width].astype(jnp.float32)
    projected = dot(attended.astype(jnp.bfloat16), weight_ref[...], ROWS_BY_ROWS).astype(jnp.bfloat16)
    residual = columns_ref[...] + projected.astype(jnp.float32)
    residual_ref[...] = residual
    table = dot(turned_ref[...].astype(jnp.bfloat16), residual.astype(jnp.bfloat16))
    groups = lax.axis_size("exp")
    local_experts = EXPERTS // groups
    for s in range(devices):
        for x in range(groups):
            row = (x * local_experts + s // (devices // local_experts)) * CAP
            out_ref[s * groups + x] = table[row : row + CAP].astype(jnp.bfloat16)


def home_kernel(devices, *refs):
    residual_refs, refs = refs[:devices], refs[devices:]
    gain_ref, router_ref, select_ref, chosen_ref, residual_ref, gates_ref, ordered_ref = refs
    in_order(residual_refs, ordered_ref)
    residual = jnp.concatenate([ordered_ref[d] for d in range(devices)], axis=1)
    residual_ref[...] = residual
    normed = rms_rows(residual, gain_ref[...])
    logits = dot(normed, router_ref[...], ROWS_BY_ROWS)
    gates = jnp.zeros(select_ref.shape[1:], jnp.float32)
    for c in range(TOPK):
        logit = jnp.sum(chosen_ref[c][:, :EXPERTS] * logits, axis=-1, keepdims=True)
        gates = gates + jax.nn.sigmoid(logit) * select_ref[c]
    gates_ref[...] = gates


def expert_kernel(
    received_ref, gain_ref, piece_ref, in_ref, down_ref, keep_ref, send_ref, in_buf, down_buf, sems
):
    hidden_units, width = down_buf.shape
    held = piece_ref.shape[1]
    pieces = [(at, min(PIECE, hidden_units - at)) for at in range(held, hidden_units, PIECE)]
    downs = [(0, held)] + pieces
    stages = []
    for at, count in pieces:
        stages.append(
            [
                (in_ref.at[p, 0, pl.ds(at, count)], in_buf.at[p, pl.ds(at - held, count)])
                for p in range(2)
            ]
        )
    for at, count in downs:
        stages.append([(down_ref.at[0, pl.ds(at, count)], down_buf.at[pl.ds(at, count)])])
    flying = []

    def start_next():
        if len(flying) < len(stages):
            first = sum(len(stage) for stage in stages[: len(flying)])
            flying.append(started(stages[len(flying)], [sems.at[first + i] for i in range(len(stages[len(flying)]))]))

    def wait_for(stage):
        for copy in flying[stage]:
            copy.wait()
        start_next()

    for _ in range(AHEAD):
        start_next()
    devices = lax.axis_size("seq")
    groups = lax.axis_size("exp")
    columns = []
    for s in range(devices):
        columns.append(
            jnp.concatenate(
                [received_ref[s * groups + g].astype(jnp.float32) for g in range(groups)], axis=0
            )
        )
    rows = rms_rows(jnp.concatenate(columns, axis=1), gain_ref[...])

    def layer(gate_weight, up_weight):
        gate = dot(rows, gate_weight, ROWS_BY_ROWS)
        up = dot(rows, up_weight, ROWS_BY_ROWS)
        return (jax.nn.gelu(gate, approximate=True) * up).astype(jnp.bfloat16)

    hidden = [layer(piece_ref[0], piece_ref[1])]
    for i, (at, count) in enumerate(pieces):
        wait_for(i)
        own = slice(at - held, at - held + count)
        hidden.append(layer(in_buf[0, own], in_buf[1, own]))
    outputs = jnp.zeros((groups * CAP, width), jnp.float32)
    for i, (at, count) in enumerate(downs):
        wait_for(len(pieces) + i)
        outputs = outputs + dot(hidden[i], down_buf[at : at + count])
    half = width // 2
    odd = lax.axis_index("seq") % 2 == 1
    keep_ref[...] = jnp.where(odd, outputs[:, half:], outputs[:, :half])
    send_ref[...] = jnp.where(odd, outputs[:, :half], outputs[:, half:])


def spread_kernel(kept_ref, other_ref, out_ref):
    slots = out_ref.shape[1]
    groups = kept_ref.shape[0] // slots
    outputs = kept_ref[...] + other_ref[...]
    for block in range(out_ref.shape[0]):
        first = block % groups * slots
        out_ref[block] = outputs[first : first + slots].astype(jnp.bfloat16)


def column_block(sharer, sharers):
    block = 0
    while sharers > 1:
        sharers //= 2
        block += (sharer & 1) * sharers
        sharer >>= 1
    return block


def final_kernel(gates_ref, returned_ref, residual_ref, out_ref, table_ref):
    requests, steps, width = out_ref.shape
    devices, groups, slots, part = returned_ref.shape
    local_experts = EXPERTS // groups
    sharers = devices // local_experts
    for s in range(devices):
        first = column_block(s % sharers, sharers) * part
        for x in range(groups):
            row = (x * local_experts + s // sharers) * slots
            table_ref[row : row + slots, first : first + part] = returned_ref[s, x].astype(jnp.float32)
    table = table_ref[...].astype(jnp.bfloat16)
    moe = exact_dot(gates_ref[...], table)
    total = residual_ref[...] + moe
    for r in range(requests):
        out_ref[r] = total[r * steps : (r + 1) * steps].astype(jnp.bfloat16)


def gather_seq(values, meanwhile=None):
    count = lax.axis_size("seq")

    def exchange(value, bits):
        return lax.ppermute(value, "seq", [(i, i ^ bits) for i in range(count)])

    near = [exchange(values, k) for k in range(2, count, 2)]
    if meanwhile is not None:
        values = meanwhile(values)
    near = [values] + near
    return [part for value in near for part in (value, exchange(value, 1))]


def shape(dims, dtype):
    return jax.ShapeDtypeStruct(dims, dtype)


def body(
    tokens,
    attn_gain,
    w_qkv,
    window_cache,
    sink_cache,
    lengths,
    w_out,
    moe_gain,
    router,
    expert_ids,
    slot_order,
    expert_in,
    expert_down,
):
    requests, steps, width = tokens.shape
    rows = requests * steps
    seq_index = lax.axis_index("seq")
    seq_count = lax.axis_size("seq")
    groups = lax.axis_size("exp")
    local_experts = EXPERTS // groups
    sharers = seq_count // local_experts
    span = window_cache.shape[2]
    share = w_qkv.shape[0]
    slots = EXPERTS * CAP
    f32, bf16 = jnp.float32, jnp.bfloat16

    vmem = pl.BlockSpec(memory_space=pltpu.VMEM)
    hbm = pl.BlockSpec(memory_space=pltpu.HBM)

    gain_row = attn_gain.reshape(1, width)
    local_mix = pl.pallas_call(
        qkv_kernel,
        in_specs=[hbm] * 4,
        out_shape=shape((rows, share), bf16),
        scratch_shapes=[
            pltpu.VMEM(tokens.shape, bf16),
            pltpu.VMEM(gain_row.shape, f32),
            pltpu.VMEM(w_qkv.shape, bf16),
            pltpu.VMEM((rows, width), f32),
            pltpu.SemaphoreType.DMA((4,)),
        ],
        compiler_params=params(4),
        name="qkv",
    )(in_hbm(tokens), in_hbm(gain_row), in_hbm(w_qkv), in_hbm(window_cache))

    fetched = []

    def routing(values):
        held, *outputs = pl.pallas_call(
            routing_kernel,
            in_specs=[vmem] + [hbm] * 4,
            out_shape=(
                shape(values.shape, bf16),
                shape((requests, LANES), jnp.int32),
                shape((TOPK, rows, slots), f32),
                shape((TOPK, rows, LANES), f32),
                shape((slots, rows), f32),
                shape((rows, w_out.shape[0]), f32),
            ),
            scratch_shapes=[
                pltpu.SMEM((requests,), jnp.int32),
                pltpu.VMEM((steps, TOPK, requests), jnp.int32),
                pltpu.VMEM(slot_order.shape, jnp.int32),
                pltpu.VMEM(tokens.shape, bf16),
                pltpu.VMEM((rows, width), f32),
                pltpu.SemaphoreType.DMA((4,)),
            ],
            compiler_params=params(8),
            name="routing",
        )(
            values,
            in_hbm(lengths),
            in_hbm(expert_ids.transpose(1, 2, 0)),
            in_hbm(slot_order),
            in_hbm(tokens),
        )
        fetched.extend(outputs)
        return held

    mixed = gather_seq(local_mix, routing)
    spans, select, chosen, turned, token_columns = fetched

    padded = width + LANES
    part = pl.pallas_call(
        attention_kernel,
        in_specs=[vmem] * (seq_count + 2),
        out_shape=shape((rows, padded), bf16),
        scratch_shapes=[
            pltpu.VMEM((seq_count, rows, share), bf16),
            pltpu.VMEM((rows, padded), f32),
            pltpu.VMEM((requests, BLOCK_HEADS * steps, width), bf16),
        ],
        compiler_params=params(8),
        name="attention",
    )(*mixed, spans, window_cache)
    hidden_units = expert_down.shape[1]
    held_units = min(HELD, hidden_units)
    late_units = max(hidden_units - held_units, 16)

    def fetch_expert(values):
        held, piece = pl.pallas_call(
            fetch_expert_kernel,
            in_specs=[vmem, hbm],
            out_shape=(shape(values.shape, bf16), shape((2, held_units, width), bf16)),
            scratch_shapes=[pltpu.SemaphoreType.DMA((2,))],
            compiler_params=params(8),
            cost_estimate=moving(4 * held_units * width),
            name="fetch_expert",
        )(values, in_hbm(expert_in))
        fetched.append(piece)
        return held

    parts = gather_seq(part, fetch_expert)
    piece = fetched[-1]

    extra, extra_stats = pl.pallas_call(
        extra_kernel,
        out_shape=(shape((rows, width), f32), shape((rows, LANES), f32)),
        scratch_shapes=[
            pltpu.VMEM((seq_count, rows, share), bf16),
            pltpu.VMEM((rows, 3 * width), f32),
            pltpu.VMEM((rows * BLOCK_HEADS, width), f32),
            pltpu.VMEM((2, requests * (SINKS + steps), width), f32),
        ],
        compiler_params=params(8),
        name="extra",
    )(*mixed, sink_cache)

    outgoing, residual_columns = pl.pallas_call(
        project_kernel,
        out_shape=(
            shape((seq_count * groups, CAP, w_out.shape[0]), bf16),
            shape((rows, w_out.shape[0]), f32),
        ),
        compiler_params=params(16),
        name="project",
    )(*parts, extra, extra_stats, w_out, token_columns, turned)
    received = lax.all_to_all(outgoing, ("seq", "exp"), split_axis=0, concat_axis=0, tiled=True)
    columns = gather_seq(residual_columns)

    moe_row = moe_gain.reshape(1, width)
    kept, sent = pl.pallas_call(
        expert_kernel,
        in_specs=[vmem, vmem, vmem, hbm, hbm],
        out_shape=(
            shape((groups * CAP, width // 2), f32),
            shape((groups * CAP, width // 2), f32),
        ),
        scratch_shapes=[
            pltpu.VMEM((2, late_units, width), bf16),
            pltpu.VMEM((hidden_units, width), bf16),
            pltpu.SemaphoreType.DMA((3 * pl.cdiv(late_units, PIECE) + 1,)),
        ],
        compiler_params=params(20),
        name="expert",
    )(received, moe_row, piece, in_hbm(expert_in), in_hbm(expert_down))

    reach = 1
    while True:
        other = lax.ppermute(sent, "seq", [(i, i ^ reach) for i in range(seq_count)])
        reach *= 2
        if reach >= sharers:
            break
        upper = (seq_index // reach) % 2 == 1
        low, high = jnp.split(kept + other, 2, axis=1)
        kept, sent = jnp.where(upper, high, low), jnp.where(upper, low, high)
    part_width = kept.shape[1]
    outgoing = pl.pallas_call(
        spread_kernel,
        out_shape=shape((seq_count * groups, CAP, part_width), bf16),
        compiler_params=params(8),
        name="spread",
    )(kept, other)
    returned = lax.all_to_all(
        outgoing,
        ("seq", "exp"),
        split_axis=0,
        concat_axis=0,
        tiled=True,
    ).reshape(seq_count, groups, CAP, part_width)

    columns, _ = lax.optimization_barrier((columns, outgoing))
    residual, gates = pl.pallas_call(
        functools.partial(home_kernel, seq_count),
        out_shape=(shape((rows, width), f32), shape((rows, slots), f32)),
        scratch_shapes=[pltpu.VMEM((seq_count, rows, w_out.shape[0]), f32)],
        compiler_params=params(8),
        name="home",
    )(*columns, moe_row, router.T, select, chosen)

    return pl.pallas_call(
        final_kernel,
        out_shape=shape((requests, steps, width), bf16),
        scratch_shapes=[pltpu.VMEM((slots, width), f32)],
        compiler_params=params(8),
        name="final",
    )(gates, returned, residual)


def solution(mesh):
    in_specs = (
        P("exp", None, None),
        P(),
        P("seq", None),
        P(None, "exp", "seq", None),
        P(None, "exp", None, None),
        P("exp"),
        P("seq", None),
        P(),
        P(),
        P("exp", None, None),
        P("exp", None),
        P(None, "exp", "seq", None),
        P("exp", "seq", None),
    )
    out_specs = P("exp", None, None)
    return jax.shard_map(body, mesh=mesh, in_specs=in_specs, out_specs=out_specs, check_vma=False)
```

```python
import functools

import jax
import jax.numpy as jnp
from jax import lax
from jax.experimental import pallas as pl
from jax.experimental.pallas import tpu as pltpu
from jax.sharding import PartitionSpec as P

HEADS = 16
HD = 64
EXPERTS = 16
TOPK = 2
SINKS = 4
WIN = 4096
CAP = 8
LANES = 128
PIECES = 3
FIRST_KEYS = 2
SECOND_KEYS = 8
SECOND_VALUES = 3
CORES = 2
HALF_HEADS = HEADS // CORES
HALF = HALF_HEADS * HD
PACKED = HALF + LANES
HELD = 768
PIECE = 320
AHEAD = 10
BLOCK = 256
BLOCK_HEADS = BLOCK // HD

EPSILON = 1e-06
MASKED = -1e30
MIB = 1 << 20
ROWS_BY_ROWS = (((1,), (1,)), ((), ()))
ROWS_BY_COLS = (((1,), (0,)), ((), ()))


def dot(a, b, dims=ROWS_BY_COLS):
    return lax.dot_general(a, b, dims, preferred_element_type=jnp.float32)


def params(limit_mib=32):
    return pltpu.CompilerParams(vmem_limit_bytes=limit_mib * MIB)


def moving(count):
    return pl.CostEstimate(flops=0, bytes_accessed=count, transcendentals=0)


def in_hbm(value):
    return pltpu.with_memory_space_constraint(value, pltpu.HBM)


def split(value, count):
    parts = []
    for _ in range(count):
        part = value.astype(jnp.bfloat16)
        parts.append(part)
        value = value - part.astype(jnp.float32)
    return parts


def exact_dot(values, table):
    high, low = split(values, 2)
    both = dot(jnp.concatenate([high, low], axis=0), table)
    return both[: values.shape[0]] + both[values.shape[0] :]


def rms_rows(widened, gain_row):
    inverse = lax.rsqrt(jnp.mean(widened * widened, axis=-1, keepdims=True) + EPSILON)
    return (widened * inverse * gain_row).astype(jnp.bfloat16)


def copy_rows(source_ref, rows_ref):
    requests, steps, _ = source_ref.shape
    for r in range(requests):
        rows_ref[r * steps : (r + 1) * steps, :] = source_ref[r].astype(rows_ref.dtype)


def each(sems):
    return [sems.at[i] for i in range(sems.shape[0])]


def each(sems):
    return [sems.at[i] for i in range(sems.shape[0])]


def started(pairs, sems):
    copies = [pltpu.make_async_copy(*pair, sem) for pair, sem in zip(pairs, sems)]
    for copy in copies:
        copy.start()
    return copies


def unpack(packed):
    stats = packed[:, HALF:].astype(jnp.float32)

    def joined(first):
        return sum(
            stats[:, (first + i) * HALF_HEADS : (first + i + 1) * HALF_HEADS] for i in range(PIECES)
        )

    return joined(0), joined(PIECES), packed[:, :HALF].astype(jnp.float32)


def pack(peak, total, mixed):
    parts = [part.astype(jnp.float32) for part in split(peak, PIECES) + split(total, PIECES)]
    blank = jnp.zeros((peak.shape[0], LANES - 2 * PIECES * HALF_HEADS), jnp.float32)
    return jnp.concatenate([mixed] + parts + [blank], axis=1).astype(jnp.bfloat16)


def over_heads(factor):
    row = lax.broadcasted_iota(jnp.int32, (HALF_HEADS, HALF), 0)
    col = lax.broadcasted_iota(jnp.int32, (HALF_HEADS, HALF), 1) // HD
    expand = (row == col).astype(jnp.bfloat16)
    return sum(dot(part, expand) for part in split(factor, 2))


def merge(parts):
    overall = functools.reduce(jnp.maximum, [peak for peak, _, _ in parts])
    factors = [jnp.exp(peak - overall) for peak, _, _ in parts]
    total = sum(factor * part[1] for factor, part in zip(factors, parts))
    mixed = sum(over_heads(factor) * part[2] for factor, part in zip(factors, parts))
    return overall, total, mixed


def attend(parts):
    overall = functools.reduce(jnp.maximum, [peak for peak, _, _ in parts])
    factors = [jnp.exp(peak - overall) for peak, _, _ in parts]
    total = sum(factor * part[1] for factor, part in zip(factors, parts))
    inverse = jnp.where(total > 0, 1.0 / jnp.where(total > 0, total, 1.0), 0.0)
    return sum(over_heads(factor * inverse) * part[2] for factor, part in zip(factors, parts))


def route(ids_ref, order_ref, select_ref, chosen_ref):
    steps, _, requests = ids_ref.shape
    rows = requests * steps
    lane = lax.broadcasted_iota(jnp.int32, (rows, LANES), 1)
    own_row = lax.broadcasted_iota(jnp.int32, (rows, requests), 0)
    own_request = lax.broadcasted_iota(jnp.int32, (rows, requests), 1) == own_row // steps
    chosen = []
    for c in range(TOPK):
        ids = jnp.zeros((rows, requests), jnp.int32)
        for t in range(steps):
            ids = jnp.where(own_request & (own_row % steps == t), ids_ref[t, c : c + 1, :], ids)
        chosen.append(jnp.sum(ids.astype(jnp.float32), axis=1, keepdims=True).astype(jnp.int32))
    onehot = [(lane == ids).astype(jnp.float32) for ids in chosen]
    square_row = lax.broadcasted_iota(jnp.int32, (rows, rows), 0)
    square_col = lax.broadcasted_iota(jnp.int32, (rows, rows), 1)
    order_wide = jnp.broadcast_to(order_ref[...], (rows, rows))
    down = jnp.sum(
        jnp.where(square_row == square_col, order_wide, 0).astype(jnp.float32),
        axis=1,
        keepdims=True,
    )
    earlier = (order_wide.astype(jnp.float32) < down).astype(jnp.bfloat16)
    counts = dot(earlier, sum(onehot).astype(jnp.bfloat16))
    slot = lax.broadcasted_iota(jnp.int32, (rows, EXPERTS * CAP), 1)
    both = jnp.zeros((rows, EXPERTS * CAP), jnp.float32)
    for c in range(TOPK):
        position = jnp.sum(onehot[c] * counts, axis=-1, keepdims=True).astype(jnp.int32)
        column = chosen[c] * CAP + position
        select = ((column == slot) & (position < CAP)).astype(jnp.float32)
        select_ref[c] = select
        chosen_ref[c] = onehot[c]
        both = both + select
    return jnp.transpose(both)


def qkv_kernel(
    tokens_ref,
    gain_ref,
    weight_ref,
    window_ref,
    lengths_ref,
    out_ref,
    spans_ref,
    token_buf,
    gain_buf,
    weight_buf,
    rows_ref,
    numbers_ref,
    sems,
):
    copies = started(
        (
            (tokens_ref, token_buf),
            (gain_ref, gain_buf),
            (lengths_ref, numbers_ref),
            (weight_ref, weight_buf),
        ),
        each(sems),
    )
    for copy in copies[:3]:
        copy.wait()
    copy_rows(token_buf, rows_ref)
    normed = rms_rows(rows_ref[...], gain_buf[...])
    for r in range(spans_ref.shape[0]):
        spans_ref[r : r + 1, :] = jnp.full((1, LANES), numbers_ref[r], jnp.int32)
    copies[3].wait()
    out_ref[...] = dot(normed, weight_buf[...], ROWS_BY_ROWS).astype(jnp.bfloat16)


def in_order(sent_refs, ordered_ref):
    place = lax.axis_index("seq")
    for k, sent_ref in enumerate(sent_refs):
        ordered_ref[jnp.bitwise_xor(place, k)] = sent_ref[...]


def head_masks(rows, width, steps):
    row_head = lax.broadcasted_iota(jnp.int32, (rows, width), 0) // steps % BLOCK_HEADS
    col_head = lax.broadcasted_iota(jnp.int32, (rows, width), 1) // HD % BLOCK_HEADS
    return (row_head == col_head).astype(jnp.float32)


def fetch_expert_kernel(
    sent_ref,
    in_ref,
    ids_ref,
    order_ref,
    tokens_ref,
    held_ref,
    piece_ref,
    select_ref,
    chosen_ref,
    turned_ref,
    columns_ref,
    ids_buf,
    order_buf,
    tokens_buf,
    rows_ref,
    sems,
):
    pairs = [(ids_ref, ids_buf), (order_ref, order_buf), (tokens_ref, tokens_buf)]
    pairs += [
        (in_ref.at[p, 0, pl.ds(0, piece_ref.shape[1])], piece_ref.at[p]) for p in range(2)
    ]
    copies = started(pairs, each(sems))
    held_ref[...] = sent_ref[...]
    for copy in copies[:3]:
        copy.wait()
    turned_ref[...] = route(ids_buf, order_buf, select_ref, chosen_ref)
    copy_rows(tokens_buf, rows_ref)
    width, share = rows_ref.shape[1], columns_ref.shape[1]
    feature = lax.broadcasted_iota(jnp.int32, (width, share), 0)
    column = lax.broadcasted_iota(jnp.int32, (width, share), 1)
    own = (feature == column + lax.axis_index("seq") * share).astype(jnp.bfloat16)
    columns_ref[...] = dot(rows_ref[...].astype(jnp.bfloat16), own)
    for copy in copies[3:]:
        copy.wait()


def attention_kernel(*refs):
    *mixed_refs, spans_ref, window_ref = refs[:-5]
    keep_ref, send_ref, ordered_ref, flat_ref, result_ref = refs[-5:]
    devices, rows, share = ordered_ref.shape
    _, requests, span, width = window_ref.shape
    steps = rows // requests
    block_rows = BLOCK_HEADS * steps
    place = lax.axis_index("seq")
    in_order(mixed_refs, ordered_ref)
    for d in range(devices):
        if d * share < width:
            flat_ref[:, d * share : (d + 1) * share] = ordered_ref[d].astype(jnp.float32)
    own_head = head_masks(block_rows, width, steps)
    base = place * span
    scale = HD ** (-0.5)
    pair = 2 * steps
    tiles = HEADS * steps // pair
    slot = base + lax.broadcasted_iota(jnp.int32, (pair, span), 1)
    step = lax.broadcasted_iota(jnp.int32, (pair, span), 0) % steps
    stat_lane = lax.broadcasted_iota(jnp.int32, (HEADS * steps, LANES), 1)
    stat_head = lax.broadcasted_iota(jnp.int32, (HEADS * steps, LANES), 0) // steps
    cols = [slice(c, c + BLOCK) for c in range(0, width, BLOCK)]

    def score(r):
        keys = window_ref.at[0, r]
        queries = flat_ref[r * steps : (r + 1) * steps, 0:width]
        queries = (jnp.concatenate([queries] * BLOCK_HEADS, axis=0) * own_head).astype(jnp.bfloat16)
        return jnp.concatenate(
            [dot(queries[:, c], keys[:, c], ROWS_BY_ROWS) for c in cols], axis=0
        )

    scores = score(0)
    for r in range(requests):
        following = score(r + 1) if r + 1 < requests else None
        length = spans_ref[r : r + 1, 0:1]
        age = jnp.bitwise_and(slot - (length - SINKS), WIN - 1)
        live = ((slot < jnp.minimum(WIN, length - SINKS)) & (age > step))[None]
        scores = jnp.where(live, scores.reshape(tiles, pair, span) * scale, MASKED)
        peak = jnp.max(scores, axis=-1, keepdims=True)
        weight = jnp.where(live, jnp.exp(scores - peak), 0.0)
        total = jnp.sum(weight, axis=-1, keepdims=True)
        weight = weight.reshape(HEADS * steps, span).astype(jnp.bfloat16)
        values = window_ref.at[1, r]
        outs = []
        for b, c in enumerate(cols):
            own = slice(b * block_rows, (b + 1) * block_rows)
            mixed = dot(weight[own], values[:, c]) * own_head[:, c]
            mixed = sum(mixed[i : i + pair] for i in range(0, block_rows, pair))
            outs.append(mixed[:steps] + mixed[steps:])
        stats = jnp.where(stat_lane == stat_head, peak.reshape(HEADS * steps, 1), 0.0)
        stats = jnp.where(stat_lane == stat_head + HEADS, total.reshape(HEADS * steps, 1), stats)
        stats = jnp.sum(stats.reshape(tiles, pair, LANES), axis=0)
        outs.append(stats[:steps] + stats[steps:])
        result_ref[r * steps : (r + 1) * steps, :] = jnp.concatenate(outs, axis=1)
        scores = following
    halves = []
    for c in range(CORES):
        first = width + c * HALF_HEADS
        peak = result_ref[:, first : first + HALF_HEADS]
        total = result_ref[:, first + HEADS : first + HEADS + HALF_HEADS]
        halves.append(pack(peak, total, result_ref[:, c * HALF : (c + 1) * HALF]))
    odd = place % CORES == 1
    keep_ref[...] = jnp.where(odd, halves[1], halves[0])
    send_ref[...] = jnp.where(odd, halves[0], halves[1])


def extra_kernel(*refs):
    *mixed_refs, sinks_ref = refs[:-6]
    out_ref, stats_ref, ordered_ref, flat_ref, query_ref, keys_ref = refs[-6:]
    devices, rows, share = ordered_ref.shape
    _, requests, sinks, width = sinks_ref.shape
    steps = rows // requests
    block_rows = BLOCK_HEADS * steps
    count = sinks + steps
    in_order(mixed_refs, ordered_ref)
    for d in range(devices):
        flat_ref[:, d * share : (d + 1) * share] = ordered_ref[d].astype(jnp.float32)
    own_head = head_masks(block_rows, width, steps)
    for r in range(requests):
        own = slice(r * steps, (r + 1) * steps)
        queries = jnp.concatenate([flat_ref[own, 0:width]] * BLOCK_HEADS, axis=0) * own_head
        query_ref[r * block_rows : (r + 1) * block_rows, :] = queries
        for p in range(2):
            keys_ref[p, r * count : r * count + sinks] = sinks_ref[p, r].astype(jnp.float32)
            keys_ref[p, r * count + sinks : (r + 1) * count] = flat_ref[
                own, (p + 1) * width : (p + 2) * width
            ]
    all_rows = requests * block_rows
    all_keys = requests * count
    row = lax.broadcasted_iota(jnp.int32, (all_rows, all_keys), 0)
    key = lax.broadcasted_iota(jnp.int32, (all_rows, all_keys), 1)
    live = (row // block_rows == key // count) & (key % count - sinks <= row % steps)
    stat_lane = lax.broadcasted_iota(jnp.int32, (all_rows, LANES), 1)
    stat_head = lax.broadcasted_iota(jnp.int32, (all_rows, LANES), 0) % block_rows // steps
    whole_mask = jnp.concatenate([own_head[:, :BLOCK]] * requests, axis=0)
    stats = jnp.zeros((all_rows, LANES), jnp.float32)
    pair = 2 * steps

    def by_request(values):
        values = jnp.sum(values.reshape(requests, block_rows // pair, pair, values.shape[-1]), axis=1)
        return values[:, :steps] + values[:, steps:]

    for b in range(width // BLOCK):
        c = slice(b * BLOCK, (b + 1) * BLOCK)
        scores = dot(
            query_ref[:, c].astype(jnp.bfloat16), keys_ref[0, :, c].astype(jnp.bfloat16), ROWS_BY_ROWS
        )
        scores = jnp.where(live, scores * HD ** (-0.5), MASKED)
        peak = jnp.max(scores, axis=-1, keepdims=True)
        weight = jnp.where(live, jnp.exp(scores - peak), 0.0)
        total = jnp.sum(weight, axis=-1, keepdims=True)
        mixed = dot(weight.astype(jnp.bfloat16), keys_ref[1, :, c].astype(jnp.bfloat16))
        mixed = by_request(mixed * whole_mask)
        for r in range(requests):
            out_ref[r * steps : (r + 1) * steps, c] = mixed[r]
        stats = jnp.where(stat_lane == stat_head + b * BLOCK_HEADS, peak, stats)
        stats = jnp.where(stat_lane == stat_head + b * BLOCK_HEADS + HEADS, total, stats)
    stats = by_request(stats)
    for r in range(requests):
        stats_ref[r * steps : (r + 1) * steps, :] = stats[r]


def pair_kernel(keep_ref, other_ref, extra_ref, extra_stats_ref, out_ref):
    odd = lax.axis_index("seq") % CORES == 1
    first = lax.axis_index("seq") // CORES == 0

    def own_half(value, at, width):
        return jnp.where(odd, value[:, at + width : at + 2 * width], value[:, at : at + width])

    extra_peak = jnp.where(first, own_half(extra_stats_ref[...], 0, HALF_HEADS), MASKED)
    extra_total = jnp.where(first, own_half(extra_stats_ref[...], HEADS, HALF_HEADS), 0.0)
    extra = jnp.where(first, own_half(extra_ref[...], 0, HALF), 0.0)
    parts = [unpack(keep_ref[...]), unpack(other_ref[...]), (extra_peak, extra_total, extra)]
    out_ref[...] = pack(*merge(parts))


def project_kernel(*refs):
    *part_refs, weight_ref, other_weight_ref, columns_ref, turned_ref, out_ref, residual_ref = refs
    devices = lax.axis_size("seq")
    groups = lax.axis_size("exp")
    local_experts = EXPERTS // groups
    odd = lax.axis_index("seq") % CORES == 1
    attended = attend([unpack(part_ref[...]) for part_ref in part_refs]).astype(jnp.bfloat16)

    def project(weight):
        weight = jnp.where(odd, weight[:, HALF:], weight[:, :HALF])
        return dot(attended, weight, ROWS_BY_ROWS)

    mine = project(weight_ref[...]) + columns_ref[...]
    others = project(other_weight_ref[...])
    residual = jnp.concatenate(
        [jnp.where(odd, others, mine), jnp.where(odd, mine, others)], axis=1
    )
    residual_ref[...] = residual
    table = dot(turned_ref[...].astype(jnp.bfloat16), residual.astype(jnp.bfloat16))
    for s in range(devices):
        for x in range(groups):
            row = (x * local_experts + s // (devices // local_experts)) * CAP
            out_ref[s * groups + x] = table[row : row + CAP].astype(jnp.bfloat16)


def home_kernel(devices, *refs):
    residual_refs, refs = refs[:devices], refs[devices:]
    gain_ref, router_ref, select_ref, chosen_ref, residual_ref, gates_ref, ordered_ref = refs
    in_order(residual_refs, ordered_ref)
    residual = jnp.concatenate(
        [ordered_ref[d] + ordered_ref[d + 1] for d in range(0, devices, CORES)], axis=1
    )
    residual_ref[...] = residual
    normed = rms_rows(residual, gain_ref[...])
    logits = dot(normed, router_ref[...], ROWS_BY_ROWS)
    gates = jnp.zeros(select_ref.shape[1:], jnp.float32)
    for c in range(TOPK):
        logit = jnp.sum(chosen_ref[c][:, :EXPERTS] * logits, axis=-1, keepdims=True)
        gates = gates + jax.nn.sigmoid(logit) * select_ref[c]
    gates_ref[...] = gates


def expert_kernel(
    received_ref, gain_ref, piece_ref, in_ref, down_ref, keep_ref, send_ref, in_buf, down_buf, sems
):
    hidden_units, width = down_buf.shape
    held = piece_ref.shape[1]
    pieces = [(at, min(PIECE, hidden_units - at)) for at in range(held, hidden_units, PIECE)]
    downs = [(0, held)] + pieces
    stages = []
    for at, count in pieces:
        stages.append(
            [
                (in_ref.at[p, 0, pl.ds(at, count)], in_buf.at[p, pl.ds(at - held, count)])
                for p in range(2)
            ]
        )
    for at, count in downs:
        stages.append([(down_ref.at[0, pl.ds(at, count)], down_buf.at[pl.ds(at, count)])])
    flying = []

    def start_next():
        if len(flying) < len(stages):
            first = sum(len(stage) for stage in stages[: len(flying)])
            flying.append(started(stages[len(flying)], [sems.at[first + i] for i in range(len(stages[len(flying)]))]))

    def wait_for(stage):
        for copy in flying[stage]:
            copy.wait()
        start_next()

    for _ in range(AHEAD):
        start_next()
    devices = lax.axis_size("seq")
    groups = lax.axis_size("exp")
    columns = []
    for s in range(0, devices, CORES):
        pieces_of_chip = [
            jnp.concatenate(
                [received_ref[d * groups + g].astype(jnp.float32) for g in range(groups)], axis=0
            )
            for d in range(s, s + CORES)
        ]
        columns.append(sum(pieces_of_chip))
    rows = rms_rows(jnp.concatenate(columns, axis=1), gain_ref[...])

    def layer(gate_weight, up_weight):
        gate = dot(rows, gate_weight, ROWS_BY_ROWS)
        up = dot(rows, up_weight, ROWS_BY_ROWS)
        return (jax.nn.gelu(gate, approximate=True) * up).astype(jnp.bfloat16)

    hidden = [layer(piece_ref[0], piece_ref[1])]
    for i, (at, count) in enumerate(pieces):
        wait_for(i)
        own = slice(at - held, at - held + count)
        hidden.append(layer(in_buf[0, own], in_buf[1, own]))
    outputs = jnp.zeros((groups * CAP, width), jnp.float32)
    for i, (at, count) in enumerate(downs):
        wait_for(len(pieces) + i)
        outputs = outputs + dot(hidden[i], down_buf[at : at + count])
    half = width // 2
    odd = lax.axis_index("seq") % 2 == 1
    keep_ref[...] = jnp.where(odd, outputs[:, half:], outputs[:, :half])
    send_ref[...] = jnp.where(odd, outputs[:, :half], outputs[:, half:])


def spread_kernel(kept_ref, other_ref, out_ref):
    slots = out_ref.shape[1]
    groups = kept_ref.shape[0] // slots
    outputs = kept_ref[...] + other_ref[...]
    for block in range(out_ref.shape[0]):
        first = block % groups * slots
        out_ref[block] = outputs[first : first + slots].astype(jnp.bfloat16)


def column_block(sharer, sharers):
    block = 0
    while sharers > 1:
        sharers //= 2
        block += (sharer & 1) * sharers
        sharer >>= 1
    return block


def final_kernel(gates_ref, returned_ref, residual_ref, out_ref, table_ref):
    requests, steps, width = out_ref.shape
    devices, groups, slots, part = returned_ref.shape
    local_experts = EXPERTS // groups
    sharers = devices // local_experts
    for s in range(devices):
        first = column_block(s % sharers, sharers) * part
        for x in range(groups):
            row = (x * local_experts + s // sharers) * slots
            table_ref[row : row + slots, first : first + part] = returned_ref[s, x].astype(jnp.float32)
    table = table_ref[...].astype(jnp.bfloat16)
    moe = exact_dot(gates_ref[...], table)
    total = residual_ref[...] + moe
    for r in range(requests):
        out_ref[r] = total[r * steps : (r + 1) * steps].astype(jnp.bfloat16)


def exchange(value, bits):
    return lax.ppermute(value, "seq", [(i, i ^ bits) for i in range(lax.axis_size("seq"))])


def from_chips(values, meanwhile=None):
    others = [exchange(values, k) for k in range(2, lax.axis_size("seq"), 2)]
    if meanwhile is not None:
        values = meanwhile(values)
    return [values] + others


def gather_seq(values, meanwhile=None):
    near = from_chips(values, meanwhile)
    return [part for value in near for part in (value, exchange(value, 1))]


def shape(dims, dtype):
    return jax.ShapeDtypeStruct(dims, dtype)


def body(
    tokens,
    attn_gain,
    w_qkv,
    window_cache,
    sink_cache,
    lengths,
    w_out,
    moe_gain,
    router,
    expert_ids,
    slot_order,
    expert_in,
    expert_down,
):
    requests, steps, width = tokens.shape
    rows = requests * steps
    seq_index = lax.axis_index("seq")
    seq_count = lax.axis_size("seq")
    groups = lax.axis_size("exp")
    local_experts = EXPERTS // groups
    sharers = seq_count // local_experts
    span = window_cache.shape[2]
    share = w_qkv.shape[0]
    slots = EXPERTS * CAP
    f32, bf16 = jnp.float32, jnp.bfloat16

    vmem = pl.BlockSpec(memory_space=pltpu.VMEM)
    hbm = pl.BlockSpec(memory_space=pltpu.HBM)

    gain_row = attn_gain.reshape(1, width)
    local_mix, spans = pl.pallas_call(
        qkv_kernel,
        in_specs=[hbm] * 5,
        out_shape=(shape((rows, share), bf16), shape((requests, LANES), jnp.int32)),
        scratch_shapes=[
            pltpu.VMEM(tokens.shape, bf16),
            pltpu.VMEM(gain_row.shape, f32),
            pltpu.VMEM(w_qkv.shape, bf16),
            pltpu.VMEM((rows, width), f32),
            pltpu.SMEM((requests,), jnp.int32),
            pltpu.SemaphoreType.DMA((4,)),
        ],
        compiler_params=params(4),
        name="qkv",
    )(in_hbm(tokens), in_hbm(gain_row), in_hbm(w_qkv), in_hbm(window_cache), in_hbm(lengths))

    mixed = gather_seq(local_mix)

    padded = width + LANES
    kept, sent = pl.pallas_call(
        attention_kernel,
        in_specs=[vmem] * (seq_count + 2),
        out_shape=(shape((rows, PACKED), bf16), shape((rows, PACKED), bf16)),
        scratch_shapes=[
            pltpu.VMEM((seq_count, rows, share), bf16),
            pltpu.VMEM((rows, padded), f32),
            pltpu.VMEM((rows, padded), f32),
        ],
        compiler_params=params(8),
        name="attention",
    )(*mixed, spans, window_cache)
    other = exchange(sent, 1)

    extra, extra_stats = pl.pallas_call(
        extra_kernel,
        out_shape=(shape((rows, width), f32), shape((rows, LANES), f32)),
        scratch_shapes=[
            pltpu.VMEM((seq_count, rows, share), bf16),
            pltpu.VMEM((rows, 3 * width), f32),
            pltpu.VMEM((rows * BLOCK_HEADS, width), f32),
            pltpu.VMEM((2, requests * (SINKS + steps), width), f32),
        ],
        compiler_params=params(8),
        name="extra",
    )(*mixed, sink_cache)

    part = pl.pallas_call(
        pair_kernel,
        out_shape=shape((rows, PACKED), bf16),
        compiler_params=params(8),
        name="pair",
    )(kept, other, extra, extra_stats)

    hidden_units = expert_down.shape[1]
    held_units = min(HELD, hidden_units)
    late_units = max(hidden_units - held_units, 16)

    fetched = []

    def fetch_expert(values):
        held, *outputs = pl.pallas_call(
            fetch_expert_kernel,
            in_specs=[vmem] + [hbm] * 4,
            out_shape=(
                shape(values.shape, bf16),
                shape((2, held_units, width), bf16),
                shape((TOPK, rows, slots), f32),
                shape((TOPK, rows, LANES), f32),
                shape((slots, rows), f32),
                shape((rows, w_out.shape[0]), f32),
            ),
            scratch_shapes=[
                pltpu.VMEM((steps, TOPK, requests), jnp.int32),
                pltpu.VMEM(slot_order.shape, jnp.int32),
                pltpu.VMEM(tokens.shape, bf16),
                pltpu.VMEM((rows, width), f32),
                pltpu.SemaphoreType.DMA((5,)),
            ],
            compiler_params=params(8),
            cost_estimate=moving(4 * held_units * width),
            name="fetch_expert",
        )(
            values,
            in_hbm(expert_in),
            in_hbm(expert_ids.transpose(1, 2, 0)),
            in_hbm(slot_order),
            in_hbm(tokens),
        )
        fetched.extend(outputs)
        return held

    parts = from_chips(part, fetch_expert)
    other_weight = exchange(lax.optimization_barrier((w_out, part))[0], 1)
    piece, select, chosen, turned, token_columns = fetched

    outgoing, residual_columns = pl.pallas_call(
        project_kernel,
        out_shape=(
            shape((seq_count * groups, CAP, CORES * w_out.shape[0]), bf16),
            shape((rows, CORES * w_out.shape[0]), f32),
        ),
        compiler_params=params(16),
        name="project",
    )(*parts, w_out, other_weight, token_columns, turned)
    received = lax.all_to_all(outgoing, ("seq", "exp"), split_axis=0, concat_axis=0, tiled=True)
    columns = gather_seq(residual_columns)

    moe_row = moe_gain.reshape(1, width)
    kept, sent = pl.pallas_call(
        expert_kernel,
        in_specs=[vmem, vmem, vmem, hbm, hbm],
        out_shape=(
            shape((groups * CAP, width // 2), f32),
            shape((groups * CAP, width // 2), f32),
        ),
        scratch_shapes=[
            pltpu.VMEM((2, late_units, width), bf16),
            pltpu.VMEM((hidden_units, width), bf16),
            pltpu.SemaphoreType.DMA((3 * pl.cdiv(late_units, PIECE) + 1,)),
        ],
        compiler_params=params(20),
        name="expert",
    )(received, moe_row, piece, in_hbm(expert_in), in_hbm(expert_down))

    reach = 1
    while True:
        other = lax.ppermute(sent, "seq", [(i, i ^ reach) for i in range(seq_count)])
        reach *= 2
        if reach >= sharers:
            break
        upper = (seq_index // reach) % 2 == 1
        low, high = jnp.split(kept + other, 2, axis=1)
        kept, sent = jnp.where(upper, high, low), jnp.where(upper, low, high)
    part_width = kept.shape[1]
    outgoing = pl.pallas_call(
        spread_kernel,
        out_shape=shape((seq_count * groups, CAP, part_width), bf16),
        compiler_params=params(8),
        name="spread",
    )(kept, other)
    returned = lax.all_to_all(
        outgoing,
        ("seq", "exp"),
        split_axis=0,
        concat_axis=0,
        tiled=True,
    ).reshape(seq_count, groups, CAP, part_width)

    columns, _ = lax.optimization_barrier((columns, outgoing))
    residual, gates = pl.pallas_call(
        functools.partial(home_kernel, seq_count),
        out_shape=(shape((rows, width), f32), shape((rows, slots), f32)),
        scratch_shapes=[pltpu.VMEM((seq_count, rows, CORES * w_out.shape[0]), f32)],
        compiler_params=params(8),
        name="home",
    )(*columns, moe_row, router.T, select, chosen)

    return pl.pallas_call(
        final_kernel,
        out_shape=shape((requests, steps, width), bf16),
        scratch_shapes=[pltpu.VMEM((slots, width), f32)],
        compiler_params=params(8),
        name="final",
    )(gates, returned, residual)


def solution(mesh):
    in_specs = (
        P("exp", None, None),
        P(),
        P("seq", None),
        P(None, "exp", "seq", None),
        P(None, "exp", None, None),
        P("exp"),
        P("seq", None),
        P(),
        P(),
        P("exp", None, None),
        P("exp", None),
        P(None, "exp", "seq", None),
        P("exp", "seq", None),
    )
    out_specs = P("exp", None, None)
    return jax.shard_map(body, mesh=mesh, in_specs=in_specs, out_specs=out_specs, check_vma=False)
```

```python
import functools

import jax
import jax.numpy as jnp
from jax import lax
from jax.experimental import pallas as pl
from jax.experimental.pallas import tpu as pltpu
from jax.sharding import PartitionSpec as P

HEADS = 16
HD = 64
EXPERTS = 16
TOPK = 2
SINKS = 4
WIN = 4096
CAP = 8
LANES = 128
PIECES = 3
FIRST_KEYS = 2
SECOND_KEYS = 8
SECOND_VALUES = 3
CORES = 2
HALF_HEADS = HEADS // CORES
HALF = HALF_HEADS * HD
PACKED = HALF + LANES
HELD = 768
PIECE = 320
AHEAD = 10
BLOCK = 256
BLOCK_HEADS = BLOCK // HD

EPSILON = 1e-06
MASKED = -1e30
MIB = 1 << 20
ROWS_BY_ROWS = (((1,), (1,)), ((), ()))
ROWS_BY_COLS = (((1,), (0,)), ((), ()))


def dot(a, b, dims=ROWS_BY_COLS):
    return lax.dot_general(a, b, dims, preferred_element_type=jnp.float32)


def params(limit_mib=32):
    return pltpu.CompilerParams(vmem_limit_bytes=limit_mib * MIB)


def moving(count):
    return pl.CostEstimate(flops=0, bytes_accessed=count, transcendentals=0)


def in_hbm(value):
    return pltpu.with_memory_space_constraint(value, pltpu.HBM)


def split(value, count):
    parts = []
    for _ in range(count):
        part = value.astype(jnp.bfloat16)
        parts.append(part)
        value = value - part.astype(jnp.float32)
    return parts


def exact_dot(values, table):
    high, low = split(values, 2)
    both = dot(jnp.concatenate([high, low], axis=0), table)
    return both[: values.shape[0]] + both[values.shape[0] :]


def rms_rows(widened, gain_row):
    inverse = lax.rsqrt(jnp.mean(widened * widened, axis=-1, keepdims=True) + EPSILON)
    return (widened * inverse * gain_row).astype(jnp.bfloat16)


def copy_rows(source_ref, rows_ref):
    requests, steps, _ = source_ref.shape
    for r in range(requests):
        rows_ref[r * steps : (r + 1) * steps, :] = source_ref[r].astype(rows_ref.dtype)


def each(sems):
    return [sems.at[i] for i in range(sems.shape[0])]


def each(sems):
    return [sems.at[i] for i in range(sems.shape[0])]


def started(pairs, sems):
    copies = [pltpu.make_async_copy(*pair, sem) for pair, sem in zip(pairs, sems)]
    for copy in copies:
        copy.start()
    return copies


def unpack(packed):
    stats = packed[:, HALF:].astype(jnp.float32)

    def joined(first):
        return sum(
            stats[:, (first + i) * HALF_HEADS : (first + i + 1) * HALF_HEADS] for i in range(PIECES)
        )

    return joined(0), joined(PIECES), packed[:, :HALF].astype(jnp.float32)


def pack(peak, total, mixed):
    parts = [part.astype(jnp.float32) for part in split(peak, PIECES) + split(total, PIECES)]
    blank = jnp.zeros((peak.shape[0], LANES - 2 * PIECES * HALF_HEADS), jnp.float32)
    return jnp.concatenate([mixed] + parts + [blank], axis=1).astype(jnp.bfloat16)


def over_heads(factor):
    row = lax.broadcasted_iota(jnp.int32, (HALF_HEADS, HALF), 0)
    col = lax.broadcasted_iota(jnp.int32, (HALF_HEADS, HALF), 1) // HD
    expand = (row == col).astype(jnp.bfloat16)
    return sum(dot(part, expand) for part in split(factor, 2))


def merge(parts):
    overall = functools.reduce(jnp.maximum, [peak for peak, _, _ in parts])
    factors = [jnp.exp(peak - overall) for peak, _, _ in parts]
    total = sum(factor * part[1] for factor, part in zip(factors, parts))
    mixed = sum(over_heads(factor) * part[2] for factor, part in zip(factors, parts))
    return overall, total, mixed


def attend(parts):
    overall = functools.reduce(jnp.maximum, [peak for peak, _, _ in parts])
    factors = [jnp.exp(peak - overall) for peak, _, _ in parts]
    total = sum(factor * part[1] for factor, part in zip(factors, parts))
    inverse = jnp.where(total > 0, 1.0 / jnp.where(total > 0, total, 1.0), 0.0)
    return sum(over_heads(factor * inverse) * part[2] for factor, part in zip(factors, parts))


def route(ids_ref, order_ref, select_ref, chosen_ref):
    steps, _, requests = ids_ref.shape
    rows = requests * steps
    lane = lax.broadcasted_iota(jnp.int32, (rows, LANES), 1)
    own_row = lax.broadcasted_iota(jnp.int32, (rows, requests), 0)
    own_request = lax.broadcasted_iota(jnp.int32, (rows, requests), 1) == own_row // steps
    chosen = []
    for c in range(TOPK):
        ids = jnp.zeros((rows, requests), jnp.int32)
        for t in range(steps):
            ids = jnp.where(own_request & (own_row % steps == t), ids_ref[t, c : c + 1, :], ids)
        chosen.append(jnp.sum(ids.astype(jnp.float32), axis=1, keepdims=True).astype(jnp.int32))
    onehot = [(lane == ids).astype(jnp.float32) for ids in chosen]
    square_row = lax.broadcasted_iota(jnp.int32, (rows, rows), 0)
    square_col = lax.broadcasted_iota(jnp.int32, (rows, rows), 1)
    order_wide = jnp.broadcast_to(order_ref[...], (rows, rows))
    down = jnp.sum(
        jnp.where(square_row == square_col, order_wide, 0).astype(jnp.float32),
        axis=1,
        keepdims=True,
    )
    earlier = (order_wide.astype(jnp.float32) < down).astype(jnp.bfloat16)
    counts = dot(earlier, sum(onehot).astype(jnp.bfloat16))
    slot = lax.broadcasted_iota(jnp.int32, (rows, EXPERTS * CAP), 1)
    both = jnp.zeros((rows, EXPERTS * CAP), jnp.float32)
    for c in range(TOPK):
        position = jnp.sum(onehot[c] * counts, axis=-1, keepdims=True).astype(jnp.int32)
        column = chosen[c] * CAP + position
        select = ((column == slot) & (position < CAP)).astype(jnp.float32)
        select_ref[c] = select
        chosen_ref[c] = onehot[c]
        both = both + select
    return jnp.transpose(both)


def qkv_kernel(
    tokens_ref,
    gain_ref,
    weight_ref,
    window_ref,
    lengths_ref,
    out_ref,
    spans_ref,
    token_buf,
    gain_buf,
    weight_buf,
    rows_ref,
    numbers_ref,
    sems,
):
    copies = started(
        (
            (tokens_ref, token_buf),
            (gain_ref, gain_buf),
            (lengths_ref, numbers_ref),
            (weight_ref, weight_buf),
        ),
        each(sems),
    )
    for copy in copies[:3]:
        copy.wait()
    copy_rows(token_buf, rows_ref)
    normed = rms_rows(rows_ref[...], gain_buf[...])
    for r in range(spans_ref.shape[0]):
        spans_ref[r : r + 1, :] = jnp.full((1, LANES), numbers_ref[r], jnp.int32)
    copies[3].wait()
    out_ref[...] = dot(normed, weight_buf[...], ROWS_BY_ROWS).astype(jnp.bfloat16)


def in_order(sent_refs, ordered_ref):
    place = lax.axis_index("seq")
    for k, sent_ref in enumerate(sent_refs):
        ordered_ref[jnp.bitwise_xor(place, k)] = sent_ref[...]


def head_masks(rows, width, steps):
    row_head = lax.broadcasted_iota(jnp.int32, (rows, width), 0) // steps % BLOCK_HEADS
    col_head = lax.broadcasted_iota(jnp.int32, (rows, width), 1) // HD % BLOCK_HEADS
    return (row_head == col_head).astype(jnp.float32)


def fetch_expert_kernel(
    sent_ref,
    in_ref,
    ids_ref,
    order_ref,
    tokens_ref,
    held_ref,
    piece_ref,
    select_ref,
    chosen_ref,
    turned_ref,
    columns_ref,
    ids_buf,
    order_buf,
    tokens_buf,
    rows_ref,
    sems,
):
    pairs = [(ids_ref, ids_buf), (order_ref, order_buf), (tokens_ref, tokens_buf)]
    pairs += [
        (in_ref.at[p, 0, pl.ds(0, piece_ref.shape[1])], piece_ref.at[p]) for p in range(2)
    ]
    copies = started(pairs, each(sems))
    held_ref[...] = sent_ref[...]
    for copy in copies[:3]:
        copy.wait()
    turned_ref[...] = route(ids_buf, order_buf, select_ref, chosen_ref)
    copy_rows(tokens_buf, rows_ref)
    width, share = rows_ref.shape[1], columns_ref.shape[1]
    feature = lax.broadcasted_iota(jnp.int32, (width, share), 0)
    column = lax.broadcasted_iota(jnp.int32, (width, share), 1)
    own = (feature == column + lax.axis_index("seq") * share).astype(jnp.bfloat16)
    columns_ref[...] = dot(rows_ref[...].astype(jnp.bfloat16), own)
    for copy in copies[3:]:
        copy.wait()


def attention_kernel(of_own, *refs):
    *mixed_refs, spans_ref, window_ref = refs[:-4]
    out_ref, ordered_ref, flat_ref, result_ref = refs[-4:]
    devices, rows, share = ordered_ref.shape
    _, requests, span, width = window_ref.shape
    steps = rows // requests
    block_rows = BLOCK_HEADS * steps
    place = lax.axis_index("seq")
    in_order(mixed_refs, ordered_ref)
    for d in range(devices):
        if d * share < width:
            flat_ref[:, d * share : (d + 1) * share] = ordered_ref[d].astype(jnp.float32)
    own_head = head_masks(block_rows, HALF, steps)
    half = place % CORES if of_own else 1 - place % CORES
    heads = pl.ds(pl.multiple_of(half * HALF, HALF), HALF)
    base = place * span
    scale = HD ** (-0.5)
    pair = 2 * steps
    tiles = HALF_HEADS * steps // pair
    slot = base + lax.broadcasted_iota(jnp.int32, (pair, span), 1)
    step = lax.broadcasted_iota(jnp.int32, (pair, span), 0) % steps
    stat_lane = lax.broadcasted_iota(jnp.int32, (HALF_HEADS * steps, LANES), 1)
    stat_head = lax.broadcasted_iota(jnp.int32, (HALF_HEADS * steps, LANES), 0) // steps
    cols = [slice(c, c + BLOCK) for c in range(0, HALF, BLOCK)]

    def score(r):
        keys = window_ref[0, r, :, heads]
        queries = flat_ref[r * steps : (r + 1) * steps, heads]
        queries = (jnp.concatenate([queries] * BLOCK_HEADS, axis=0) * own_head).astype(jnp.bfloat16)
        return jnp.concatenate(
            [dot(queries[:, c], keys[:, c], ROWS_BY_ROWS) for c in cols], axis=0
        )

    scores = score(0)
    for r in range(requests):
        following = score(r + 1) if r + 1 < requests else None
        length = spans_ref[r : r + 1, 0:1]
        age = jnp.bitwise_and(slot - (length - SINKS), WIN - 1)
        live = ((slot < jnp.minimum(WIN, length - SINKS)) & (age > step))[None]
        scores = jnp.where(live, scores.reshape(tiles, pair, span) * scale, MASKED)
        peak = jnp.max(scores, axis=-1, keepdims=True)
        weight = jnp.where(live, jnp.exp(scores - peak), 0.0)
        total = jnp.sum(weight, axis=-1, keepdims=True)
        weight = weight.reshape(HALF_HEADS * steps, span).astype(jnp.bfloat16)
        values = window_ref[1, r, :, heads]
        outs = []
        for b, c in enumerate(cols):
            own = slice(b * block_rows, (b + 1) * block_rows)
            mixed = dot(weight[own], values[:, c]) * own_head[:, c]
            mixed = sum(mixed[i : i + pair] for i in range(0, block_rows, pair))
            outs.append(mixed[:steps] + mixed[steps:])
        stats = jnp.where(stat_lane == stat_head, peak.reshape(HALF_HEADS * steps, 1), 0.0)
        stats = jnp.where(stat_lane == stat_head + HALF_HEADS, total.reshape(HALF_HEADS * steps, 1), stats)
        stats = jnp.sum(stats.reshape(tiles, pair, LANES), axis=0)
        outs.append(stats[:steps] + stats[steps:])
        result_ref[r * steps : (r + 1) * steps, :] = jnp.concatenate(outs, axis=1)
        scores = following
    peak = result_ref[:, HALF : HALF + HALF_HEADS]
    total = result_ref[:, HALF + HALF_HEADS : HALF + 2 * HALF_HEADS]
    out_ref[...] = pack(peak, total, result_ref[:, :HALF])


def extra_kernel(*refs):
    *mixed_refs, sinks_ref = refs[:-6]
    out_ref, stats_ref, ordered_ref, flat_ref, query_ref, keys_ref = refs[-6:]
    devices, rows, share = ordered_ref.shape
    _, requests, sinks, width = sinks_ref.shape
    steps = rows // requests
    block_rows = BLOCK_HEADS * steps
    count = sinks + steps
    in_order(mixed_refs, ordered_ref)
    for d in range(devices):
        flat_ref[:, d * share : (d + 1) * share] = ordered_ref[d].astype(jnp.float32)
    own_head = head_masks(block_rows, width, steps)
    for r in range(requests):
        own = slice(r * steps, (r + 1) * steps)
        queries = jnp.concatenate([flat_ref[own, 0:width]] * BLOCK_HEADS, axis=0) * own_head
        query_ref[r * block_rows : (r + 1) * block_rows, :] = queries
        for p in range(2):
            keys_ref[p, r * count : r * count + sinks] = sinks_ref[p, r].astype(jnp.float32)
            keys_ref[p, r * count + sinks : (r + 1) * count] = flat_ref[
                own, (p + 1) * width : (p + 2) * width
            ]
    all_rows = requests * block_rows
    all_keys = requests * count
    row = lax.broadcasted_iota(jnp.int32, (all_rows, all_keys), 0)
    key = lax.broadcasted_iota(jnp.int32, (all_rows, all_keys), 1)
    live = (row // block_rows == key // count) & (key % count - sinks <= row % steps)
    stat_lane = lax.broadcasted_iota(jnp.int32, (all_rows, LANES), 1)
    stat_head = lax.broadcasted_iota(jnp.int32, (all_rows, LANES), 0) % block_rows // steps
    whole_mask = jnp.concatenate([own_head[:, :BLOCK]] * requests, axis=0)
    stats = jnp.zeros((all_rows, LANES), jnp.float32)
    pair = 2 * steps

    def by_request(values):
        values = jnp.sum(values.reshape(requests, block_rows // pair, pair, values.shape[-1]), axis=1)
        return values[:, :steps] + values[:, steps:]

    for b in range(width // BLOCK):
        c = slice(b * BLOCK, (b + 1) * BLOCK)
        scores = dot(
            query_ref[:, c].astype(jnp.bfloat16), keys_ref[0, :, c].astype(jnp.bfloat16), ROWS_BY_ROWS
        )
        scores = jnp.where(live, scores * HD ** (-0.5), MASKED)
        peak = jnp.max(scores, axis=-1, keepdims=True)
        weight = jnp.where(live, jnp.exp(scores - peak), 0.0)
        total = jnp.sum(weight, axis=-1, keepdims=True)
        mixed = dot(weight.astype(jnp.bfloat16), keys_ref[1, :, c].astype(jnp.bfloat16))
        mixed = by_request(mixed * whole_mask)
        for r in range(requests):
            out_ref[r * steps : (r + 1) * steps, c] = mixed[r]
        stats = jnp.where(stat_lane == stat_head + b * BLOCK_HEADS, peak, stats)
        stats = jnp.where(stat_lane == stat_head + b * BLOCK_HEADS + HEADS, total, stats)
    stats = by_request(stats)
    for r in range(requests):
        stats_ref[r * steps : (r + 1) * steps, :] = stats[r]


def pair_kernel(keep_ref, other_ref, out_ref):
    out_ref[...] = pack(*merge([unpack(keep_ref[...]), unpack(other_ref[...])]))


def project_kernel(*refs):
    *part_refs, extra_ref, extra_stats_ref, weight_ref, other_weight_ref, columns_ref = refs[:-3]
    turned_ref, out_ref, residual_ref = refs[-3:]
    devices = lax.axis_size("seq")
    groups = lax.axis_size("exp")
    local_experts = EXPERTS // groups
    odd = lax.axis_index("seq") % CORES == 1

    def own_half(value, at, width):
        return jnp.where(odd, value[:, at + width : at + 2 * width], value[:, at : at + width])

    parts = [unpack(part_ref[...]) for part_ref in part_refs]
    parts.append(
        (
            own_half(extra_stats_ref[...], 0, HALF_HEADS),
            own_half(extra_stats_ref[...], HEADS, HALF_HEADS),
            own_half(extra_ref[...], 0, HALF),
        )
    )
    attended = attend(parts).astype(jnp.bfloat16)

    def project(weight):
        weight = jnp.where(odd, weight[:, HALF:], weight[:, :HALF])
        return dot(attended, weight, ROWS_BY_ROWS)

    mine = project(weight_ref[...]) + columns_ref[...]
    others = project(other_weight_ref[...])
    residual = jnp.concatenate(
        [jnp.where(odd, others, mine), jnp.where(odd, mine, others)], axis=1
    )
    residual_ref[...] = residual
    table = dot(turned_ref[...].astype(jnp.bfloat16), residual.astype(jnp.bfloat16))
    for s in range(devices):
        for x in range(groups):
            row = (x * local_experts + s // (devices // local_experts)) * CAP
            out_ref[s * groups + x] = table[row : row + CAP].astype(jnp.bfloat16)


def home_kernel(devices, *refs):
    residual_refs, refs = refs[:devices], refs[devices:]
    gain_ref, router_ref, select_ref, chosen_ref, residual_ref, gates_ref, ordered_ref = refs
    in_order(residual_refs, ordered_ref)
    residual = jnp.concatenate(
        [ordered_ref[d] + ordered_ref[d + 1] for d in range(0, devices, CORES)], axis=1
    )
    residual_ref[...] = residual
    normed = rms_rows(residual, gain_ref[...])
    logits = dot(normed, router_ref[...], ROWS_BY_ROWS)
    gates = jnp.zeros(select_ref.shape[1:], jnp.float32)
    for c in range(TOPK):
        logit = jnp.sum(chosen_ref[c][:, :EXPERTS] * logits, axis=-1, keepdims=True)
        gates = gates + jax.nn.sigmoid(logit) * select_ref[c]
    gates_ref[...] = gates


def expert_kernel(
    received_ref, gain_ref, piece_ref, in_ref, down_ref, keep_ref, send_ref, in_buf, down_buf, sems
):
    hidden_units, width = down_buf.shape
    held = piece_ref.shape[1]
    pieces = [(at, min(PIECE, hidden_units - at)) for at in range(held, hidden_units, PIECE)]
    downs = [(0, held)] + pieces
    stages = []
    for at, count in pieces:
        stages.append(
            [
                (in_ref.at[p, 0, pl.ds(at, count)], in_buf.at[p, pl.ds(at - held, count)])
                for p in range(2)
            ]
        )
    for at, count in downs:
        stages.append([(down_ref.at[0, pl.ds(at, count)], down_buf.at[pl.ds(at, count)])])
    flying = []

    def start_next():
        if len(flying) < len(stages):
            first = sum(len(stage) for stage in stages[: len(flying)])
            flying.append(started(stages[len(flying)], [sems.at[first + i] for i in range(len(stages[len(flying)]))]))

    def wait_for(stage):
        for copy in flying[stage]:
            copy.wait()
        start_next()

    for _ in range(AHEAD):
        start_next()
    devices = lax.axis_size("seq")
    groups = lax.axis_size("exp")
    columns = []
    for s in range(0, devices, CORES):
        pieces_of_chip = [
            jnp.concatenate(
                [received_ref[d * groups + g].astype(jnp.float32) for g in range(groups)], axis=0
            )
            for d in range(s, s + CORES)
        ]
        columns.append(sum(pieces_of_chip))
    rows = rms_rows(jnp.concatenate(columns, axis=1), gain_ref[...])

    def layer(gate_weight, up_weight):
        gate = dot(rows, gate_weight, ROWS_BY_ROWS)
        up = dot(rows, up_weight, ROWS_BY_ROWS)
        return (jax.nn.gelu(gate, approximate=True) * up).astype(jnp.bfloat16)

    hidden = [layer(piece_ref[0], piece_ref[1])]
    for i, (at, count) in enumerate(pieces):
        wait_for(i)
        own = slice(at - held, at - held + count)
        hidden.append(layer(in_buf[0, own], in_buf[1, own]))
    outputs = jnp.zeros((groups * CAP, width), jnp.float32)
    for i, (at, count) in enumerate(downs):
        wait_for(len(pieces) + i)
        outputs = outputs + dot(hidden[i], down_buf[at : at + count])
    half = width // 2
    odd = lax.axis_index("seq") % 2 == 1
    keep_ref[...] = jnp.where(odd, outputs[:, half:], outputs[:, :half])
    send_ref[...] = jnp.where(odd, outputs[:, :half], outputs[:, half:])


def spread_kernel(kept_ref, other_ref, out_ref):
    slots = out_ref.shape[1]
    groups = kept_ref.shape[0] // slots
    outputs = kept_ref[...] + other_ref[...]
    for block in range(out_ref.shape[0]):
        first = block % groups * slots
        out_ref[block] = outputs[first : first + slots].astype(jnp.bfloat16)


def column_block(sharer, sharers):
    block = 0
    while sharers > 1:
        sharers //= 2
        block += (sharer & 1) * sharers
        sharer >>= 1
    return block


def final_kernel(gates_ref, returned_ref, residual_ref, out_ref, table_ref):
    requests, steps, width = out_ref.shape
    devices, groups, slots, part = returned_ref.shape
    local_experts = EXPERTS // groups
    sharers = devices // local_experts
    for s in range(devices):
        first = column_block(s % sharers, sharers) * part
        for x in range(groups):
            row = (x * local_experts + s // sharers) * slots
            table_ref[row : row + slots, first : first + part] = returned_ref[s, x].astype(jnp.float32)
    table = table_ref[...].astype(jnp.bfloat16)
    moe = exact_dot(gates_ref[...], table)
    total = residual_ref[...] + moe
    for r in range(requests):
        out_ref[r] = total[r * steps : (r + 1) * steps].astype(jnp.bfloat16)


def exchange(value, bits):
    return lax.ppermute(value, "seq", [(i, i ^ bits) for i in range(lax.axis_size("seq"))])


def from_chips(values, meanwhile=None):
    others = [exchange(values, k) for k in range(2, lax.axis_size("seq"), 2)]
    if meanwhile is not None:
        values = meanwhile(values)
    return [values] + others


def gather_seq(values, meanwhile=None):
    near = from_chips(values, meanwhile)
    return [part for value in near for part in (value, exchange(value, 1))]


def shape(dims, dtype):
    return jax.ShapeDtypeStruct(dims, dtype)


def body(
    tokens,
    attn_gain,
    w_qkv,
    window_cache,
    sink_cache,
    lengths,
    w_out,
    moe_gain,
    router,
    expert_ids,
    slot_order,
    expert_in,
    expert_down,
):
    requests, steps, width = tokens.shape
    rows = requests * steps
    seq_index = lax.axis_index("seq")
    seq_count = lax.axis_size("seq")
    groups = lax.axis_size("exp")
    local_experts = EXPERTS // groups
    sharers = seq_count // local_experts
    span = window_cache.shape[2]
    share = w_qkv.shape[0]
    slots = EXPERTS * CAP
    f32, bf16 = jnp.float32, jnp.bfloat16

    vmem = pl.BlockSpec(memory_space=pltpu.VMEM)
    hbm = pl.BlockSpec(memory_space=pltpu.HBM)

    gain_row = attn_gain.reshape(1, width)
    local_mix, spans = pl.pallas_call(
        qkv_kernel,
        in_specs=[hbm] * 5,
        out_shape=(shape((rows, share), bf16), shape((requests, LANES), jnp.int32)),
        scratch_shapes=[
            pltpu.VMEM(tokens.shape, bf16),
            pltpu.VMEM(gain_row.shape, f32),
            pltpu.VMEM(w_qkv.shape, bf16),
            pltpu.VMEM((rows, width), f32),
            pltpu.SMEM((requests,), jnp.int32),
            pltpu.SemaphoreType.DMA((4,)),
        ],
        compiler_params=params(4),
        name="qkv",
    )(in_hbm(tokens), in_hbm(gain_row), in_hbm(w_qkv), in_hbm(window_cache), in_hbm(lengths))

    mixed = gather_seq(local_mix)

    padded = width + LANES
    def attention(of_own):
        return pl.pallas_call(
            functools.partial(attention_kernel, of_own),
            in_specs=[vmem] * (seq_count + 2),
            out_shape=shape((rows, PACKED), bf16),
            scratch_shapes=[
                pltpu.VMEM((seq_count, rows, share), bf16),
                pltpu.VMEM((rows, padded), f32),
                pltpu.VMEM((rows, PACKED), f32),
            ],
            compiler_params=params(8),
            name="attention_own" if of_own else "attention_other",
        )(*mixed, spans, window_cache)

    sent = attention(False)
    other = exchange(sent, 1)
    kept = attention(True)

    extra, extra_stats = pl.pallas_call(
        extra_kernel,
        out_shape=(shape((rows, width), f32), shape((rows, LANES), f32)),
        scratch_shapes=[
            pltpu.VMEM((seq_count, rows, share), bf16),
            pltpu.VMEM((rows, 3 * width), f32),
            pltpu.VMEM((rows * BLOCK_HEADS, width), f32),
            pltpu.VMEM((2, requests * (SINKS + steps), width), f32),
        ],
        compiler_params=params(8),
        name="extra",
    )(*mixed, sink_cache)

    part = pl.pallas_call(
        pair_kernel,
        out_shape=shape((rows, PACKED), bf16),
        compiler_params=params(8),
        name="pair",
    )(kept, other)

    hidden_units = expert_down.shape[1]
    held_units = min(HELD, hidden_units)
    late_units = max(hidden_units - held_units, 16)

    fetched = []

    def fetch_expert(values):
        held, *outputs = pl.pallas_call(
            fetch_expert_kernel,
            in_specs=[vmem] + [hbm] * 4,
            out_shape=(
                shape(values.shape, bf16),
                shape((2, held_units, width), bf16),
                shape((TOPK, rows, slots), f32),
                shape((TOPK, rows, LANES), f32),
                shape((slots, rows), f32),
                shape((rows, w_out.shape[0]), f32),
            ),
            scratch_shapes=[
                pltpu.VMEM((steps, TOPK, requests), jnp.int32),
                pltpu.VMEM(slot_order.shape, jnp.int32),
                pltpu.VMEM(tokens.shape, bf16),
                pltpu.VMEM((rows, width), f32),
                pltpu.SemaphoreType.DMA((5,)),
            ],
            compiler_params=params(8),
            cost_estimate=moving(4 * held_units * width),
            name="fetch_expert",
        )(
            values,
            in_hbm(expert_in),
            in_hbm(expert_ids.transpose(1, 2, 0)),
            in_hbm(slot_order),
            in_hbm(tokens),
        )
        fetched.extend(outputs)
        return held

    parts = from_chips(part, fetch_expert)
    other_weight = exchange(lax.optimization_barrier((w_out, part))[0], 1)
    piece, select, chosen, turned, token_columns = fetched

    outgoing, residual_columns = pl.pallas_call(
        project_kernel,
        out_shape=(
            shape((seq_count * groups, CAP, CORES * w_out.shape[0]), bf16),
            shape((rows, CORES * w_out.shape[0]), f32),
        ),
        compiler_params=params(16),
        name="project",
    )(*parts, extra, extra_stats, w_out, other_weight, token_columns, turned)
    received = lax.all_to_all(outgoing, ("seq", "exp"), split_axis=0, concat_axis=0, tiled=True)
    columns = gather_seq(residual_columns)

    moe_row = moe_gain.reshape(1, width)
    kept, sent = pl.pallas_call(
        expert_kernel,
        in_specs=[vmem, vmem, vmem, hbm, hbm],
        out_shape=(
            shape((groups * CAP, width // 2), f32),
            shape((groups * CAP, width // 2), f32),
        ),
        scratch_shapes=[
            pltpu.VMEM((2, late_units, width), bf16),
            pltpu.VMEM((hidden_units, width), bf16),
            pltpu.SemaphoreType.DMA((3 * pl.cdiv(late_units, PIECE) + 1,)),
        ],
        compiler_params=params(20),
        name="expert",
    )(received, moe_row, piece, in_hbm(expert_in), in_hbm(expert_down))

    reach = 1
    while True:
        other = lax.ppermute(sent, "seq", [(i, i ^ reach) for i in range(seq_count)])
        reach *= 2
        if reach >= sharers:
            break
        upper = (seq_index // reach) % 2 == 1
        low, high = jnp.split(kept + other, 2, axis=1)
        kept, sent = jnp.where(upper, high, low), jnp.where(upper, low, high)
    part_width = kept.shape[1]
    outgoing = pl.pallas_call(
        spread_kernel,
        out_shape=shape((seq_count * groups, CAP, part_width), bf16),
        compiler_params=params(8),
        name="spread",
    )(kept, other)
    returned = lax.all_to_all(
        outgoing,
        ("seq", "exp"),
        split_axis=0,
        concat_axis=0,
        tiled=True,
    ).reshape(seq_count, groups, CAP, part_width)

    columns, _ = lax.optimization_barrier((columns, outgoing))
    residual, gates = pl.pallas_call(
        functools.partial(home_kernel, seq_count),
        out_shape=(shape((rows, width), f32), shape((rows, slots), f32)),
        scratch_shapes=[pltpu.VMEM((seq_count, rows, CORES * w_out.shape[0]), f32)],
        compiler_params=params(8),
        name="home",
    )(*columns, moe_row, router.T, select, chosen)

    return pl.pallas_call(
        final_kernel,
        out_shape=shape((requests, steps, width), bf16),
        scratch_shapes=[pltpu.VMEM((slots, width), f32)],
        compiler_params=params(8),
        name="final",
    )(gates, returned, residual)


def solution(mesh):
    in_specs = (
        P("exp", None, None),
        P(),
        P("seq", None),
        P(None, "exp", "seq", None),
        P(None, "exp", None, None),
        P("exp"),
        P("seq", None),
        P(),
        P(),
        P("exp", None, None),
        P("exp", None),
        P(None, "exp", "seq", None),
        P("exp", "seq", None),
    )
    out_specs = P("exp", None, None)
    return jax.shard_map(body, mesh=mesh, in_specs=in_specs, out_specs=out_specs, check_vma=False)
```

```python
import functools

import jax
import jax.numpy as jnp
from jax import lax
from jax.experimental import pallas as pl
from jax.experimental.pallas import tpu as pltpu
from jax.sharding import PartitionSpec as P

HEADS = 16
HD = 64
EXPERTS = 16
TOPK = 2
SINKS = 4
WIN = 4096
CAP = 8
LANES = 128
PIECES = 3
FIRST_KEYS = 2
SECOND_KEYS = 8
SECOND_VALUES = 3
CORES = 2
HALF_HEADS = HEADS // CORES
HALF = HALF_HEADS * HD
PACKED = HALF + LANES
HELD = 800
PIECE = 304
AHEAD = 10
BLOCK = 256
BLOCK_HEADS = BLOCK // HD

EPSILON = 1e-06
MASKED = -1e30
MIB = 1 << 20
ROWS_BY_ROWS = (((1,), (1,)), ((), ()))
ROWS_BY_COLS = (((1,), (0,)), ((), ()))


def dot(a, b, dims=ROWS_BY_COLS):
    return lax.dot_general(a, b, dims, preferred_element_type=jnp.float32)


def params(limit_mib=32):
    return pltpu.CompilerParams(vmem_limit_bytes=limit_mib * MIB)


def moving(count):
    return pl.CostEstimate(flops=0, bytes_accessed=count, transcendentals=0)


def in_hbm(value):
    return pltpu.with_memory_space_constraint(value, pltpu.HBM)


def split(value, count):
    parts = []
    for _ in range(count):
        part = value.astype(jnp.bfloat16)
        parts.append(part)
        value = value - part.astype(jnp.float32)
    return parts


def exact_dot(values, table):
    high, low = split(values, 2)
    both = dot(jnp.concatenate([high, low], axis=0), table)
    return both[: values.shape[0]] + both[values.shape[0] :]


def rms_rows(widened, gain_row):
    inverse = lax.rsqrt(jnp.mean(widened * widened, axis=-1, keepdims=True) + EPSILON)
    return (widened * inverse * gain_row).astype(jnp.bfloat16)


def copy_rows(source_ref, rows_ref):
    requests, steps, _ = source_ref.shape
    for r in range(requests):
        rows_ref[r * steps : (r + 1) * steps, :] = source_ref[r].astype(rows_ref.dtype)


def each(sems):
    return [sems.at[i] for i in range(sems.shape[0])]


def each(sems):
    return [sems.at[i] for i in range(sems.shape[0])]


def started(pairs, sems):
    copies = [pltpu.make_async_copy(*pair, sem) for pair, sem in zip(pairs, sems)]
    for copy in copies:
        copy.start()
    return copies


def unpack(packed):
    stats = packed[:, HALF:].astype(jnp.float32)

    def joined(first):
        return sum(
            stats[:, (first + i) * HALF_HEADS : (first + i + 1) * HALF_HEADS] for i in range(PIECES)
        )

    return joined(0), joined(PIECES), packed[:, :HALF].astype(jnp.float32)


def pack(peak, total, mixed):
    parts = [part.astype(jnp.float32) for part in split(peak, PIECES) + split(total, PIECES)]
    blank = jnp.zeros((peak.shape[0], LANES - 2 * PIECES * HALF_HEADS), jnp.float32)
    return jnp.concatenate([mixed] + parts + [blank], axis=1).astype(jnp.bfloat16)


def over_heads(factor):
    row = lax.broadcasted_iota(jnp.int32, (HALF_HEADS, HALF), 0)
    col = lax.broadcasted_iota(jnp.int32, (HALF_HEADS, HALF), 1) // HD
    expand = (row == col).astype(jnp.bfloat16)
    return sum(dot(part, expand) for part in split(factor, 2))


def merge(parts):
    overall = functools.reduce(jnp.maximum, [peak for peak, _, _ in parts])
    factors = [jnp.exp(peak - overall) for peak, _, _ in parts]
    total = sum(factor * part[1] for factor, part in zip(factors, parts))
    mixed = sum(over_heads(factor) * part[2] for factor, part in zip(factors, parts))
    return overall, total, mixed


def attend(parts):
    overall = functools.reduce(jnp.maximum, [peak for peak, _, _ in parts])
    factors = [jnp.exp(peak - overall) for peak, _, _ in parts]
    total = sum(factor * part[1] for factor, part in zip(factors, parts))
    inverse = jnp.where(total > 0, 1.0 / jnp.where(total > 0, total, 1.0), 0.0)
    return sum(over_heads(factor * inverse) * part[2] for factor, part in zip(factors, parts))


def route(ids_ref, order_ref, select_ref, chosen_ref):
    steps, _, requests = ids_ref.shape
    rows = requests * steps
    lane = lax.broadcasted_iota(jnp.int32, (rows, LANES), 1)
    own_row = lax.broadcasted_iota(jnp.int32, (rows, requests), 0)
    own_request = lax.broadcasted_iota(jnp.int32, (rows, requests), 1) == own_row // steps
    chosen = []
    for c in range(TOPK):
        ids = jnp.zeros((rows, requests), jnp.int32)
        for t in range(steps):
            ids = jnp.where(own_request & (own_row % steps == t), ids_ref[t, c : c + 1, :], ids)
        chosen.append(jnp.sum(ids.astype(jnp.float32), axis=1, keepdims=True).astype(jnp.int32))
    onehot = [(lane == ids).astype(jnp.float32) for ids in chosen]
    square_row = lax.broadcasted_iota(jnp.int32, (rows, rows), 0)
    square_col = lax.broadcasted_iota(jnp.int32, (rows, rows), 1)
    order_wide = jnp.broadcast_to(order_ref[...], (rows, rows))
    down = jnp.sum(
        jnp.where(square_row == square_col, order_wide, 0).astype(jnp.float32),
        axis=1,
        keepdims=True,
    )
    earlier = (order_wide.astype(jnp.float32) < down).astype(jnp.bfloat16)
    counts = dot(earlier, sum(onehot).astype(jnp.bfloat16))
    slot = lax.broadcasted_iota(jnp.int32, (rows, EXPERTS * CAP), 1)
    both = jnp.zeros((rows, EXPERTS * CAP), jnp.float32)
    for c in range(TOPK):
        position = jnp.sum(onehot[c] * counts, axis=-1, keepdims=True).astype(jnp.int32)
        column = chosen[c] * CAP + position
        select = ((column == slot) & (position < CAP)).astype(jnp.float32)
        select_ref[c] = select
        chosen_ref[c] = onehot[c]
        both = both + select
    return jnp.transpose(both)


def qkv_kernel(
    tokens_ref,
    gain_ref,
    weight_ref,
    window_ref,
    lengths_ref,
    out_ref,
    spans_ref,
    token_buf,
    gain_buf,
    weight_buf,
    rows_ref,
    numbers_ref,
    sems,
):
    copies = started(
        (
            (tokens_ref, token_buf),
            (gain_ref, gain_buf),
            (lengths_ref, numbers_ref),
            (weight_ref, weight_buf),
        ),
        each(sems),
    )
    for copy in copies[:3]:
        copy.wait()
    copy_rows(token_buf, rows_ref)
    normed = rms_rows(rows_ref[...], gain_buf[...])
    for r in range(spans_ref.shape[0]):
        spans_ref[r : r + 1, :] = jnp.full((1, LANES), numbers_ref[r], jnp.int32)
    copies[3].wait()
    out_ref[...] = dot(normed, weight_buf[...], ROWS_BY_ROWS).astype(jnp.bfloat16)


def in_order(sent_refs, ordered_ref):
    place = lax.axis_index("seq")
    for k, sent_ref in enumerate(sent_refs):
        ordered_ref[jnp.bitwise_xor(place, k)] = sent_ref[...]


def head_masks(rows, width, steps):
    row_head = lax.broadcasted_iota(jnp.int32, (rows, width), 0) // steps % BLOCK_HEADS
    col_head = lax.broadcasted_iota(jnp.int32, (rows, width), 1) // HD % BLOCK_HEADS
    return (row_head == col_head).astype(jnp.float32)


def fetch_expert_kernel(
    sent_ref,
    in_ref,
    ids_ref,
    order_ref,
    tokens_ref,
    held_ref,
    piece_ref,
    select_ref,
    chosen_ref,
    turned_ref,
    columns_ref,
    ids_buf,
    order_buf,
    tokens_buf,
    rows_ref,
    sems,
):
    pairs = [(ids_ref, ids_buf), (order_ref, order_buf), (tokens_ref, tokens_buf)]
    pairs += [
        (in_ref.at[p, 0, pl.ds(0, piece_ref.shape[1])], piece_ref.at[p]) for p in range(2)
    ]
    copies = started(pairs, each(sems))
    held_ref[...] = sent_ref[...]
    for copy in copies[:3]:
        copy.wait()
    turned_ref[...] = route(ids_buf, order_buf, select_ref, chosen_ref)
    copy_rows(tokens_buf, rows_ref)
    width, share = rows_ref.shape[1], columns_ref.shape[1]
    feature = lax.broadcasted_iota(jnp.int32, (width, share), 0)
    column = lax.broadcasted_iota(jnp.int32, (width, share), 1)
    own = (feature == column + lax.axis_index("seq") * share).astype(jnp.bfloat16)
    columns_ref[...] = dot(rows_ref[...].astype(jnp.bfloat16), own)
    for copy in copies[3:]:
        copy.wait()


def attention_kernel(of_own, *refs):
    *mixed_refs, spans_ref, window_ref = refs[:-4]
    out_ref, ordered_ref, flat_ref, result_ref = refs[-4:]
    devices, rows, share = ordered_ref.shape
    _, requests, span, width = window_ref.shape
    steps = rows // requests
    block_rows = BLOCK_HEADS * steps
    place = lax.axis_index("seq")
    in_order(mixed_refs, ordered_ref)
    for d in range(devices):
        if d * share < width:
            flat_ref[:, d * share : (d + 1) * share] = ordered_ref[d].astype(jnp.float32)
    own_head = head_masks(block_rows, HALF, steps)
    half = place % CORES if of_own else 1 - place % CORES
    heads = pl.ds(pl.multiple_of(half * HALF, HALF), HALF)
    base = place * span
    scale = HD ** (-0.5)
    pair = 2 * steps
    tiles = HALF_HEADS * steps // pair
    slot = base + lax.broadcasted_iota(jnp.int32, (pair, span), 1)
    step = lax.broadcasted_iota(jnp.int32, (pair, span), 0) % steps
    stat_lane = lax.broadcasted_iota(jnp.int32, (HALF_HEADS * steps, LANES), 1)
    stat_head = lax.broadcasted_iota(jnp.int32, (HALF_HEADS * steps, LANES), 0) // steps
    cols = [slice(c, c + BLOCK) for c in range(0, HALF, BLOCK)]

    def score(r):
        keys = window_ref[0, r, :, heads]
        queries = flat_ref[r * steps : (r + 1) * steps, heads]
        queries = (jnp.concatenate([queries] * BLOCK_HEADS, axis=0) * own_head).astype(jnp.bfloat16)
        return jnp.concatenate(
            [dot(queries[:, c], keys[:, c], ROWS_BY_ROWS) for c in cols], axis=0
        )

    scores = score(0)
    for r in range(requests):
        following = score(r + 1) if r + 1 < requests else None
        length = spans_ref[r : r + 1, 0:1]
        age = jnp.bitwise_and(slot - (length - SINKS), WIN - 1)
        live = ((slot < jnp.minimum(WIN, length - SINKS)) & (age > step))[None]
        scores = jnp.where(live, scores.reshape(tiles, pair, span) * scale, MASKED)
        peak = jnp.max(scores, axis=-1, keepdims=True)
        weight = jnp.where(live, jnp.exp(scores - peak), 0.0)
        total = jnp.sum(weight, axis=-1, keepdims=True)
        weight = weight.reshape(HALF_HEADS * steps, span).astype(jnp.bfloat16)
        values = window_ref[1, r, :, heads]
        outs = []
        for b, c in enumerate(cols):
            own = slice(b * block_rows, (b + 1) * block_rows)
            mixed = dot(weight[own], values[:, c]) * own_head[:, c]
            mixed = sum(mixed[i : i + pair] for i in range(0, block_rows, pair))
            outs.append(mixed[:steps] + mixed[steps:])
        stats = jnp.where(stat_lane == stat_head, peak.reshape(HALF_HEADS * steps, 1), 0.0)
        stats = jnp.where(stat_lane == stat_head + HALF_HEADS, total.reshape(HALF_HEADS * steps, 1), stats)
        stats = jnp.sum(stats.reshape(tiles, pair, LANES), axis=0)
        outs.append(stats[:steps] + stats[steps:])
        result_ref[r * steps : (r + 1) * steps, :] = jnp.concatenate(outs, axis=1)
        scores = following
    peak = result_ref[:, HALF : HALF + HALF_HEADS]
    total = result_ref[:, HALF + HALF_HEADS : HALF + 2 * HALF_HEADS]
    out_ref[...] = pack(peak, total, result_ref[:, :HALF])


def extra_kernel(*refs):
    *mixed_refs, sinks_ref = refs[:-6]
    out_ref, stats_ref, ordered_ref, flat_ref, query_ref, keys_ref = refs[-6:]
    devices, rows, share = ordered_ref.shape
    _, requests, sinks, width = sinks_ref.shape
    steps = rows // requests
    block_rows = BLOCK_HEADS * steps
    count = sinks + steps
    in_order(mixed_refs, ordered_ref)
    for d in range(devices):
        flat_ref[:, d * share : (d + 1) * share] = ordered_ref[d].astype(jnp.float32)
    own_head = head_masks(block_rows, width, steps)
    for r in range(requests):
        own = slice(r * steps, (r + 1) * steps)
        queries = jnp.concatenate([flat_ref[own, 0:width]] * BLOCK_HEADS, axis=0) * own_head
        query_ref[r * block_rows : (r + 1) * block_rows, :] = queries
        for p in range(2):
            keys_ref[p, r * count : r * count + sinks] = sinks_ref[p, r].astype(jnp.float32)
            keys_ref[p, r * count + sinks : (r + 1) * count] = flat_ref[
                own, (p + 1) * width : (p + 2) * width
            ]
    all_rows = requests * block_rows
    all_keys = requests * count
    row = lax.broadcasted_iota(jnp.int32, (all_rows, all_keys), 0)
    key = lax.broadcasted_iota(jnp.int32, (all_rows, all_keys), 1)
    live = (row // block_rows == key // count) & (key % count - sinks <= row % steps)
    stat_lane = lax.broadcasted_iota(jnp.int32, (all_rows, LANES), 1)
    stat_head = lax.broadcasted_iota(jnp.int32, (all_rows, LANES), 0) % block_rows // steps
    whole_mask = jnp.concatenate([own_head[:, :BLOCK]] * requests, axis=0)
    stats = jnp.zeros((all_rows, LANES), jnp.float32)
    pair = 2 * steps

    def by_request(values):
        values = jnp.sum(values.reshape(requests, block_rows // pair, pair, values.shape[-1]), axis=1)
        return values[:, :steps] + values[:, steps:]

    for b in range(width // BLOCK):
        c = slice(b * BLOCK, (b + 1) * BLOCK)
        scores = dot(
            query_ref[:, c].astype(jnp.bfloat16), keys_ref[0, :, c].astype(jnp.bfloat16), ROWS_BY_ROWS
        )
        scores = jnp.where(live, scores * HD ** (-0.5), MASKED)
        peak = jnp.max(scores, axis=-1, keepdims=True)
        weight = jnp.where(live, jnp.exp(scores - peak), 0.0)
        total = jnp.sum(weight, axis=-1, keepdims=True)
        mixed = dot(weight.astype(jnp.bfloat16), keys_ref[1, :, c].astype(jnp.bfloat16))
        mixed = by_request(mixed * whole_mask)
        for r in range(requests):
            out_ref[r * steps : (r + 1) * steps, c] = mixed[r]
        stats = jnp.where(stat_lane == stat_head + b * BLOCK_HEADS, peak, stats)
        stats = jnp.where(stat_lane == stat_head + b * BLOCK_HEADS + HEADS, total, stats)
    stats = by_request(stats)
    for r in range(requests):
        stats_ref[r * steps : (r + 1) * steps, :] = stats[r]


def pair_kernel(keep_ref, other_ref, out_ref):
    out_ref[...] = pack(*merge([unpack(keep_ref[...]), unpack(other_ref[...])]))


def project_kernel(*refs):
    *part_refs, extra_ref, extra_stats_ref, weight_ref, other_weight_ref, columns_ref = refs[:-3]
    turned_ref, out_ref, residual_ref = refs[-3:]
    devices = lax.axis_size("seq")
    groups = lax.axis_size("exp")
    local_experts = EXPERTS // groups
    odd = lax.axis_index("seq") % CORES == 1

    def own_half(value, at, width):
        return jnp.where(odd, value[:, at + width : at + 2 * width], value[:, at : at + width])

    parts = [unpack(part_ref[...]) for part_ref in part_refs]
    parts.append(
        (
            own_half(extra_stats_ref[...], 0, HALF_HEADS),
            own_half(extra_stats_ref[...], HEADS, HALF_HEADS),
            own_half(extra_ref[...], 0, HALF),
        )
    )
    attended = attend(parts).astype(jnp.bfloat16)

    def project(weight):
        weight = jnp.where(odd, weight[:, HALF:], weight[:, :HALF])
        return dot(attended, weight, ROWS_BY_ROWS)

    mine = project(weight_ref[...]) + columns_ref[...]
    others = project(other_weight_ref[...])
    residual = jnp.concatenate(
        [jnp.where(odd, others, mine), jnp.where(odd, mine, others)], axis=1
    )
    residual_ref[...] = residual
    table = dot(turned_ref[...].astype(jnp.bfloat16), residual.astype(jnp.bfloat16))
    for s in range(devices):
        for x in range(groups):
            row = (x * local_experts + s // (devices // local_experts)) * CAP
            out_ref[s * groups + x] = table[row : row + CAP].astype(jnp.bfloat16)


def home_kernel(devices, *refs):
    residual_refs, refs = refs[:devices], refs[devices:]
    gain_ref, router_ref, select_ref, chosen_ref, residual_ref, gates_ref, ordered_ref = refs
    in_order(residual_refs, ordered_ref)
    residual = jnp.concatenate(
        [ordered_ref[d] + ordered_ref[d + 1] for d in range(0, devices, CORES)], axis=1
    )
    residual_ref[...] = residual
    normed = rms_rows(residual, gain_ref[...])
    logits = dot(normed, router_ref[...], ROWS_BY_ROWS)
    gates = jnp.zeros(select_ref.shape[1:], jnp.float32)
    for c in range(TOPK):
        logit = jnp.sum(chosen_ref[c][:, :EXPERTS] * logits, axis=-1, keepdims=True)
        gates = gates + jax.nn.sigmoid(logit) * select_ref[c]
    gates_ref[...] = gates


def expert_kernel(
    received_ref, gain_ref, piece_ref, in_ref, down_ref, keep_ref, send_ref, in_buf, down_buf, sems
):
    hidden_units, width = down_buf.shape
    held = piece_ref.shape[1]
    pieces = [(at, min(PIECE, hidden_units - at)) for at in range(held, hidden_units, PIECE)]
    downs = [(0, held)] + pieces
    stages = []
    for at, count in pieces:
        stages.append(
            [
                (in_ref.at[p, 0, pl.ds(at, count)], in_buf.at[p, pl.ds(at - held, count)])
                for p in range(2)
            ]
        )
    for at, count in downs:
        stages.append([(down_ref.at[0, pl.ds(at, count)], down_buf.at[pl.ds(at, count)])])
    flying = []

    def start_next():
        if len(flying) < len(stages):
            first = sum(len(stage) for stage in stages[: len(flying)])
            flying.append(started(stages[len(flying)], [sems.at[first + i] for i in range(len(stages[len(flying)]))]))

    def wait_for(stage):
        for copy in flying[stage]:
            copy.wait()
        start_next()

    for _ in range(AHEAD):
        start_next()
    devices = lax.axis_size("seq")
    groups = lax.axis_size("exp")
    columns = []
    for s in range(0, devices, CORES):
        pieces_of_chip = [
            jnp.concatenate(
                [received_ref[d * groups + g].astype(jnp.float32) for g in range(groups)], axis=0
            )
            for d in range(s, s + CORES)
        ]
        columns.append(sum(pieces_of_chip))
    rows = rms_rows(jnp.concatenate(columns, axis=1), gain_ref[...])

    def layer(gate_weight, up_weight):
        gate = dot(rows, gate_weight, ROWS_BY_ROWS)
        up = dot(rows, up_weight, ROWS_BY_ROWS)
        return (jax.nn.gelu(gate, approximate=True) * up).astype(jnp.bfloat16)

    hidden = [layer(piece_ref[0], piece_ref[1])]
    for i, (at, count) in enumerate(pieces):
        wait_for(i)
        own = slice(at - held, at - held + count)
        hidden.append(layer(in_buf[0, own], in_buf[1, own]))
    outputs = jnp.zeros((groups * CAP, width), jnp.float32)
    for i, (at, count) in enumerate(downs):
        wait_for(len(pieces) + i)
        outputs = outputs + dot(hidden[i], down_buf[at : at + count])
    half = width // 2
    odd = lax.axis_index("seq") % 2 == 1
    keep_ref[...] = jnp.where(odd, outputs[:, half:], outputs[:, :half])
    send_ref[...] = jnp.where(odd, outputs[:, :half], outputs[:, half:])


def spread_kernel(kept_ref, other_ref, out_ref):
    slots = out_ref.shape[1]
    groups = kept_ref.shape[0] // slots
    outputs = kept_ref[...] + other_ref[...]
    for block in range(out_ref.shape[0]):
        first = block % groups * slots
        out_ref[block] = outputs[first : first + slots].astype(jnp.bfloat16)


def column_block(sharer, sharers):
    block = 0
    while sharers > 1:
        sharers //= 2
        block += (sharer & 1) * sharers
        sharer >>= 1
    return block


def final_kernel(gates_ref, returned_ref, residual_ref, out_ref, table_ref):
    requests, steps, width = out_ref.shape
    devices, groups, slots, part = returned_ref.shape
    local_experts = EXPERTS // groups
    sharers = devices // local_experts
    for s in range(devices):
        first = column_block(s % sharers, sharers) * part
        for x in range(groups):
            row = (x * local_experts + s // sharers) * slots
            table_ref[row : row + slots, first : first + part] = returned_ref[s, x].astype(jnp.float32)
    table = table_ref[...].astype(jnp.bfloat16)
    moe = exact_dot(gates_ref[...], table)
    total = residual_ref[...] + moe
    for r in range(requests):
        out_ref[r] = total[r * steps : (r + 1) * steps].astype(jnp.bfloat16)


def exchange(value, bits):
    return lax.ppermute(value, "seq", [(i, i ^ bits) for i in range(lax.axis_size("seq"))])


def from_chips(values, meanwhile=None):
    others = [exchange(values, k) for k in range(2, lax.axis_size("seq"), 2)]
    if meanwhile is not None:
        values = meanwhile(values)
    return [values] + others


def gather_seq(values, meanwhile=None):
    near = from_chips(values, meanwhile)
    return [part for value in near for part in (value, exchange(value, 1))]


def shape(dims, dtype):
    return jax.ShapeDtypeStruct(dims, dtype)


def body(
    tokens,
    attn_gain,
    w_qkv,
    window_cache,
    sink_cache,
    lengths,
    w_out,
    moe_gain,
    router,
    expert_ids,
    slot_order,
    expert_in,
    expert_down,
):
    requests, steps, width = tokens.shape
    rows = requests * steps
    seq_index = lax.axis_index("seq")
    seq_count = lax.axis_size("seq")
    groups = lax.axis_size("exp")
    local_experts = EXPERTS // groups
    sharers = seq_count // local_experts
    span = window_cache.shape[2]
    share = w_qkv.shape[0]
    slots = EXPERTS * CAP
    f32, bf16 = jnp.float32, jnp.bfloat16

    vmem = pl.BlockSpec(memory_space=pltpu.VMEM)
    hbm = pl.BlockSpec(memory_space=pltpu.HBM)

    gain_row = attn_gain.reshape(1, width)
    local_mix, spans = pl.pallas_call(
        qkv_kernel,
        in_specs=[hbm] * 5,
        out_shape=(shape((rows, share), bf16), shape((requests, LANES), jnp.int32)),
        scratch_shapes=[
            pltpu.VMEM(tokens.shape, bf16),
            pltpu.VMEM(gain_row.shape, f32),
            pltpu.VMEM(w_qkv.shape, bf16),
            pltpu.VMEM((rows, width), f32),
            pltpu.SMEM((requests,), jnp.int32),
            pltpu.SemaphoreType.DMA((4,)),
        ],
        compiler_params=params(4),
        name="qkv",
    )(in_hbm(tokens), in_hbm(gain_row), in_hbm(w_qkv), in_hbm(window_cache), in_hbm(lengths))

    mixed = gather_seq(local_mix)

    padded = width + LANES
    def attention(of_own):
        return pl.pallas_call(
            functools.partial(attention_kernel, of_own),
            in_specs=[vmem] * (seq_count + 2),
            out_shape=shape((rows, PACKED), bf16),
            scratch_shapes=[
                pltpu.VMEM((seq_count, rows, share), bf16),
                pltpu.VMEM((rows, padded), f32),
                pltpu.VMEM((rows, PACKED), f32),
            ],
            compiler_params=params(8),
            name="attention_own" if of_own else "attention_other",
        )(*mixed, spans, window_cache)

    sent = attention(False)
    other = exchange(sent, 1)
    kept = attention(True)

    extra, extra_stats = pl.pallas_call(
        extra_kernel,
        out_shape=(shape((rows, width), f32), shape((rows, LANES), f32)),
        scratch_shapes=[
            pltpu.VMEM((seq_count, rows, share), bf16),
            pltpu.VMEM((rows, 3 * width), f32),
            pltpu.VMEM((rows * BLOCK_HEADS, width), f32),
            pltpu.VMEM((2, requests * (SINKS + steps), width), f32),
        ],
        compiler_params=params(8),
        name="extra",
    )(*mixed, sink_cache)

    part = pl.pallas_call(
        pair_kernel,
        out_shape=shape((rows, PACKED), bf16),
        compiler_params=params(8),
        name="pair",
    )(kept, other)

    hidden_units = expert_down.shape[1]
    held_units = min(HELD, hidden_units)
    late_units = max(hidden_units - held_units, 16)

    fetched = []

    def fetch_expert(values):
        held, *outputs = pl.pallas_call(
            fetch_expert_kernel,
            in_specs=[vmem] + [hbm] * 4,
            out_shape=(
                shape(values.shape, bf16),
                shape((2, held_units, width), bf16),
                shape((TOPK, rows, slots), f32),
                shape((TOPK, rows, LANES), f32),
                shape((slots, rows), f32),
                shape((rows, w_out.shape[0]), f32),
            ),
            scratch_shapes=[
                pltpu.VMEM((steps, TOPK, requests), jnp.int32),
                pltpu.VMEM(slot_order.shape, jnp.int32),
                pltpu.VMEM(tokens.shape, bf16),
                pltpu.VMEM((rows, width), f32),
                pltpu.SemaphoreType.DMA((5,)),
            ],
            compiler_params=params(8),
            cost_estimate=moving(4 * held_units * width),
            name="fetch_expert",
        )(
            values,
            in_hbm(expert_in),
            in_hbm(expert_ids.transpose(1, 2, 0)),
            in_hbm(slot_order),
            in_hbm(tokens),
        )
        fetched.extend(outputs)
        return held

    parts = from_chips(part, fetch_expert)
    other_weight = exchange(lax.optimization_barrier((w_out, part))[0], 1)
    piece, select, chosen, turned, token_columns = fetched

    outgoing, residual_columns = pl.pallas_call(
        project_kernel,
        out_shape=(
            shape((seq_count * groups, CAP, CORES * w_out.shape[0]), bf16),
            shape((rows, CORES * w_out.shape[0]), f32),
        ),
        compiler_params=params(16),
        name="project",
    )(*parts, extra, extra_stats, w_out, other_weight, token_columns, turned)
    received = lax.all_to_all(outgoing, ("seq", "exp"), split_axis=0, concat_axis=0, tiled=True)
    columns = gather_seq(residual_columns)

    moe_row = moe_gain.reshape(1, width)
    kept, sent = pl.pallas_call(
        expert_kernel,
        in_specs=[vmem, vmem, vmem, hbm, hbm],
        out_shape=(
            shape((groups * CAP, width // 2), f32),
            shape((groups * CAP, width // 2), f32),
        ),
        scratch_shapes=[
            pltpu.VMEM((2, late_units, width), bf16),
            pltpu.VMEM((hidden_units, width), bf16),
            pltpu.SemaphoreType.DMA((3 * pl.cdiv(late_units, PIECE) + 1,)),
        ],
        compiler_params=params(20),
        name="expert",
    )(received, moe_row, piece, in_hbm(expert_in), in_hbm(expert_down))

    reach = 1
    while True:
        other = lax.ppermute(sent, "seq", [(i, i ^ reach) for i in range(seq_count)])
        reach *= 2
        if reach >= sharers:
            break
        upper = (seq_index // reach) % 2 == 1
        low, high = jnp.split(kept + other, 2, axis=1)
        kept, sent = jnp.where(upper, high, low), jnp.where(upper, low, high)
    part_width = kept.shape[1]
    outgoing = pl.pallas_call(
        spread_kernel,
        out_shape=shape((seq_count * groups, CAP, part_width), bf16),
        compiler_params=params(8),
        name="spread",
    )(kept, other)
    returned = lax.all_to_all(
        outgoing,
        ("seq", "exp"),
        split_axis=0,
        concat_axis=0,
        tiled=True,
    ).reshape(seq_count, groups, CAP, part_width)

    columns, _ = lax.optimization_barrier((columns, outgoing))
    residual, gates = pl.pallas_call(
        functools.partial(home_kernel, seq_count),
        out_shape=(shape((rows, width), f32), shape((rows, slots), f32)),
        scratch_shapes=[pltpu.VMEM((seq_count, rows, CORES * w_out.shape[0]), f32)],
        compiler_params=params(8),
        name="home",
    )(*columns, moe_row, router.T, select, chosen)

    return pl.pallas_call(
        final_kernel,
        out_shape=shape((requests, steps, width), bf16),
        scratch_shapes=[pltpu.VMEM((slots, width), f32)],
        compiler_params=params(8),
        name="final",
    )(gates, returned, residual)


def solution(mesh):
    in_specs = (
        P("exp", None, None),
        P(),
        P("seq", None),
        P(None, "exp", "seq", None),
        P(None, "exp", None, None),
        P("exp"),
        P("seq", None),
        P(),
        P(),
        P("exp", None, None),
        P("exp", None),
        P(None, "exp", "seq", None),
        P("exp", "seq", None),
    )
    out_specs = P("exp", None, None)
    return jax.shard_map(body, mesh=mesh, in_specs=in_specs, out_specs=out_specs, check_vma=False)
```

```python
import functools

import jax
import jax.numpy as jnp
from jax import lax
from jax.experimental import pallas as pl
from jax.experimental.pallas import tpu as pltpu
from jax.sharding import PartitionSpec as P

HEADS = 16
HD = 64
EXPERTS = 16
TOPK = 2
SINKS = 4
WIN = 4096
CAP = 8
LANES = 128
PIECES = 3
FIRST_KEYS = 2
SECOND_KEYS = 8
SECOND_VALUES = 3
CORES = 2
HALF_HEADS = HEADS // CORES
HALF = HALF_HEADS * HD
PACKED = HALF + LANES
HELD = 800
PIECE = 304
AHEAD = 10
BLOCK = 256
BLOCK_HEADS = BLOCK // HD

EPSILON = 1e-06
MASKED = -1e30
MIB = 1 << 20
ROWS_BY_ROWS = (((1,), (1,)), ((), ()))
ROWS_BY_COLS = (((1,), (0,)), ((), ()))


def dot(a, b, dims=ROWS_BY_COLS):
    return lax.dot_general(a, b, dims, preferred_element_type=jnp.float32)


def params(limit_mib=32):
    return pltpu.CompilerParams(vmem_limit_bytes=limit_mib * MIB)


def moving(count):
    return pl.CostEstimate(flops=0, bytes_accessed=count, transcendentals=0)


def in_hbm(value):
    return pltpu.with_memory_space_constraint(value, pltpu.HBM)


def split(value, count):
    parts = []
    for _ in range(count):
        part = value.astype(jnp.bfloat16)
        parts.append(part)
        value = value - part.astype(jnp.float32)
    return parts


def exact_dot(values, table):
    high, low = split(values, 2)
    both = dot(jnp.concatenate([high, low], axis=0), table)
    return both[: values.shape[0]] + both[values.shape[0] :]


def rms_rows(widened, gain_row):
    inverse = lax.rsqrt(jnp.mean(widened * widened, axis=-1, keepdims=True) + EPSILON)
    return (widened * inverse * gain_row).astype(jnp.bfloat16)


def copy_rows(source_ref, rows_ref):
    requests, steps, _ = source_ref.shape
    for r in range(requests):
        rows_ref[r * steps : (r + 1) * steps, :] = source_ref[r].astype(rows_ref.dtype)


def each(sems):
    return [sems.at[i] for i in range(sems.shape[0])]


def each(sems):
    return [sems.at[i] for i in range(sems.shape[0])]


def started(pairs, sems):
    copies = [pltpu.make_async_copy(*pair, sem) for pair, sem in zip(pairs, sems)]
    for copy in copies:
        copy.start()
    return copies


def unpack(packed):
    stats = packed[:, HALF:].astype(jnp.float32)

    def joined(first):
        return sum(
            stats[:, (first + i) * HALF_HEADS : (first + i + 1) * HALF_HEADS] for i in range(PIECES)
        )

    return joined(0), joined(PIECES), packed[:, :HALF].astype(jnp.float32)


def pack(peak, total, mixed):
    parts = [part.astype(jnp.float32) for part in split(peak, PIECES) + split(total, PIECES)]
    blank = jnp.zeros((peak.shape[0], LANES - 2 * PIECES * HALF_HEADS), jnp.float32)
    return jnp.concatenate([mixed] + parts + [blank], axis=1).astype(jnp.bfloat16)


def over_heads(factor):
    row = lax.broadcasted_iota(jnp.int32, (HALF_HEADS, HALF), 0)
    col = lax.broadcasted_iota(jnp.int32, (HALF_HEADS, HALF), 1) // HD
    expand = (row == col).astype(jnp.bfloat16)
    return sum(dot(part, expand) for part in split(factor, 2))


def merge(parts):
    overall = functools.reduce(jnp.maximum, [peak for peak, _, _ in parts])
    factors = [jnp.exp(peak - overall) for peak, _, _ in parts]
    total = sum(factor * part[1] for factor, part in zip(factors, parts))
    mixed = sum(over_heads(factor) * part[2] for factor, part in zip(factors, parts))
    return overall, total, mixed


def attend(parts):
    overall = functools.reduce(jnp.maximum, [peak for peak, _, _ in parts])
    factors = [jnp.exp(peak - overall) for peak, _, _ in parts]
    total = sum(factor * part[1] for factor, part in zip(factors, parts))
    inverse = jnp.where(total > 0, 1.0 / jnp.where(total > 0, total, 1.0), 0.0)
    return sum(over_heads(factor * inverse) * part[2] for factor, part in zip(factors, parts))


def route(ids_ref, order_ref, select_ref, chosen_ref):
    steps, _, requests = ids_ref.shape
    rows = requests * steps
    lane = lax.broadcasted_iota(jnp.int32, (rows, LANES), 1)
    own_row = lax.broadcasted_iota(jnp.int32, (rows, requests), 0)
    own_request = lax.broadcasted_iota(jnp.int32, (rows, requests), 1) == own_row // steps
    chosen = []
    for c in range(TOPK):
        ids = jnp.zeros((rows, requests), jnp.int32)
        for t in range(steps):
            ids = jnp.where(own_request & (own_row % steps == t), ids_ref[t, c : c + 1, :], ids)
        chosen.append(jnp.sum(ids.astype(jnp.float32), axis=1, keepdims=True).astype(jnp.int32))
    onehot = [(lane == ids).astype(jnp.float32) for ids in chosen]
    square_row = lax.broadcasted_iota(jnp.int32, (rows, rows), 0)
    square_col = lax.broadcasted_iota(jnp.int32, (rows, rows), 1)
    order_wide = jnp.broadcast_to(order_ref[...], (rows, rows))
    down = jnp.sum(
        jnp.where(square_row == square_col, order_wide, 0).astype(jnp.float32),
        axis=1,
        keepdims=True,
    )
    earlier = (order_wide.astype(jnp.float32) < down).astype(jnp.bfloat16)
    counts = dot(earlier, sum(onehot).astype(jnp.bfloat16))
    slot = lax.broadcasted_iota(jnp.int32, (rows, EXPERTS * CAP), 1)
    both = jnp.zeros((rows, EXPERTS * CAP), jnp.float32)
    for c in range(TOPK):
        position = jnp.sum(onehot[c] * counts, axis=-1, keepdims=True).astype(jnp.int32)
        column = chosen[c] * CAP + position
        select = ((column == slot) & (position < CAP)).astype(jnp.float32)
        select_ref[c] = select
        chosen_ref[c] = onehot[c]
        both = both + select
    return jnp.transpose(both)


def qkv_kernel(
    tokens_ref,
    gain_ref,
    weight_ref,
    window_ref,
    lengths_ref,
    out_ref,
    spans_ref,
    token_buf,
    gain_buf,
    weight_buf,
    rows_ref,
    numbers_ref,
    sems,
):
    copies = started(
        (
            (tokens_ref, token_buf),
            (gain_ref, gain_buf),
            (lengths_ref, numbers_ref),
            (weight_ref, weight_buf),
        ),
        each(sems),
    )
    for copy in copies[:3]:
        copy.wait()
    copy_rows(token_buf, rows_ref)
    normed = rms_rows(rows_ref[...], gain_buf[...])
    for r in range(spans_ref.shape[0]):
        spans_ref[r : r + 1, :] = jnp.full((1, LANES), numbers_ref[r], jnp.int32)
    copies[3].wait()
    out_ref[...] = dot(normed, weight_buf[...], ROWS_BY_ROWS).astype(jnp.bfloat16)


def in_order(sent_refs, ordered_ref):
    place = lax.axis_index("seq")
    for k, sent_ref in enumerate(sent_refs):
        ordered_ref[jnp.bitwise_xor(place, k)] = sent_ref[...]


def head_masks(rows, width, steps):
    row_head = lax.broadcasted_iota(jnp.int32, (rows, width), 0) // steps % BLOCK_HEADS
    col_head = lax.broadcasted_iota(jnp.int32, (rows, width), 1) // HD % BLOCK_HEADS
    return (row_head == col_head).astype(jnp.float32)


def fetch_expert_kernel(
    sent_ref,
    in_ref,
    ids_ref,
    order_ref,
    tokens_ref,
    held_ref,
    piece_ref,
    select_ref,
    chosen_ref,
    turned_ref,
    columns_ref,
    ids_buf,
    order_buf,
    tokens_buf,
    rows_ref,
    sems,
):
    pairs = [(ids_ref, ids_buf), (order_ref, order_buf), (tokens_ref, tokens_buf)]
    pairs += [
        (in_ref.at[p, 0, pl.ds(0, piece_ref.shape[1])], piece_ref.at[p]) for p in range(2)
    ]
    copies = started(pairs, each(sems))
    held_ref[...] = sent_ref[...]
    for copy in copies[:3]:
        copy.wait()
    turned_ref[...] = route(ids_buf, order_buf, select_ref, chosen_ref)
    copy_rows(tokens_buf, rows_ref)
    width, share = rows_ref.shape[1], columns_ref.shape[1]
    feature = lax.broadcasted_iota(jnp.int32, (width, share), 0)
    column = lax.broadcasted_iota(jnp.int32, (width, share), 1)
    own = (feature == column + lax.axis_index("seq") * share).astype(jnp.bfloat16)
    columns_ref[...] = dot(rows_ref[...].astype(jnp.bfloat16), own)
    for copy in copies[3:]:
        copy.wait()


def attention_kernel(of_own, *refs):
    if of_own:
        flat_ref, spans_ref, window_ref, out_ref, result_ref = refs
    else:
        *mixed_refs, spans_ref, window_ref = refs[:-4]
        out_ref, flat_ref, ordered_ref, result_ref = refs[-4:]
        devices, _, share = ordered_ref.shape
    rows = result_ref.shape[0]
    _, requests, span, width = window_ref.shape
    steps = rows // requests
    block_rows = BLOCK_HEADS * steps
    place = lax.axis_index("seq")
    if not of_own:
        in_order(mixed_refs, ordered_ref)
        for d in range(devices):
            if d * share < width:
                flat_ref[:, d * share : (d + 1) * share] = ordered_ref[d].astype(jnp.float32)
    own_head = head_masks(block_rows, HALF, steps)
    half = place % CORES if of_own else 1 - place % CORES
    heads = pl.ds(pl.multiple_of(half * HALF, HALF), HALF)
    base = place * span
    scale = HD ** (-0.5)
    pair = 2 * steps
    tiles = HALF_HEADS * steps // pair
    slot = base + lax.broadcasted_iota(jnp.int32, (pair, span), 1)
    step = lax.broadcasted_iota(jnp.int32, (pair, span), 0) % steps
    stat_lane = lax.broadcasted_iota(jnp.int32, (HALF_HEADS * steps, LANES), 1)
    stat_head = lax.broadcasted_iota(jnp.int32, (HALF_HEADS * steps, LANES), 0) // steps
    cols = [slice(c, c + BLOCK) for c in range(0, HALF, BLOCK)]

    def score(r):
        keys = window_ref[0, r, :, heads]
        queries = flat_ref[r * steps : (r + 1) * steps, heads]
        queries = (jnp.concatenate([queries] * BLOCK_HEADS, axis=0) * own_head).astype(jnp.bfloat16)
        return jnp.concatenate(
            [dot(queries[:, c], keys[:, c], ROWS_BY_ROWS) for c in cols], axis=0
        )

    scores = score(0)
    for r in range(requests):
        following = score(r + 1) if r + 1 < requests else None
        length = spans_ref[r : r + 1, 0:1]
        age = jnp.bitwise_and(slot - (length - SINKS), WIN - 1)
        live = ((slot < jnp.minimum(WIN, length - SINKS)) & (age > step))[None]
        scores = jnp.where(live, scores.reshape(tiles, pair, span) * scale, MASKED)
        peak = jnp.max(scores, axis=-1, keepdims=True)
        weight = jnp.where(live, jnp.exp(scores - peak), 0.0)
        total = jnp.sum(weight, axis=-1, keepdims=True)
        weight = weight.reshape(HALF_HEADS * steps, span).astype(jnp.bfloat16)
        values = window_ref[1, r, :, heads]
        outs = []
        for b, c in enumerate(cols):
            own = slice(b * block_rows, (b + 1) * block_rows)
            mixed = dot(weight[own], values[:, c]) * own_head[:, c]
            mixed = sum(mixed[i : i + pair] for i in range(0, block_rows, pair))
            outs.append(mixed[:steps] + mixed[steps:])
        stats = jnp.where(stat_lane == stat_head, peak.reshape(HALF_HEADS * steps, 1), 0.0)
        stats = jnp.where(stat_lane == stat_head + HALF_HEADS, total.reshape(HALF_HEADS * steps, 1), stats)
        stats = jnp.sum(stats.reshape(tiles, pair, LANES), axis=0)
        outs.append(stats[:steps] + stats[steps:])
        result_ref[r * steps : (r + 1) * steps, :] = jnp.concatenate(outs, axis=1)
        scores = following
    peak = result_ref[:, HALF : HALF + HALF_HEADS]
    total = result_ref[:, HALF + HALF_HEADS : HALF + 2 * HALF_HEADS]
    out_ref[...] = pack(peak, total, result_ref[:, :HALF])


def extra_kernel(*refs):
    *mixed_refs, sinks_ref = refs[:-6]
    out_ref, stats_ref, ordered_ref, flat_ref, query_ref, keys_ref = refs[-6:]
    devices, rows, share = ordered_ref.shape
    _, requests, sinks, width = sinks_ref.shape
    steps = rows // requests
    block_rows = BLOCK_HEADS * steps
    count = sinks + steps
    in_order(mixed_refs, ordered_ref)
    for d in range(devices):
        flat_ref[:, d * share : (d + 1) * share] = ordered_ref[d].astype(jnp.float32)
    own_head = head_masks(block_rows, width, steps)
    for r in range(requests):
        own = slice(r * steps, (r + 1) * steps)
        queries = jnp.concatenate([flat_ref[own, 0:width]] * BLOCK_HEADS, axis=0) * own_head
        query_ref[r * block_rows : (r + 1) * block_rows, :] = queries
        for p in range(2):
            keys_ref[p, r * count : r * count + sinks] = sinks_ref[p, r].astype(jnp.float32)
            keys_ref[p, r * count + sinks : (r + 1) * count] = flat_ref[
                own, (p + 1) * width : (p + 2) * width
            ]
    all_rows = requests * block_rows
    all_keys = requests * count
    row = lax.broadcasted_iota(jnp.int32, (all_rows, all_keys), 0)
    key = lax.broadcasted_iota(jnp.int32, (all_rows, all_keys), 1)
    live = (row // block_rows == key // count) & (key % count - sinks <= row % steps)
    stat_lane = lax.broadcasted_iota(jnp.int32, (all_rows, LANES), 1)
    stat_head = lax.broadcasted_iota(jnp.int32, (all_rows, LANES), 0) % block_rows // steps
    whole_mask = jnp.concatenate([own_head[:, :BLOCK]] * requests, axis=0)
    stats = jnp.zeros((all_rows, LANES), jnp.float32)
    pair = 2 * steps

    def by_request(values):
        values = jnp.sum(values.reshape(requests, block_rows // pair, pair, values.shape[-1]), axis=1)
        return values[:, :steps] + values[:, steps:]

    for b in range(width // BLOCK):
        c = slice(b * BLOCK, (b + 1) * BLOCK)
        scores = dot(
            query_ref[:, c].astype(jnp.bfloat16), keys_ref[0, :, c].astype(jnp.bfloat16), ROWS_BY_ROWS
        )
        scores = jnp.where(live, scores * HD ** (-0.5), MASKED)
        peak = jnp.max(scores, axis=-1, keepdims=True)
        weight = jnp.where(live, jnp.exp(scores - peak), 0.0)
        total = jnp.sum(weight, axis=-1, keepdims=True)
        mixed = dot(weight.astype(jnp.bfloat16), keys_ref[1, :, c].astype(jnp.bfloat16))
        mixed = by_request(mixed * whole_mask)
        for r in range(requests):
            out_ref[r * steps : (r + 1) * steps, c] = mixed[r]
        stats = jnp.where(stat_lane == stat_head + b * BLOCK_HEADS, peak, stats)
        stats = jnp.where(stat_lane == stat_head + b * BLOCK_HEADS + HEADS, total, stats)
    stats = by_request(stats)
    for r in range(requests):
        stats_ref[r * steps : (r + 1) * steps, :] = stats[r]


def pair_kernel(keep_ref, other_ref, out_ref):
    out_ref[...] = pack(*merge([unpack(keep_ref[...]), unpack(other_ref[...])]))


def project_kernel(*refs):
    *part_refs, extra_ref, extra_stats_ref, weight_ref, other_weight_ref, columns_ref = refs[:-3]
    turned_ref, out_ref, residual_ref = refs[-3:]
    devices = lax.axis_size("seq")
    groups = lax.axis_size("exp")
    local_experts = EXPERTS // groups
    odd = lax.axis_index("seq") % CORES == 1

    def own_half(value, at, width):
        return jnp.where(odd, value[:, at + width : at + 2 * width], value[:, at : at + width])

    parts = [unpack(part_ref[...]) for part_ref in part_refs]
    parts.append(
        (
            own_half(extra_stats_ref[...], 0, HALF_HEADS),
            own_half(extra_stats_ref[...], HEADS, HALF_HEADS),
            own_half(extra_ref[...], 0, HALF),
        )
    )
    attended = attend(parts).astype(jnp.bfloat16)

    def project(weight):
        weight = jnp.where(odd, weight[:, HALF:], weight[:, :HALF])
        return dot(attended, weight, ROWS_BY_ROWS)

    mine = project(weight_ref[...]) + columns_ref[...]
    others = project(other_weight_ref[...])
    residual = jnp.concatenate(
        [jnp.where(odd, others, mine), jnp.where(odd, mine, others)], axis=1
    )
    residual_ref[...] = residual
    table = dot(turned_ref[...].astype(jnp.bfloat16), residual.astype(jnp.bfloat16))
    for s in range(devices):
        for x in range(groups):
            row = (x * local_experts + s // (devices // local_experts)) * CAP
            out_ref[s * groups + x] = table[row : row + CAP].astype(jnp.bfloat16)


def home_kernel(devices, *refs):
    residual_refs, refs = refs[:devices], refs[devices:]
    gain_ref, router_ref, select_ref, chosen_ref, residual_ref, gates_ref, ordered_ref = refs
    in_order(residual_refs, ordered_ref)
    residual = jnp.concatenate(
        [ordered_ref[d] + ordered_ref[d + 1] for d in range(0, devices, CORES)], axis=1
    )
    residual_ref[...] = residual
    normed = rms_rows(residual, gain_ref[...])
    logits = dot(normed, router_ref[...], ROWS_BY_ROWS)
    gates = jnp.zeros(select_ref.shape[1:], jnp.float32)
    for c in range(TOPK):
        logit = jnp.sum(chosen_ref[c][:, :EXPERTS] * logits, axis=-1, keepdims=True)
        gates = gates + jax.nn.sigmoid(logit) * select_ref[c]
    gates_ref[...] = gates


def expert_kernel(
    received_ref, gain_ref, piece_ref, in_ref, down_ref, keep_ref, send_ref, in_buf, down_buf, sems
):
    hidden_units, width = down_buf.shape
    held = piece_ref.shape[1]
    pieces = [(at, min(PIECE, hidden_units - at)) for at in range(held, hidden_units, PIECE)]
    downs = [(0, held)] + pieces
    stages = []
    for at, count in pieces:
        stages.append(
            [
                (in_ref.at[p, 0, pl.ds(at, count)], in_buf.at[p, pl.ds(at - held, count)])
                for p in range(2)
            ]
        )
    for at, count in downs:
        stages.append([(down_ref.at[0, pl.ds(at, count)], down_buf.at[pl.ds(at, count)])])
    flying = []

    def start_next():
        if len(flying) < len(stages):
            first = sum(len(stage) for stage in stages[: len(flying)])
            flying.append(started(stages[len(flying)], [sems.at[first + i] for i in range(len(stages[len(flying)]))]))

    def wait_for(stage):
        for copy in flying[stage]:
            copy.wait()
        start_next()

    for _ in range(AHEAD):
        start_next()
    devices = lax.axis_size("seq")
    groups = lax.axis_size("exp")
    columns = []
    for s in range(0, devices, CORES):
        pieces_of_chip = [
            jnp.concatenate(
                [received_ref[d * groups + g].astype(jnp.float32) for g in range(groups)], axis=0
            )
            for d in range(s, s + CORES)
        ]
        columns.append(sum(pieces_of_chip))
    rows = rms_rows(jnp.concatenate(columns, axis=1), gain_ref[...])

    def layer(gate_weight, up_weight):
        gate = dot(rows, gate_weight, ROWS_BY_ROWS)
        up = dot(rows, up_weight, ROWS_BY_ROWS)
        return (jax.nn.gelu(gate, approximate=True) * up).astype(jnp.bfloat16)

    hidden = [layer(piece_ref[0], piece_ref[1])]
    for i, (at, count) in enumerate(pieces):
        wait_for(i)
        own = slice(at - held, at - held + count)
        hidden.append(layer(in_buf[0, own], in_buf[1, own]))
    outputs = jnp.zeros((groups * CAP, width), jnp.float32)
    for i, (at, count) in enumerate(downs):
        wait_for(len(pieces) + i)
        outputs = outputs + dot(hidden[i], down_buf[at : at + count])
    half = width // 2
    odd = lax.axis_index("seq") % 2 == 1
    keep_ref[...] = jnp.where(odd, outputs[:, half:], outputs[:, :half])
    send_ref[...] = jnp.where(odd, outputs[:, :half], outputs[:, half:])


def spread_kernel(kept_ref, other_ref, out_ref):
    slots = out_ref.shape[1]
    groups = kept_ref.shape[0] // slots
    outputs = kept_ref[...] + other_ref[...]
    for block in range(out_ref.shape[0]):
        first = block % groups * slots
        out_ref[block] = outputs[first : first + slots].astype(jnp.bfloat16)


def column_block(sharer, sharers):
    block = 0
    while sharers > 1:
        sharers //= 2
        block += (sharer & 1) * sharers
        sharer >>= 1
    return block


def final_kernel(gates_ref, returned_ref, residual_ref, out_ref, table_ref):
    requests, steps, width = out_ref.shape
    devices, groups, slots, part = returned_ref.shape
    local_experts = EXPERTS // groups
    sharers = devices // local_experts
    for s in range(devices):
        first = column_block(s % sharers, sharers) * part
        for x in range(groups):
            row = (x * local_experts + s // sharers) * slots
            table_ref[row : row + slots, first : first + part] = returned_ref[s, x].astype(jnp.float32)
    table = table_ref[...].astype(jnp.bfloat16)
    moe = exact_dot(gates_ref[...], table)
    total = residual_ref[...] + moe
    for r in range(requests):
        out_ref[r] = total[r * steps : (r + 1) * steps].astype(jnp.bfloat16)


def exchange(value, bits):
    return lax.ppermute(value, "seq", [(i, i ^ bits) for i in range(lax.axis_size("seq"))])


def from_chips(values, meanwhile=None):
    others = [exchange(values, k) for k in range(2, lax.axis_size("seq"), 2)]
    if meanwhile is not None:
        values = meanwhile(values)
    return [values] + others


def gather_seq(values, meanwhile=None):
    near = from_chips(values, meanwhile)
    return [part for value in near for part in (value, exchange(value, 1))]


def shape(dims, dtype):
    return jax.ShapeDtypeStruct(dims, dtype)


def body(
    tokens,
    attn_gain,
    w_qkv,
    window_cache,
    sink_cache,
    lengths,
    w_out,
    moe_gain,
    router,
    expert_ids,
    slot_order,
    expert_in,
    expert_down,
):
    requests, steps, width = tokens.shape
    rows = requests * steps
    seq_index = lax.axis_index("seq")
    seq_count = lax.axis_size("seq")
    groups = lax.axis_size("exp")
    local_experts = EXPERTS // groups
    sharers = seq_count // local_experts
    span = window_cache.shape[2]
    share = w_qkv.shape[0]
    slots = EXPERTS * CAP
    f32, bf16 = jnp.float32, jnp.bfloat16

    vmem = pl.BlockSpec(memory_space=pltpu.VMEM)
    hbm = pl.BlockSpec(memory_space=pltpu.HBM)

    gain_row = attn_gain.reshape(1, width)
    local_mix, spans = pl.pallas_call(
        qkv_kernel,
        in_specs=[hbm] * 5,
        out_shape=(shape((rows, share), bf16), shape((requests, LANES), jnp.int32)),
        scratch_shapes=[
            pltpu.VMEM(tokens.shape, bf16),
            pltpu.VMEM(gain_row.shape, f32),
            pltpu.VMEM(w_qkv.shape, bf16),
            pltpu.VMEM((rows, width), f32),
            pltpu.SMEM((requests,), jnp.int32),
            pltpu.SemaphoreType.DMA((4,)),
        ],
        compiler_params=params(4),
        name="qkv",
    )(in_hbm(tokens), in_hbm(gain_row), in_hbm(w_qkv), in_hbm(window_cache), in_hbm(lengths))

    mixed = gather_seq(local_mix)

    padded = width + LANES
    packed_shape = shape((rows, PACKED), bf16)
    sent, queries = pl.pallas_call(
        functools.partial(attention_kernel, False),
        in_specs=[vmem] * (seq_count + 2),
        out_shape=(packed_shape, shape((rows, padded), f32)),
        scratch_shapes=[
            pltpu.VMEM((seq_count, rows, share), bf16),
            pltpu.VMEM((rows, PACKED), f32),
        ],
        compiler_params=params(8),
        cost_estimate=moving(2 * window_cache.size),
        name="attention_other",
    )(*mixed, spans, window_cache)
    other = exchange(sent, 1)
    kept = pl.pallas_call(
        functools.partial(attention_kernel, True),
        in_specs=[vmem] * 3,
        out_shape=packed_shape,
        scratch_shapes=[pltpu.VMEM((rows, PACKED), f32)],
        compiler_params=params(8),
        cost_estimate=moving(2 * window_cache.size),
        name="attention_own",
    )(queries, spans, window_cache)

    extra, extra_stats = pl.pallas_call(
        extra_kernel,
        out_shape=(shape((rows, width), f32), shape((rows, LANES), f32)),
        scratch_shapes=[
            pltpu.VMEM((seq_count, rows, share), bf16),
            pltpu.VMEM((rows, 3 * width), f32),
            pltpu.VMEM((rows * BLOCK_HEADS, width), f32),
            pltpu.VMEM((2, requests * (SINKS + steps), width), f32),
        ],
        compiler_params=params(8),
        name="extra",
    )(*mixed, sink_cache)

    part = pl.pallas_call(
        pair_kernel,
        out_shape=shape((rows, PACKED), bf16),
        compiler_params=params(8),
        name="pair",
    )(kept, other)

    hidden_units = expert_down.shape[1]
    held_units = min(HELD, hidden_units)
    late_units = max(hidden_units - held_units, 16)

    fetched = []

    def fetch_expert(values):
        held, *outputs = pl.pallas_call(
            fetch_expert_kernel,
            in_specs=[vmem] + [hbm] * 4,
            out_shape=(
                shape(values.shape, bf16),
                shape((2, held_units, width), bf16),
                shape((TOPK, rows, slots), f32),
                shape((TOPK, rows, LANES), f32),
                shape((slots, rows), f32),
                shape((rows, w_out.shape[0]), f32),
            ),
            scratch_shapes=[
                pltpu.VMEM((steps, TOPK, requests), jnp.int32),
                pltpu.VMEM(slot_order.shape, jnp.int32),
                pltpu.VMEM(tokens.shape, bf16),
                pltpu.VMEM((rows, width), f32),
                pltpu.SemaphoreType.DMA((5,)),
            ],
            compiler_params=params(8),
            cost_estimate=moving(4 * held_units * width),
            name="fetch_expert",
        )(
            values,
            in_hbm(expert_in),
            in_hbm(expert_ids.transpose(1, 2, 0)),
            in_hbm(slot_order),
            in_hbm(tokens),
        )
        fetched.extend(outputs)
        return held

    parts = from_chips(part, fetch_expert)
    other_weight = exchange(lax.optimization_barrier((w_out, part))[0], 1)
    piece, select, chosen, turned, token_columns = fetched

    outgoing, residual_columns = pl.pallas_call(
        project_kernel,
        out_shape=(
            shape((seq_count * groups, CAP, CORES * w_out.shape[0]), bf16),
            shape((rows, CORES * w_out.shape[0]), f32),
        ),
        compiler_params=params(16),
        name="project",
    )(*parts, extra, extra_stats, w_out, other_weight, token_columns, turned)
    received = lax.all_to_all(outgoing, ("seq", "exp"), split_axis=0, concat_axis=0, tiled=True)
    columns = gather_seq(residual_columns)

    moe_row = moe_gain.reshape(1, width)
    kept, sent = pl.pallas_call(
        expert_kernel,
        in_specs=[vmem, vmem, vmem, hbm, hbm],
        out_shape=(
            shape((groups * CAP, width // 2), f32),
            shape((groups * CAP, width // 2), f32),
        ),
        scratch_shapes=[
            pltpu.VMEM((2, late_units, width), bf16),
            pltpu.VMEM((hidden_units, width), bf16),
            pltpu.SemaphoreType.DMA((3 * pl.cdiv(late_units, PIECE) + 1,)),
        ],
        compiler_params=params(20),
        name="expert",
    )(received, moe_row, piece, in_hbm(expert_in), in_hbm(expert_down))

    reach = 1
    while True:
        other = lax.ppermute(sent, "seq", [(i, i ^ reach) for i in range(seq_count)])
        reach *= 2
        if reach >= sharers:
            break
        upper = (seq_index // reach) % 2 == 1
        low, high = jnp.split(kept + other, 2, axis=1)
        kept, sent = jnp.where(upper, high, low), jnp.where(upper, low, high)
    part_width = kept.shape[1]
    outgoing = pl.pallas_call(
        spread_kernel,
        out_shape=shape((seq_count * groups, CAP, part_width), bf16),
        compiler_params=params(8),
        name="spread",
    )(kept, other)
    returned = lax.all_to_all(
        outgoing,
        ("seq", "exp"),
        split_axis=0,
        concat_axis=0,
        tiled=True,
    ).reshape(seq_count, groups, CAP, part_width)

    columns, _ = lax.optimization_barrier((columns, outgoing))
    residual, gates = pl.pallas_call(
        functools.partial(home_kernel, seq_count),
        out_shape=(shape((rows, width), f32), shape((rows, slots), f32)),
        scratch_shapes=[pltpu.VMEM((seq_count, rows, CORES * w_out.shape[0]), f32)],
        compiler_params=params(8),
        name="home",
    )(*columns, moe_row, router.T, select, chosen)

    return pl.pallas_call(
        final_kernel,
        out_shape=shape((requests, steps, width), bf16),
        scratch_shapes=[pltpu.VMEM((slots, width), f32)],
        compiler_params=params(8),
        name="final",
    )(gates, returned, residual)


def solution(mesh):
    in_specs = (
        P("exp", None, None),
        P(),
        P("seq", None),
        P(None, "exp", "seq", None),
        P(None, "exp", None, None),
        P("exp"),
        P("seq", None),
        P(),
        P(),
        P("exp", None, None),
        P("exp", None),
        P(None, "exp", "seq", None),
        P("exp", "seq", None),
    )
    out_specs = P("exp", None, None)
    return jax.shard_map(body, mesh=mesh, in_specs=in_specs, out_specs=out_specs, check_vma=False)
```
